128 devices in a mesh: row: 8 (over y, core), col: 16 (over x, z).
Axes of the slice: x: 4, y: 4, z: 4, core: 2. Of those that a mesh axis runs over, the one named last changes fastest.
Arguments:
- object_planes: float32 [2, 4096, 8192], P(None, 'row', 'col'), may hold values from -6 to 6
- probe_planes: float32 [2, 2, 256, 256], replicated, may hold values from -3 to 3
- offsets: int32 [1024, 2], P(('row', 'col')), may hold values from 0 to 7936, as said below
- photon_counts: int32 [1024, 256, 256], P(('row', 'col')), may hold values from 0 to 8
- live_counts: int32 [8, 16], P('row', 'col'), may hold values from 1 to 8, as said below
Outputs:
- new_object: float32 [2, 4096, 8192], P(None, 'row', 'col')
- new_probe: float32 [2, 2, 256, 256], replicated
The draws below stay inside these ranges and needn't reach their ends.
Inputs may be any that keep to these rules, and one draw needn't show every extreme that they name: `offsets`: each slot's patch lies inside the object and its top-left pixel lies in the tile of the device that holds the slot (tiles of 512 x 512 pixels, device (r, c) holding tile (r, c)). `live_counts`: some device has all 8 slots live in every draw.
All inputs are finite; a program needn't handle non-finite values.
Results may differ from the reference program's by a relative error of at most 0.0003.
Values sent between devices are 32-bit elements; how exact they have to be, the bound alone decides.
No kernel may reach another device: no remote copies, remote signals or barrier semaphores. Data moves between devices by JAX's collectives and lax.ppermute only.
A program may use at most 64 MiB of HBM per device.

```python
import jax
import jax.numpy as jnp
from jax import lax

PS = 256
MODES = 2
TR = 512
TC = 512
POS_DEV = 8
NY = 4096
NX = 8192
NPOS = 1024
N_ROW = 8
N_COL = 16


def draw_offsets(key, part):
    key = jax.random.fold_in(key, 11)
    key_rows, key_cols = jax.random.split(key)
    slot_index = jnp.arange(NPOS, dtype=jnp.int32)
    device_index = slot_index // POS_DEV
    tile_row = device_index // N_COL
    tile_col = device_index % N_COL
    high_row = jnp.where(tile_row == N_ROW - 1, TR - PS + 1, TR)
    high_col = jnp.where(tile_col == N_COL - 1, TC - PS + 1, TC)
    inner_row = jax.random.randint(key_rows, (NPOS,), 0, high_row, dtype=jnp.int32)
    inner_col = jax.random.randint(key_cols, (NPOS,), 0, high_col, dtype=jnp.int32)
    return jnp.stack([inner_row + tile_row * TR, inner_col + tile_col * TC], axis=1)


def draw_live_counts(key, part):
    key = jax.random.fold_in(key, 23)
    key_counts, key_full = jax.random.split(key)
    devices_all = N_ROW * N_COL
    values = jax.random.randint(key_counts, (devices_all,), 1, POS_DEV + 1, dtype=jnp.int32)
    full_device = jax.random.randint(key_full, (), 0, devices_all, dtype=jnp.int32)
    values = jnp.where(jnp.arange(devices_all, dtype=jnp.int32) == full_device, POS_DEV, values)
    return values.reshape(N_ROW, N_COL)


def plant(drawn, rng, low, largest):
    spot = [jax.random.randint(jax.random.fold_in(rng, axis), (), 0, length) for axis, length in enumerate(drawn.shape)]
    longest = drawn.shape.index(max(drawn.shape))
    beside = spot[:longest] + [(spot[longest] + 1) % drawn.shape[longest]] + spot[longest + 1:]
    return drawn.at[tuple(spot)].set(low).at[tuple(beside)].set(largest)


def block_scale(rng, shape, shards, least, top_value):
    def one(axis_at, shards_of):
        draws = jax.random.uniform(jax.random.fold_in(jax.random.fold_in(rng, 6), axis_at), (shards_of,), jnp.float32, least / len(shards), top_value / len(shards))
        return jnp.repeat(jnp.exp(draws), shape[axis_at] // shards_of).reshape((-1,) + (1,) * (len(shape) - axis_at - 1))

    level = one(*shards[0])
    for cut in shards[1:]:
        level = level * one(*cut)
    return level


def bell_draw(own_key, dims, deviation, bound, pieces=(), held_as=jnp.bfloat16):
    level = block_scale(own_key, dims, pieces, -0.22, 0.18) if pieces else 1.0
    drawn = jax.random.normal(own_key, dims, jnp.float32) * deviation * level
    return jnp.minimum(jnp.maximum(drawn, -bound), bound).astype(held_as)


def setup_inputs(seed: int = 0) -> dict:
    seeds = jax.random.split(jax.random.key(seed), 6)
    return {
        "object_planes": bell_draw(seeds[0], (2, NY, NX), 1.0, 6.0, ((1, 8), (2, 16)), jnp.float32),
        "probe_planes": bell_draw(seeds[1], (2, MODES, PS, PS), 0.5, 3.0, (), jnp.float32),
        "offsets": draw_offsets(jax.random.fold_in(seeds[5], 71), 0),
        "photon_counts": plant(jax.random.randint(seeds[3], (NPOS, PS, PS), 0, 9), jax.random.fold_in(seeds[3], 1), 0, 8).astype(jnp.int32),
        "live_counts": draw_live_counts(jax.random.fold_in(seeds[5], 71), 0),
    }


def reference(object_planes, probe_planes, offsets, photon_counts, live_counts):
    object_complex = lax.complex(object_planes[0], object_planes[1])
    probe_complex = lax.complex(probe_planes[0], probe_planes[1])
    flat_live = live_counts.reshape(-1)

    def visit_slot(state_pair, slot_index):
        object_grad, probe_grad = state_pair
        top_row = offsets[slot_index, 0].astype(jnp.int32)
        left_col = offsets[slot_index, 1].astype(jnp.int32)
        zero_index = jnp.zeros((), jnp.int32)
        patch_complex = lax.dynamic_slice(object_complex, (top_row, left_col), (PS, PS))
        wave_field = probe_complex * patch_complex[None]
        far_field = jnp.fft.fft2(wave_field, norm='ortho')
        modelled = lax.optimization_barrier(jnp.sum(jnp.real(far_field) ** 2 + jnp.imag(far_field) ** 2, axis=0))
        amplitude = jnp.sqrt(jnp.maximum(modelled, 0.1))
        factor = 1.0 - jnp.sqrt(photon_counts[slot_index].astype(amplitude.dtype)) / amplitude
        back_wave = jnp.fft.ifft2(factor[None] * far_field, norm='ortho')
        used_flag = (slot_index % POS_DEV < flat_live[slot_index // POS_DEV]).astype(amplitude.dtype)
        object_term = lax.optimization_barrier(jnp.sum(jnp.conj(probe_complex) * back_wave, axis=0))
        probe_term = jnp.conj(patch_complex)[None] * back_wave
        current = lax.dynamic_slice(object_grad, (zero_index, top_row, left_col), (2, PS, PS))
        added = current + used_flag * jnp.stack([jnp.real(object_term), jnp.imag(object_term)])
        object_grad = lax.dynamic_update_slice(object_grad, added, (zero_index, top_row, left_col))
        probe_grad = probe_grad + used_flag * jnp.stack([jnp.real(probe_term), jnp.imag(probe_term)])
        return ((object_grad, probe_grad), None)
    initial = (jnp.zeros(object_planes.shape, object_planes.dtype), jnp.zeros(probe_planes.shape, probe_planes.dtype))
    (object_grad, probe_grad), unused = lax.scan(visit_slot, initial, jnp.arange(NPOS, dtype=jnp.int32))
    new_object = object_planes - 0.5 * object_grad
    new_probe = probe_planes - probe_grad / jnp.sqrt(jnp.float32(NPOS)).astype(probe_planes.dtype)
    return (new_object, new_probe)
```

```python
import math

import ml_dtypes
import numpy as np
import jax
import jax.numpy as jnp
from jax import lax
from jax.experimental import pallas as pl
from jax.experimental.pallas import tpu as pltpu
from jax.sharding import PartitionSpec as P

f32, bf16 = jnp.float32, jnp.bfloat16
W = 256
H = 128


def make_tables():
    b = np.arange(H)[:, None]
    q = np.arange(H)[None, :]
    right = []
    for p in (0, 1):
        ang = 2.0 * np.pi * (((2 * q + p) * b) % W) / W
        c, s = np.cos(ang) / 16.0, np.sin(ang) / 16.0
        right.append(np.block([[c, -s], [s, c]]))
    def split(t):
        hi = t.astype(np.float32).astype(ml_dtypes.bfloat16)
        lo = (t - hi.astype(np.float64)).astype(np.float32).astype(ml_dtypes.bfloat16)
        return hi, lo
    as_rhs = []
    as_lhs = []
    for t in (right[0], right[1], right[0].T, right[1].T):
        hi, lo = split(t)
        as_rhs.append(np.concatenate([hi, hi, lo], 0))
        as_lhs.append(np.concatenate([hi, hi, lo], 1))
    rhs = np.stack(as_rhs)
    lhs = np.stack(as_lhs)
    return rhs, lhs


def split(x):
    hi = x.astype(bf16)
    lo = (x - hi.astype(f32)).astype(bf16)
    return hi, lo


def rmul(x, t):
    hi, lo = split(x)
    return jnp.dot(jnp.concatenate([hi, lo, hi], 1), t, preferred_element_type=f32)


def lmul(t, x):
    hi, lo = split(x)
    return jnp.dot(t, jnp.concatenate([hi, lo, hi], 0), preferred_element_type=f32)


def cat1(a, b):
    return jnp.concatenate([a, b], 1)


def cat0(a, b):
    return jnp.concatenate([a, b], 0)


def main_kernel(offs, live, anchor, obj, right_top, right_bot, below, corner, probe, sq, rhs, lhs,
                o_part, o_rtop, o_rbot, o_corner, o_below, o_probe,
                cov, acc, patch, pacc, prv, sqv, rt, lt, far, term, sems):
    ins = [
        (obj, cov.at[:, 0:512, 0:512]),
        (right_top, cov.at[:, 0:256, 512:768]),
        (right_bot, cov.at[:, 256:512, 512:768]),
        (below, cov.at[:, 512:768, 0:512]),
        (corner, cov.at[:, 512:768, 512:768]),
        (probe, prv),
        (rhs, rt),
        (lhs, lt),
        (sq, sqv),
    ]
    copies = [pltpu.make_async_copy(s, d, sems.at[i]) for i, (s, d) in enumerate(ins)]
    for c in copies:
        c.start()
    acc[...] = jnp.zeros_like(acc)
    pacc[...] = jnp.zeros_like(pacc)
    for c in copies:
        c.wait()
    lane = lax.broadcasted_iota(jnp.int32, (W, H), 1)
    sub9 = lax.broadcasted_iota(jnp.int32, (33, 8, H), 1)
    sub = lax.broadcasted_iota(jnp.int32, (32, 8, H), 1)

    def slot(s, carry):
        top = offs[s, 0] - anchor[0]
        left = offs[s, 1] - anchor[1]
        la = pl.multiple_of(lax.div(left, 128) * 128, 128)
        ls = lax.rem(left, 128)
        back = lax.rem(128 - ls, 128)
        ta = pl.multiple_of(lax.div(top, 8) * 8, 8)
        rs = lax.rem(top, 8)
        rback = lax.rem(8 - rs, 8)
        for c in range(2):
            t = []
            for k in range(3):
                v = cov[c, pl.ds(ta, W + 8), pl.ds(la + 128 * k, H)]
                v = pltpu.roll(pltpu.roll(v, back, 1).reshape(33, 8, H), rback, 1)
                t.append(jnp.where(sub < 8 - rs, v[:32], v[1:]).reshape(W, H))
            for k in range(2):
                patch[c, :, 128 * k:128 * k + 128] = jnp.where(lane < 128 - ls, t[k], t[k + 1])
        for m in range(2):
            pr, pi = prv[0, m], prv[1, m]
            xr, xi = patch[0], patch[1]
            wr = pr * xr - pi * xi
            wi = pr * xi + pi * xr
            e = cat1(wr[:, :H] + wr[:, H:], wi[:, :H] + wi[:, H:])
            o = cat1(wr[:, :H] - wr[:, H:], wi[:, :H] - wi[:, H:])
            ye = rmul(e, rt[0])
            yo = rmul(o, rt[1])
            er, ei = cat1(ye[:, :H], yo[:, :H]), cat1(ye[:, H:], yo[:, H:])
            fe = cat0(er[:H] + er[H:], ei[:H] + ei[H:])
            fo = cat0(er[:H] - er[H:], ei[:H] - ei[H:])
            far[m, 0] = lmul(lt[2], fe)
            far[m, 1] = lmul(lt[3], fo)
        facs = []
        for p in range(2):
            mod = None
            for m in range(2):
                a = far[m, p]
                v = a[:H] * a[:H] + a[H:] * a[H:]
                mod = v if mod is None else mod + v
            facs.append(1.0 - sqv[s, H * p:H * p + H, :] * lax.rsqrt(jnp.maximum(mod, 0.1)))
        for m in range(2):
            be = lmul(lt[0], far[m, 0] * cat0(facs[0], facs[0]))
            bo = lmul(lt[1], far[m, 1] * cat0(facs[1], facs[1]))
            s_, d_ = be + bo, be - bo
            xr = cat0(s_[:H], d_[:H])
            xi = cat0(s_[H:], d_[H:])
            de = rmul(cat1(xr[:, :H], xi[:, :H]), rt[2])
            do = rmul(cat1(xr[:, H:], xi[:, H:]), rt[3])
            s_, d_ = de + do, de - do
            br = cat1(s_[:, :H], d_[:, :H])
            bi = cat1(s_[:, H:], d_[:, H:])
            pr, pi = prv[0, m], prv[1, m]
            xr, xi = patch[0], patch[1]
            tr, ti = pr * br + pi * bi, pr * bi - pi * br
            if m == 0:
                term[0], term[1] = tr, ti
            else:
                term[0] += tr
                term[1] += ti
            pacc[0, m] += xr * br + xi * bi
            pacc[1, m] += xr * bi - xi * br
        for c in range(2):
            r = [pltpu.roll(term[c, :, 128 * k:128 * k + 128], ls, 1) for k in range(2)]
            z = jnp.zeros_like(r[0])
            keep = lane >= ls
            parts = [jnp.where(keep, r[0], z), jnp.where(keep, r[1], r[0]), jnp.where(keep, z, r[1])]
            for k in range(3):
                v = pltpu.roll(parts[k].reshape(32, 8, H), rs, 1)
                z8 = jnp.zeros((1, 8, H), f32)
                v = jnp.where(sub9 >= rs, jnp.concatenate([v, z8], 0), jnp.concatenate([z8, v], 0))
                acc[c, pl.ds(ta, W + 8), pl.ds(la + 128 * k, H)] += v.reshape(W + 8, H)
        return carry

    lax.fori_loop(0, live[0], slot, 0)
    cov[:, 0:512, 0:512] = cov[:, 0:512, 0:512] - 0.5 * acc[:, 0:512, 0:512]
    outs = [
        (cov.at[:, 0:512, 0:512], o_part),
        (acc.at[:, 0:256, 512:768], o_rtop),
        (acc.at[:, 256:512, 512:768], o_rbot),
        (acc.at[:, 512:768, 512:768], o_corner),
        (acc.at[:, 512:768, 0:512], o_below),
        (pacc, o_probe),
    ]
    copies = [pltpu.make_async_copy(s, d, sems.at[i]) for i, (s, d) in enumerate(outs)]
    for c in copies:
        c.start()
    for c in copies:
        c.wait()


def main_call(offs, live, anchor, obj, right_top, right_bot, below, corner, probe, sq):
    rhs, lhs = (jnp.asarray(t) for t in make_tables())
    any_ = pl.BlockSpec(memory_space=pl.ANY)
    smem = pl.BlockSpec(memory_space=pltpu.SMEM)
    S = lambda *s: jax.ShapeDtypeStruct(s, f32)
    return pl.pallas_call(
        main_kernel,
        out_shape=(S(2, 512, 512), S(2, 256, 256), S(2, 256, 256), S(2, 256, 256), S(2, 256, 512), S(2, 2, 256, 256)),
        in_specs=[smem] * 3 + [any_] * 9,
        out_specs=[any_] * 6,
        scratch_shapes=[
            pltpu.VMEM((2, 768, 768), f32),
            pltpu.VMEM((2, 768, 768), f32),
            pltpu.VMEM((2, W, W), f32),
            pltpu.VMEM((2, 2, W, W), f32),
            pltpu.VMEM((2, 2, W, W), f32),
            pltpu.VMEM((8, W, W), f32),
            pltpu.VMEM((4, 768, W), bf16),
            pltpu.VMEM((4, W, 768), bf16),
            pltpu.VMEM((2, 2, W, W), f32),
            pltpu.VMEM((2, W, W), f32),
            pltpu.SemaphoreType.DMA((9,)),
        ],
        compiler_params=pltpu.CompilerParams(vmem_limit_bytes=40 * 2**20),
        name="slots",
    )(offs, live, anchor, obj, right_top, right_bot, below, corner, probe, sq, rhs, lhs)


def prep_kernel(counts, pm, pmt, out):
    i = counts[0].astype(f32).astype(bf16)
    a = jnp.dot(pm[...], i, preferred_element_type=f32).astype(bf16)
    out[0] = jnp.sqrt(jnp.dot(a, pmt[...], preferred_element_type=f32))


def prep_call(counts):
    order = np.concatenate([np.arange(0, W, 2), np.arange(1, W, 2)])
    pm = np.zeros((W, W), np.float32)
    pm[np.arange(W), order] = 1.0
    full = pl.BlockSpec((W, W), lambda s: (0, 0))
    blk = pl.BlockSpec((1, W, W), lambda s: (s, 0, 0))
    return pl.pallas_call(
        prep_kernel,
        grid=(8,),
        out_shape=jax.ShapeDtypeStruct((8, W, W), f32),
        in_specs=[blk, full, full],
        out_specs=blk,
        name="roots",
    )(counts, jnp.asarray(pm.astype(ml_dtypes.bfloat16)), jnp.asarray(pm.T.astype(ml_dtypes.bfloat16)))


def moved(value, axes, pairs):
    return lax.ppermute(value, axes, pairs)


def finish_kernel(part, above, top, bot, out):
    h = pl.program_id(1)

    @pl.when(h == 0)
    def _():
        out[0] = part[0] - 0.5 * above[0]
        out[0, :, :W] -= 0.5 * top[0]

    @pl.when(h == 1)
    def _():
        out[0, :, W:] = part[0, :, W:]
        out[0, :, :W] = part[0, :, :W] - 0.5 * bot[0]


def finish_call(part, above, top, bot):
    wide = pl.BlockSpec((1, W, 512), lambda c, h: (c, h, 0))
    return pl.pallas_call(
        finish_kernel,
        grid=(2, 2),
        out_shape=jax.ShapeDtypeStruct((2, 512, 512), f32),
        in_specs=[
            wide,
            pl.BlockSpec((1, W, 512), lambda c, h: (c, 0, 0)),
            pl.BlockSpec((1, W, W), lambda c, h: (c, 0, 0)),
            pl.BlockSpec((1, W, W), lambda c, h: (c, 0, 0)),
        ],
        out_specs=wide,
        name="finish",
    )(part, above, top, bot)


def swap_cores(value):
    return lax.ppermute(value, "core", [(0, 1), (1, 0)])


def summed_over_all(x):
    n = x.shape[0] // 2
    chips = lax.axis_size("y") * lax.axis_size("col")
    c = lax.axis_index("core")
    mine = lax.dynamic_slice_in_dim(x, c * n, n, 0)
    other = lax.dynamic_slice_in_dim(x, (1 - c) * n, n, 0)
    half = mine + swap_cores(other)
    rows = n // chips
    axes = ("y", "col")
    piece = lax.all_to_all(half.reshape(chips, rows, W), axes, 0, 0).sum(0)
    half = lax.all_to_all(jnp.broadcast_to(piece[None], (chips, rows, W)), axes, 0, 0).reshape(n, W)
    rest = swap_cores(half)
    return jnp.where(c == 0, jnp.concatenate([half, rest], 0), jnp.concatenate([rest, half], 0))


def shards(object_planes, probe_planes, offsets, photon_counts, live_counts):
    n_row = lax.axis_size("y") * lax.axis_size("core")
    n_col = lax.axis_size("col")
    rows = ("y", "core")
    row = lax.axis_index(rows)
    col = lax.axis_index("col")
    up = [(i, i - 1) for i in range(1, n_row)]
    down = [(i - 1, i) for i in range(1, n_row)]
    to_left = [(i, i - 1) for i in range(1, n_col)]
    to_right = [(i - 1, i) for i in range(1, n_col)]

    right_top = lax.ppermute(object_planes[:, :W, :W], "col", to_left)
    below = lax.ppermute(object_planes[:, :W, :], rows, up)
    right_bot = lax.ppermute(object_planes[:, W:, :W], "col", to_left)
    corner = lax.ppermute(right_top, rows, up)
    roots = prep_call(photon_counts)
    anchor = jnp.stack([row * 512, col * 512]).astype(jnp.int32)
    part, g_top, g_bot, g_corner, g_below, g_probe = main_call(
        offsets, live_counts.reshape(1), anchor, object_planes, right_top, right_bot, below, corner, probe_planes, roots
    )
    corner_in = lax.ppermute(g_corner, rows, down)
    bot_in = lax.ppermute(g_bot, "col", to_right)
    above_in = lax.ppermute(g_below, rows, down)
    top_in = lax.ppermute(g_top + corner_in, "col", to_right)
    total = summed_over_all(g_probe.reshape(1024, W)).reshape(probe_planes.shape)
    new_probe = probe_planes - total * (1.0 / math.sqrt(offsets.shape[0] * n_row * n_col))
    new_object = finish_call(part, above_in, top_in, bot_in)
    return new_object, new_probe


def solution(mesh):
    split = jax.sharding.Mesh(
        mesh.devices.reshape(mesh.shape["row"] // 2, 2, mesh.shape["col"]), ("y", "core", "col")
    )
    rows = ("y", "core")
    in_specs = (
        P(None, rows, "col"),
        P(),
        P(("y", "core", "col"), None),
        P(("y", "core", "col"), None, None),
        P(rows, "col"),
    )
    out_specs = (P(None, rows, "col"), P())
    return jax.shard_map(shards, mesh=split, in_specs=in_specs, out_specs=out_specs, check_vma=False)
```

```python
import math

import ml_dtypes
import numpy as np
import jax
import jax.numpy as jnp
from jax import lax
from jax.experimental import pallas as pl
from jax.experimental.pallas import tpu as pltpu
from jax.sharding import PartitionSpec as P

f32, bf16 = jnp.float32, jnp.bfloat16
W = 256
H = 128


def make_tables():
    b = np.arange(H)[:, None]
    q = np.arange(H)[None, :]
    right = []
    for p in (0, 1):
        ang = 2.0 * np.pi * (((2 * q + p) * b) % W) / W
        c, s = np.cos(ang) / 16.0, np.sin(ang) / 16.0
        right.append(np.block([[c, -s], [s, c]]))
    def split(t):
        hi = t.astype(np.float32).astype(ml_dtypes.bfloat16)
        lo = (t - hi.astype(np.float64)).astype(np.float32).astype(ml_dtypes.bfloat16)
        return hi, lo
    as_rhs = []
    as_lhs = []
    for t in (right[0], right[1], right[0].T, right[1].T):
        hi, lo = split(t)
        as_rhs.append(np.concatenate([hi, hi, lo], 0))
        as_lhs.append(np.concatenate([hi, hi, lo], 1))
    rhs = np.stack(as_rhs)
    lhs = np.stack(as_lhs)
    return rhs, lhs


def split(x):
    hi = x.astype(bf16)
    lo = (x - hi.astype(f32)).astype(bf16)
    return hi, lo


def rmul(x, t):
    hi, lo = split(x)
    return jnp.dot(jnp.concatenate([hi, lo, hi], 1), t, preferred_element_type=f32)


def lmul(t, x):
    hi, lo = split(x)
    return jnp.dot(t, jnp.concatenate([hi, lo, hi], 0), preferred_element_type=f32)


def cat1(a, b):
    return jnp.concatenate([a, b], 1)


def cat0(a, b):
    return jnp.concatenate([a, b], 0)


def main_kernel(offs, live, anchor, obj, right_top, right_bot, below, corner, probe, sq, rhs, lhs,
                o_part, o_rtop, o_rbot, o_corner, o_below, o_probe,
                cov, acc, patch, pacc, prv, sqv, rt, lt, far, term, sems):
    ins = [
        (obj, cov.at[:, 0:512, 0:512]),
        (right_top, cov.at[:, 0:256, 512:768]),
        (right_bot, cov.at[:, 256:512, 512:768]),
        (below, cov.at[:, 512:768, 0:512]),
        (corner, cov.at[:, 512:768, 512:768]),
        (probe, prv),
        (rhs, rt),
        (lhs, lt),
        (sq, sqv),
    ]
    copies = [pltpu.make_async_copy(s, d, sems.at[i]) for i, (s, d) in enumerate(ins)]
    for c in copies:
        c.start()
    acc[...] = jnp.zeros_like(acc)
    pacc[...] = jnp.zeros_like(pacc)
    for c in copies:
        c.wait()
    lane = lax.broadcasted_iota(jnp.int32, (W, H), 1)
    sub9 = lax.broadcasted_iota(jnp.int32, (33, 8, H), 1)
    sub = lax.broadcasted_iota(jnp.int32, (32, 8, H), 1)

    def slot(s, carry):
        top = offs[s, 0] - anchor[0]
        left = offs[s, 1] - anchor[1]
        la = pl.multiple_of(lax.div(left, 128) * 128, 128)
        ls = lax.rem(left, 128)
        back = lax.rem(128 - ls, 128)
        ta = pl.multiple_of(lax.div(top, 8) * 8, 8)
        rs = lax.rem(top, 8)
        rback = lax.rem(8 - rs, 8)
        for c in range(2):
            t = []
            for k in range(3):
                v = cov[c, pl.ds(ta, W + 8), pl.ds(la + 128 * k, H)]
                v = pltpu.roll(pltpu.roll(v, back, 1).reshape(33, 8, H), rback, 1)
                t.append(jnp.where(sub < 8 - rs, v[:32], v[1:]).reshape(W, H))
            for k in range(2):
                patch[c, :, 128 * k:128 * k + 128] = jnp.where(lane < 128 - ls, t[k], t[k + 1])
        for m in range(2):
            pr, pi = prv[0, m], prv[1, m]
            xr, xi = patch[0], patch[1]
            wr = pr * xr - pi * xi
            wi = pr * xi + pi * xr
            e = cat1(wr[:, :H] + wr[:, H:], wi[:, :H] + wi[:, H:])
            o = cat1(wr[:, :H] - wr[:, H:], wi[:, :H] - wi[:, H:])
            ye = rmul(e, rt[0])
            yo = rmul(o, rt[1])
            er, ei = cat1(ye[:, :H], yo[:, :H]), cat1(ye[:, H:], yo[:, H:])
            fe = cat0(er[:H] + er[H:], ei[:H] + ei[H:])
            fo = cat0(er[:H] - er[H:], ei[:H] - ei[H:])
            far[m, 0] = lmul(lt[2], fe)
            far[m, 1] = lmul(lt[3], fo)
        facs = []
        for p in range(2):
            mod = None
            for m in range(2):
                a = far[m, p]
                v = a[:H] * a[:H] + a[H:] * a[H:]
                mod = v if mod is None else mod + v
            facs.append(1.0 - sqv[s, H * p:H * p + H, :] * lax.rsqrt(jnp.maximum(mod, 0.1)))
        for m in range(2):
            be = lmul(lt[0], far[m, 0] * cat0(facs[0], facs[0]))
            bo = lmul(lt[1], far[m, 1] * cat0(facs[1], facs[1]))
            s_, d_ = be + bo, be - bo
            xr = cat0(s_[:H], d_[:H])
            xi = cat0(s_[H:], d_[H:])
            de = rmul(cat1(xr[:, :H], xi[:, :H]), rt[2])
            do = rmul(cat1(xr[:, H:], xi[:, H:]), rt[3])
            s_, d_ = de + do, de - do
            br = cat1(s_[:, :H], d_[:, :H])
            bi = cat1(s_[:, H:], d_[:, H:])
            pr, pi = prv[0, m], prv[1, m]
            xr, xi = patch[0], patch[1]
            tr, ti = pr * br + pi * bi, pr * bi - pi * br
            if m == 0:
                term[0], term[1] = tr, ti
            else:
                term[0] += tr
                term[1] += ti
            pacc[0, m] += xr * br + xi * bi
            pacc[1, m] += xr * bi - xi * br
        for c in range(2):
            r = [pltpu.roll(term[c, :, 128 * k:128 * k + 128], ls, 1) for k in range(2)]
            z = jnp.zeros_like(r[0])
            keep = lane >= ls
            parts = [jnp.where(keep, r[0], z), jnp.where(keep, r[1], r[0]), jnp.where(keep, z, r[1])]
            for k in range(3):
                v = pltpu.roll(parts[k].reshape(32, 8, H), rs, 1)
                z8 = jnp.zeros((1, 8, H), f32)
                v = jnp.where(sub9 >= rs, jnp.concatenate([v, z8], 0), jnp.concatenate([z8, v], 0))
                acc[c, pl.ds(ta, W + 8), pl.ds(la + 128 * k, H)] += v.reshape(W + 8, H)
        return carry

    lax.fori_loop(0, live[0], slot, 0)
    cov[:, 0:512, 0:512] = cov[:, 0:512, 0:512] - 0.5 * acc[:, 0:512, 0:512]
    outs = [
        (cov.at[:, 0:512, 0:512], o_part),
        (acc.at[:, 0:256, 512:768], o_rtop),
        (acc.at[:, 256:512, 512:768], o_rbot),
        (acc.at[:, 512:768, 512:768], o_corner),
        (acc.at[:, 512:768, 0:512], o_below),
        (pacc, o_probe),
    ]
    copies = [pltpu.make_async_copy(s, d, sems.at[i]) for i, (s, d) in enumerate(outs)]
    for c in copies:
        c.start()
    for c in copies:
        c.wait()


def main_call(offs, live, anchor, obj, right_top, right_bot, below, corner, probe, sq):
    rhs, lhs = (jnp.asarray(t) for t in make_tables())
    any_ = pl.BlockSpec(memory_space=pl.ANY)
    smem = pl.BlockSpec(memory_space=pltpu.SMEM)
    S = lambda *s: jax.ShapeDtypeStruct(s, f32)
    return pl.pallas_call(
        main_kernel,
        out_shape=(S(2, 512, 512), S(2, 256, 256), S(2, 256, 256), S(2, 256, 256), S(2, 256, 512), S(2, 2, 256, 256)),
        in_specs=[smem] * 3 + [any_] * 9,
        out_specs=[any_] * 6,
        scratch_shapes=[
            pltpu.VMEM((2, 768, 768), f32),
            pltpu.VMEM((2, 768, 768), f32),
            pltpu.VMEM((2, W, W), f32),
            pltpu.VMEM((2, 2, W, W), f32),
            pltpu.VMEM((2, 2, W, W), f32),
            pltpu.VMEM((8, W, W), f32),
            pltpu.VMEM((4, 768, W), bf16),
            pltpu.VMEM((4, W, 768), bf16),
            pltpu.VMEM((2, 2, W, W), f32),
            pltpu.VMEM((2, W, W), f32),
            pltpu.SemaphoreType.DMA((9,)),
        ],
        compiler_params=pltpu.CompilerParams(vmem_limit_bytes=62 * 2**20),
        name="slots",
    )(offs, live, anchor, obj, right_top, right_bot, below, corner, probe, sq, rhs, lhs)


def prep_kernel(counts, pm, pmt, out):
    i = counts[0].astype(f32).astype(bf16)
    a = jnp.dot(pm[...], i, preferred_element_type=f32).astype(bf16)
    out[0] = jnp.sqrt(jnp.dot(a, pmt[...], preferred_element_type=f32))


def prep_call(counts):
    order = np.concatenate([np.arange(0, W, 2), np.arange(1, W, 2)])
    pm = np.zeros((W, W), np.float32)
    pm[np.arange(W), order] = 1.0
    full = pl.BlockSpec((W, W), lambda s: (0, 0))
    blk = pl.BlockSpec((1, W, W), lambda s: (s, 0, 0))
    return pl.pallas_call(
        prep_kernel,
        grid=(8,),
        out_shape=jax.ShapeDtypeStruct((8, W, W), f32),
        in_specs=[blk, full, full],
        out_specs=blk,
        name="roots",
    )(counts, jnp.asarray(pm.astype(ml_dtypes.bfloat16)), jnp.asarray(pm.T.astype(ml_dtypes.bfloat16)))


def moved(value, axes, pairs):
    return lax.ppermute(value, axes, pairs)


def finish_kernel(part, above, left, out):
    h = pl.program_id(1)
    out[0, :, :W] = part[0, :, :W] - 0.5 * left[0]

    @pl.when(h == 0)
    def _():
        out[0, :, :W] -= 0.5 * above[0, :, :W]
        out[0, :, W:] = part[0, :, W:] - 0.5 * above[0, :, W:]

    @pl.when(h == 1)
    def _():
        out[0, :, W:] = part[0, :, W:]


def finish_call(part, above, left):
    wide = pl.BlockSpec((1, W, 512), lambda c, h: (c, h, 0))
    return pl.pallas_call(
        finish_kernel,
        grid=(2, 2),
        out_shape=jax.ShapeDtypeStruct((2, 512, 512), f32),
        in_specs=[
            wide,
            pl.BlockSpec((1, W, 512), lambda c, h: (c, 0, 0)),
            pl.BlockSpec((1, W, W), lambda c, h: (c, h, 0)),
        ],
        out_specs=wide,
        name="finish",
    )(part, above, left)


def swap_cores(value):
    return lax.ppermute(value, "core", [(0, 1), (1, 0)])


def core_half(x):
    n = x.shape[0] // 2
    chips = lax.axis_size("y") * lax.axis_size("col")
    c = lax.axis_index("core")
    mine = lax.dynamic_slice_in_dim(x, c * n, n, 0)
    other = lax.dynamic_slice_in_dim(x, (1 - c) * n, n, 0)
    return (mine + swap_cores(other)).reshape(chips, n // chips, W)


def both_halves(half):
    rest = swap_cores(half)
    first = lax.axis_index("core") == 0
    return jnp.where(first, jnp.concatenate([half, rest], 0), jnp.concatenate([rest, half], 0))


def shards(object_planes, probe_planes, offsets, photon_counts, live_counts):
    n_row = lax.axis_size("y") * lax.axis_size("core")
    n_col = lax.axis_size("col")
    rows = ("y", "core")
    axes = ("y", "col")
    row = lax.axis_index(rows)
    col = lax.axis_index("col")
    up = [(i, i - 1) for i in range(1, n_row)]
    down = [(i - 1, i) for i in range(1, n_row)]
    to_left = [(i, i - 1) for i in range(1, n_col)]
    to_right = [(i - 1, i) for i in range(1, n_col)]

    right_top = lax.ppermute(object_planes[:, :W, :W], "col", to_left)
    below = lax.ppermute(object_planes[:, :W, :], rows, up)
    right_bot = lax.ppermute(object_planes[:, W:, :W], "col", to_left)
    corner = lax.ppermute(right_top, rows, up)
    roots = prep_call(photon_counts)
    anchor = jnp.stack([row * 512, col * 512]).astype(jnp.int32)
    part, g_top, g_bot, g_corner, g_below, g_probe = main_call(
        offsets, live_counts.reshape(1), anchor, object_planes, right_top, right_bot, below, corner, probe_planes, roots
    )
    corner_in = lax.ppermute(g_corner, rows, down)
    above_in = lax.ppermute(g_below, rows, down)
    g_right = jnp.concatenate([g_top + corner_in, g_bot], 1)
    left_in = lax.ppermute(g_right, "col", to_right)
    pieces = core_half(g_probe.reshape(1024, W))

    def exchange(step, pieces):
        got = lax.all_to_all(pieces, axes, 0, 0)
        return jnp.where(step == 0, jnp.broadcast_to(got.sum(0)[None], got.shape), got)

    pieces = lax.fori_loop(0, 2, exchange, pieces)
    pieces, left_in, above_in = lax.optimization_barrier((pieces, left_in, above_in))
    total = both_halves(pieces.reshape(512, W)).reshape(probe_planes.shape)
    new_probe = probe_planes - total * (1.0 / math.sqrt(offsets.shape[0] * n_row * n_col))
    new_object = finish_call(part, above_in, left_in)
    return new_object, new_probe


def solution(mesh):
    split = jax.sharding.Mesh(
        mesh.devices.reshape(mesh.shape["row"] // 2, 2, mesh.shape["col"]), ("y", "core", "col")
    )
    rows = ("y", "core")
    in_specs = (
        P(None, rows, "col"),
        P(),
        P(("y", "core", "col"), None),
        P(("y", "core", "col"), None, None),
        P(rows, "col"),
    )
    out_specs = (P(None, rows, "col"), P())
    return jax.shard_map(shards, mesh=split, in_specs=in_specs, out_specs=out_specs, check_vma=False)
```

```python
import functools
import math

import ml_dtypes
import numpy as np
import jax
import jax.numpy as jnp
from jax import lax
from jax.experimental import pallas as pl
from jax.experimental.pallas import tpu as pltpu
from jax.sharding import PartitionSpec as P

f32, bf16 = jnp.float32, jnp.bfloat16
W = 256
H = 128


def make_tables():
    b = np.arange(H)[:, None]
    q = np.arange(H)[None, :]
    right = []
    for p in (0, 1):
        ang = 2.0 * np.pi * (((2 * q + p) * b) % W) / W
        c, s = np.cos(ang) / 16.0, np.sin(ang) / 16.0
        right.append(np.block([[c, -s], [s, c]]))
    def split(t):
        hi = t.astype(np.float32).astype(ml_dtypes.bfloat16)
        lo = (t - hi.astype(np.float64)).astype(np.float32).astype(ml_dtypes.bfloat16)
        return hi, lo
    as_rhs = []
    as_lhs = []
    for t in (right[0], right[1], right[0].T, right[1].T):
        hi, lo = split(t)
        as_rhs.append(np.concatenate([hi, hi, lo], 0))
        as_lhs.append(np.concatenate([hi, hi, lo], 1))
    rhs = np.stack(as_rhs)
    lhs = np.stack(as_lhs)
    return rhs, lhs


def split(x):
    hi = x.astype(bf16)
    lo = (x - hi.astype(f32)).astype(bf16)
    return hi, lo


def rmul(x, t):
    hi, lo = split(x)
    return jnp.dot(jnp.concatenate([hi, lo, hi], 1), t, preferred_element_type=f32)


def lmul(t, x):
    hi, lo = split(x)
    return jnp.dot(t, jnp.concatenate([hi, lo, hi], 0), preferred_element_type=f32)


def cat1(a, b):
    return jnp.concatenate([a, b], 1)


def cat0(a, b):
    return jnp.concatenate([a, b], 0)


def main_kernel(offs, live, anchor, obj, right_top, right_bot, below, corner, probe, sq, rhs, lhs,
                o_part, o_rtop, o_rbot, o_corner, o_below, o_mine, o_other,
                cov, acc, patch, pacc, prv, sqv, rt, lt, far, term, sems):
    ins = [
        (obj, cov.at[:, 0:512, 0:512]),
        (right_top, cov.at[:, 0:256, 512:768]),
        (right_bot, cov.at[:, 256:512, 512:768]),
        (below, cov.at[:, 512:768, 0:512]),
        (corner, cov.at[:, 512:768, 512:768]),
        (probe, prv),
        (rhs, rt),
        (lhs, lt),
        (sq, sqv),
    ]
    copies = [pltpu.make_async_copy(s, d, sems.at[i]) for i, (s, d) in enumerate(ins)]
    for c in copies:
        c.start()
    acc[...] = jnp.zeros_like(acc)
    pacc[...] = jnp.zeros_like(pacc)
    for c in copies:
        c.wait()
    lane = lax.broadcasted_iota(jnp.int32, (W, H), 1)
    sub9 = lax.broadcasted_iota(jnp.int32, (33, 8, H), 1)
    sub = lax.broadcasted_iota(jnp.int32, (32, 8, H), 1)

    def slot(s, carry):
        top = offs[s, 0] - anchor[0]
        left = offs[s, 1] - anchor[1]
        la = pl.multiple_of(lax.div(left, 128) * 128, 128)
        ls = lax.rem(left, 128)
        back = lax.rem(128 - ls, 128)
        ta = pl.multiple_of(lax.div(top, 8) * 8, 8)
        rs = lax.rem(top, 8)
        rback = lax.rem(8 - rs, 8)
        for c in range(2):
            t = []
            for k in range(3):
                v = cov[c, pl.ds(ta, W + 8), pl.ds(la + 128 * k, H)]
                v = pltpu.roll(pltpu.roll(v, back, 1).reshape(33, 8, H), rback, 1)
                t.append(jnp.where(sub < 8 - rs, v[:32], v[1:]).reshape(W, H))
            for k in range(2):
                patch[c, :, 128 * k:128 * k + 128] = jnp.where(lane < 128 - ls, t[k], t[k + 1])
        for m in range(2):
            pr, pi = prv[0, m], prv[1, m]
            xr, xi = patch[0], patch[1]
            wr = pr * xr - pi * xi
            wi = pr * xi + pi * xr
            e = cat1(wr[:, :H] + wr[:, H:], wi[:, :H] + wi[:, H:])
            o = cat1(wr[:, :H] - wr[:, H:], wi[:, :H] - wi[:, H:])
            ye = rmul(e, rt[0])
            yo = rmul(o, rt[1])
            er, ei = cat1(ye[:, :H], yo[:, :H]), cat1(ye[:, H:], yo[:, H:])
            fe = cat0(er[:H] + er[H:], ei[:H] + ei[H:])
            fo = cat0(er[:H] - er[H:], ei[:H] - ei[H:])
            far[m, 0] = lmul(lt[2], fe)
            far[m, 1] = lmul(lt[3], fo)
        facs = []
        for p in range(2):
            mod = None
            for m in range(2):
                a = far[m, p]
                v = a[:H] * a[:H] + a[H:] * a[H:]
                mod = v if mod is None else mod + v
            facs.append(1.0 - sqv[s, H * p:H * p + H, :] * lax.rsqrt(jnp.maximum(mod, 0.1)))
        for m in range(2):
            be = lmul(lt[0], far[m, 0] * cat0(facs[0], facs[0]))
            bo = lmul(lt[1], far[m, 1] * cat0(facs[1], facs[1]))
            s_, d_ = be + bo, be - bo
            xr = cat0(s_[:H], d_[:H])
            xi = cat0(s_[H:], d_[H:])
            de = rmul(cat1(xr[:, :H], xi[:, :H]), rt[2])
            do = rmul(cat1(xr[:, H:], xi[:, H:]), rt[3])
            s_, d_ = de + do, de - do
            br = cat1(s_[:, :H], d_[:, :H])
            bi = cat1(s_[:, H:], d_[:, H:])
            pr, pi = prv[0, m], prv[1, m]
            xr, xi = patch[0], patch[1]
            tr, ti = pr * br + pi * bi, pr * bi - pi * br
            if m == 0:
                term[0], term[1] = tr, ti
            else:
                term[0] += tr
                term[1] += ti
            pacc[0, m] += xr * br + xi * bi
            pacc[1, m] += xr * bi - xi * br
        for c in range(2):
            r = [pltpu.roll(term[c, :, 128 * k:128 * k + 128], ls, 1) for k in range(2)]
            z = jnp.zeros_like(r[0])
            keep = lane >= ls
            parts = [jnp.where(keep, r[0], z), jnp.where(keep, r[1], r[0]), jnp.where(keep, z, r[1])]
            for k in range(3):
                v = pltpu.roll(parts[k].reshape(32, 8, H), rs, 1)
                z8 = jnp.zeros((1, 8, H), f32)
                v = jnp.where(sub9 >= rs, jnp.concatenate([v, z8], 0), jnp.concatenate([z8, v], 0))
                acc[c, pl.ds(ta, W + 8), pl.ds(la + 128 * k, H)] += v.reshape(W + 8, H)
        return carry

    lax.fori_loop(0, live[0], slot, 0)
    for n, (kc, kz, kx, ky) in enumerate(np.ndindex(2, 4, 4, 4)):
        c = lax.rem(anchor[2] + kc, 2)
        row = lax.rem(anchor[3] + kz, 4) * 128 + lax.rem(anchor[4] + kx, 4) * 32 + lax.rem(anchor[5] + ky, 4) * 8
        r = pl.multiple_of(lax.rem(row, W), 8)
        n8 = n % 64 * 8
        prv[kc, n8 // W, n8 % W:n8 % W + 8, :] = pacc[c, lax.div(row, W), pl.ds(r, 8), :]
    cov[:, 0:512, 0:512] = cov[:, 0:512, 0:512] - 0.5 * acc[:, 0:512, 0:512]
    outs = [
        (cov.at[:, 0:512, 0:512], o_part),
        (acc.at[:, 0:256, 512:768], o_rtop),
        (acc.at[:, 256:512, 512:768], o_rbot),
        (acc.at[:, 512:768, 512:768], o_corner),
        (acc.at[:, 512:768, 0:512], o_below),
        (prv.at[0], o_mine),
        (prv.at[1], o_other),
    ]
    copies = [pltpu.make_async_copy(s, d, sems.at[i]) for i, (s, d) in enumerate(outs)]
    for c in copies:
        c.start()
    for c in copies:
        c.wait()


def main_call(offs, live, anchor, obj, right_top, right_bot, below, corner, probe, sq):
    rhs, lhs = (jnp.asarray(t) for t in make_tables())
    any_ = pl.BlockSpec(memory_space=pl.ANY)
    smem = pl.BlockSpec(memory_space=pltpu.SMEM)
    S = lambda *s: jax.ShapeDtypeStruct(s, f32)
    return pl.pallas_call(
        main_kernel,
        out_shape=(S(2, 512, 512), S(2, 256, 256), S(2, 256, 256), S(2, 256, 256), S(2, 256, 512), S(2, 256, 256), S(2, 256, 256)),
        in_specs=[smem] * 3 + [any_] * 9,
        out_specs=[any_] * 7,
        scratch_shapes=[
            pltpu.VMEM((2, 768, 768), f32),
            pltpu.VMEM((2, 768, 768), f32),
            pltpu.VMEM((2, W, W), f32),
            pltpu.VMEM((2, 2, W, W), f32),
            pltpu.VMEM((2, 2, W, W), f32),
            pltpu.VMEM((8, W, W), f32),
            pltpu.VMEM((4, 768, W), bf16),
            pltpu.VMEM((4, W, 768), bf16),
            pltpu.VMEM((2, 2, W, W), f32),
            pltpu.VMEM((2, W, W), f32),
            pltpu.SemaphoreType.DMA((9,)),
        ],
        compiler_params=pltpu.CompilerParams(vmem_limit_bytes=62 * 2**20),
        name="slots",
    )(offs, live, anchor, obj, right_top, right_bot, below, corner, probe, sq, rhs, lhs)


def prep_kernel(counts, pm, pmt, out):
    i = counts[0].astype(f32).astype(bf16)
    a = jnp.dot(pm[...], i, preferred_element_type=f32).astype(bf16)
    out[0] = jnp.sqrt(jnp.dot(a, pmt[...], preferred_element_type=f32))


def prep_call(counts):
    order = np.concatenate([np.arange(0, W, 2), np.arange(1, W, 2)])
    pm = np.zeros((W, W), np.float32)
    pm[np.arange(W), order] = 1.0
    full = pl.BlockSpec((W, W), lambda s: (0, 0))
    blk = pl.BlockSpec((1, W, W), lambda s: (s, 0, 0))
    return pl.pallas_call(
        prep_kernel,
        grid=(8,),
        out_shape=jax.ShapeDtypeStruct((8, W, W), f32),
        in_specs=[blk, full, full],
        out_specs=blk,
        name="roots",
    )(counts, jnp.asarray(pm.astype(ml_dtypes.bfloat16)), jnp.asarray(pm.T.astype(ml_dtypes.bfloat16)))


def moved(value, axes, pairs):
    return lax.ppermute(value, axes, pairs)


def finish_kernel(part, above, left, out):
    h = pl.program_id(1)
    out[0, :, :W] = part[0, :, :W] - 0.5 * left[0]

    @pl.when(h == 0)
    def _():
        out[0, :, :W] -= 0.5 * above[0, :, :W]
        out[0, :, W:] = part[0, :, W:] - 0.5 * above[0, :, W:]

    @pl.when(h == 1)
    def _():
        out[0, :, W:] = part[0, :, W:]


def finish_call(part, above, left):
    wide = pl.BlockSpec((1, W, 512), lambda c, h: (c, h, 0))
    return pl.pallas_call(
        finish_kernel,
        grid=(2, 2),
        out_shape=jax.ShapeDtypeStruct((2, 512, 512), f32),
        in_specs=[
            wide,
            pl.BlockSpec((1, W, 512), lambda c, h: (c, 0, 0)),
            pl.BlockSpec((1, W, W), lambda c, h: (c, h, 0)),
        ],
        out_specs=wide,
        compiler_params=pltpu.CompilerParams(vmem_limit_bytes=8 * 2**20),
        name="finish",
    )(part, above, left)


def swap_cores(value):
    return lax.ppermute(value, "core", [(0, 1), (1, 0)])


def sum_along(pieces, axis):
    got = [lax.ppermute(pieces[k], axis, [(i, (i + k) % 4) for i in range(4)]) for k in (2, 1, 3)]
    return pieces[0] + got[0] + got[1] + got[2]


def spread_along(value, axis):
    return [value] + [lax.ppermute(value, axis, [(i, (i + k) % 4) for i in range(4)]) for k in (1, 2, 3)]


def probe_kernel(step, place, probe, z0, z1, z2, z3, rest, out):
    for n, (kc, kz, kx, ky) in enumerate(np.ndindex(2, 4, 4, 4)):
        c = lax.rem(place[2] + kc, 2)
        row = (
            lax.rem(place[3] - kz + 4, 4) * 128
            + lax.rem(place[4] - kx + 4, 4) * 32
            + lax.rem(place[5] - ky + 4, 4) * 8
        )
        at = pl.multiple_of(c * 512 + row, 8)
        total = (z0, z1, z2, z3)[kz][kx, ky] if kc == 0 else rest[kz, kx, ky]
        out[pl.ds(at, 8), :] = probe[pl.ds(at, 8), :] - step * total


def shards(object_planes, probe_planes, offsets, photon_counts, live_counts):
    n_row = lax.axis_size("y") * lax.axis_size("core")
    n_col = lax.axis_size("x") * lax.axis_size("z")
    rows, cols = ("y", "core"), ("x", "z")
    up = [(i, i - 1) for i in range(1, n_row)]
    down = [(i - 1, i) for i in range(1, n_row)]
    to_left = [(i, i - 1) for i in range(1, n_col)]
    to_right = [(i - 1, i) for i in range(1, n_col)]

    right_top = lax.ppermute(object_planes[:, :W, :W], cols, to_left)
    below = lax.ppermute(object_planes[:, :W, :], rows, up)
    right_bot = lax.ppermute(object_planes[:, W:, :W], cols, to_left)
    corner = lax.ppermute(right_top, rows, up)
    roots = prep_call(photon_counts)
    place = jnp.stack(
        [lax.axis_index(rows) * 512, lax.axis_index(cols) * 512] + [lax.axis_index(a) for a in ("core", "z", "x", "y")]
    ).astype(jnp.int32)
    part, g_top, g_bot, g_corner, g_below, mine, other = main_call(
        offsets, live_counts.reshape(1), place, object_planes, right_top, right_bot, below, corner, probe_planes, roots
    )
    corner_in = lax.ppermute(g_corner, rows, down)
    above_in = lax.ppermute(g_below, rows, down)
    half = (mine + swap_cores(other)).reshape(4, 4, 4, 8, W)
    piece = sum_along(half, "z")
    g_right = jnp.concatenate([g_top + corner_in, g_bot], 1)
    left_in = lax.ppermute(g_right, cols, to_right)
    piece = sum_along(piece, "x")
    piece = sum_along(piece, "y")
    piece = jnp.stack(spread_along(piece, "y"))
    piece = jnp.stack(spread_along(piece, "x"))
    piece, left_in, above_in = lax.optimization_barrier((piece, left_in, above_in))
    new_object = finish_call(part, above_in, left_in)
    quarters = spread_along(piece, "z")
    rest = swap_cores(jnp.stack(quarters))
    smem, vmem = pl.BlockSpec(memory_space=pltpu.SMEM), pl.BlockSpec(memory_space=pltpu.VMEM)
    step = 1.0 / math.sqrt(offsets.shape[0] * n_row * n_col)
    new_probe = pl.pallas_call(
        functools.partial(probe_kernel, step),
        out_shape=jax.ShapeDtypeStruct((1024, W), f32),
        in_specs=[smem] + [vmem] * 6,
        out_specs=vmem,
        compiler_params=pltpu.CompilerParams(vmem_limit_bytes=8 * 2**20),
        name="probe",
    )(place, probe_planes.reshape(1024, W), *quarters, rest)
    return new_object, new_probe.reshape(probe_planes.shape)


def solution(mesh):
    split = jax.sharding.Mesh(
        mesh.devices.reshape(mesh.shape["row"] // 2, 2, mesh.shape["col"] // 4, 4), ("y", "core", "x", "z")
    )
    rows, cols = ("y", "core"), ("x", "z")
    in_specs = (
        P(None, rows, cols),
        P(),
        P(rows + cols, None),
        P(rows + cols, None, None),
        P(rows, cols),
    )
    out_specs = (P(None, rows, cols), P())
    return jax.shard_map(shards, mesh=split, in_specs=in_specs, out_specs=out_specs, check_vma=False)
```

```python
import functools
import math

import ml_dtypes
import numpy as np
import jax
import jax.numpy as jnp
from jax import lax
from jax.experimental import pallas as pl
from jax.experimental.pallas import tpu as pltpu
from jax.sharding import PartitionSpec as P

f32, bf16 = jnp.float32, jnp.bfloat16
W = 256
H = 128


def make_tables():
    b = np.arange(H)[:, None]
    q = np.arange(H)[None, :]
    right = []
    for p in (0, 1):
        ang = 2.0 * np.pi * (((2 * q + p) * b) % W) / W
        c, s = np.cos(ang) / 16.0, np.sin(ang) / 16.0
        right.append(np.block([[c, -s], [s, c]]))
    def split(t):
        hi = t.astype(np.float32).astype(ml_dtypes.bfloat16)
        lo = (t - hi.astype(np.float64)).astype(np.float32).astype(ml_dtypes.bfloat16)
        return hi, lo
    as_rhs = []
    as_lhs = []
    for t in (right[0], right[1], right[0].T, right[1].T):
        hi, lo = split(t)
        as_rhs.append(np.concatenate([hi, hi, lo], 0))
        as_lhs.append(np.concatenate([hi, hi, lo], 1))
    rhs = np.stack(as_rhs)
    lhs = np.stack(as_lhs)
    return rhs, lhs


def split(x):
    hi = x.astype(bf16)
    lo = (x - hi.astype(f32)).astype(bf16)
    return hi, lo


def rmul(x, t):
    hi, lo = split(x)
    return jnp.dot(jnp.concatenate([hi, lo, hi], 1), t, preferred_element_type=f32)


def lmul(t, x):
    hi, lo = split(x)
    return jnp.dot(t, jnp.concatenate([hi, lo, hi], 0), preferred_element_type=f32)


def cat1(a, b):
    return jnp.concatenate([a, b], 1)


def cat0(a, b):
    return jnp.concatenate([a, b], 0)


def main_kernel(offs, live, anchor, obj, right_top, right_bot, below, corner, probe, sq, rhs, lhs,
                o_part, o_rtop, o_rbot, o_corner, o_below, o_mine, o_other,
                cov, acc, patch, pacc, prv, sqv, rt, lt, far, term, sems):
    ins = [
        (obj, cov.at[:, 0:512, 0:512]),
        (right_top, cov.at[:, 0:256, 512:768]),
        (right_bot, cov.at[:, 256:512, 512:768]),
        (below, cov.at[:, 512:768, 0:512]),
        (corner, cov.at[:, 512:768, 512:768]),
        (probe, prv),
        (rhs, rt),
        (lhs, lt),
        (sq, sqv),
    ]
    copies = [pltpu.make_async_copy(s, d, sems.at[i]) for i, (s, d) in enumerate(ins)]
    for c in copies:
        c.start()
    acc[...] = jnp.zeros_like(acc)
    pacc[...] = jnp.zeros_like(pacc)
    for c in copies:
        c.wait()
    lane = lax.broadcasted_iota(jnp.int32, (W, H), 1)
    sub9 = lax.broadcasted_iota(jnp.int32, (33, 8, H), 1)
    sub = lax.broadcasted_iota(jnp.int32, (32, 8, H), 1)

    def slot(s, carry):
        top = offs[s, 0] - anchor[0]
        left = offs[s, 1] - anchor[1]
        la = pl.multiple_of(lax.div(left, 128) * 128, 128)
        ls = lax.rem(left, 128)
        back = lax.rem(128 - ls, 128)
        ta = pl.multiple_of(lax.div(top, 8) * 8, 8)
        rs = lax.rem(top, 8)
        rback = lax.rem(8 - rs, 8)
        for c in range(2):
            t = []
            for k in range(3):
                v = cov[c, pl.ds(ta, W + 8), pl.ds(la + 128 * k, H)]
                v = pltpu.roll(pltpu.roll(v, back, 1).reshape(33, 8, H), rback, 1)
                t.append(jnp.where(sub < 8 - rs, v[:32], v[1:]).reshape(W, H))
            for k in range(2):
                patch[c, :, 128 * k:128 * k + 128] = jnp.where(lane < 128 - ls, t[k], t[k + 1])
        for m in range(2):
            pr, pi = prv[0, m], prv[1, m]
            xr, xi = patch[0], patch[1]
            wr = pr * xr - pi * xi
            wi = pr * xi + pi * xr
            e = cat1(wr[:, :H] + wr[:, H:], wi[:, :H] + wi[:, H:])
            o = cat1(wr[:, :H] - wr[:, H:], wi[:, :H] - wi[:, H:])
            ye = rmul(e, rt[0])
            yo = rmul(o, rt[1])
            er, ei = cat1(ye[:, :H], yo[:, :H]), cat1(ye[:, H:], yo[:, H:])
            fe = cat0(er[:H] + er[H:], ei[:H] + ei[H:])
            fo = cat0(er[:H] - er[H:], ei[:H] - ei[H:])
            far[m, 0] = lmul(lt[2], fe)
            far[m, 1] = lmul(lt[3], fo)
        facs = []
        for p in range(2):
            mod = None
            for m in range(2):
                a = far[m, p]
                v = a[:H] * a[:H] + a[H:] * a[H:]
                mod = v if mod is None else mod + v
            facs.append(1.0 - sqv[s, H * p:H * p + H, :] * lax.rsqrt(jnp.maximum(mod, 0.1)))
        for m in range(2):
            be = lmul(lt[0], far[m, 0] * cat0(facs[0], facs[0]))
            bo = lmul(lt[1], far[m, 1] * cat0(facs[1], facs[1]))
            s_, d_ = be + bo, be - bo
            xr = cat0(s_[:H], d_[:H])
            xi = cat0(s_[H:], d_[H:])
            de = rmul(cat1(xr[:, :H], xi[:, :H]), rt[2])
            do = rmul(cat1(xr[:, H:], xi[:, H:]), rt[3])
            s_, d_ = de + do, de - do
            br = cat1(s_[:, :H], d_[:, :H])
            bi = cat1(s_[:, H:], d_[:, H:])
            pr, pi = prv[0, m], prv[1, m]
            xr, xi = patch[0], patch[1]
            tr, ti = pr * br + pi * bi, pr * bi - pi * br
            if m == 0:
                term[0], term[1] = tr, ti
            else:
                term[0] += tr
                term[1] += ti
            pacc[0, m] += xr * br + xi * bi
            pacc[1, m] += xr * bi - xi * br
        for c in range(2):
            r = [pltpu.roll(term[c, :, 128 * k:128 * k + 128], ls, 1) for k in range(2)]
            z = jnp.zeros_like(r[0])
            keep = lane >= ls
            parts = [jnp.where(keep, r[0], z), jnp.where(keep, r[1], r[0]), jnp.where(keep, z, r[1])]
            for k in range(3):
                v = pltpu.roll(parts[k].reshape(32, 8, H), rs, 1)
                z8 = jnp.zeros((1, 8, H), f32)
                v = jnp.where(sub9 >= rs, jnp.concatenate([v, z8], 0), jnp.concatenate([z8, v], 0))
                acc[c, pl.ds(ta, W + 8), pl.ds(la + 128 * k, H)] += v.reshape(W + 8, H)
        return carry

    lax.fori_loop(0, live[0], slot, 0)
    for kc, kx in np.ndindex(2, 4):
        c, x = lax.rem(anchor[2] + kc, 2), lax.rem(anchor[3] + kx, 4)
        at = pl.multiple_of(lax.rem(x, 2) * H, H)
        prv[kc, kx // 2, kx % 2 * H:kx % 2 * H + H, :] = pacc[c, lax.div(x, 2), pl.ds(at, H), :]
    cov[:, 0:512, 0:512] = cov[:, 0:512, 0:512] - 0.5 * acc[:, 0:512, 0:512]
    outs = [
        (cov.at[:, 0:512, 0:512], o_part),
        (acc.at[:, 0:256, 512:768], o_rtop),
        (acc.at[:, 256:512, 512:768], o_rbot),
        (acc.at[:, 512:768, 512:768], o_corner),
        (acc.at[:, 512:768, 0:512], o_below),
        (prv.at[0], o_mine),
        (prv.at[1], o_other),
    ]
    copies = [pltpu.make_async_copy(s, d, sems.at[i]) for i, (s, d) in enumerate(outs)]
    for c in copies:
        c.start()
    for c in copies:
        c.wait()


def main_call(offs, live, anchor, obj, right_top, right_bot, below, corner, probe, sq):
    rhs, lhs = (jnp.asarray(t) for t in make_tables())
    any_ = pl.BlockSpec(memory_space=pl.ANY)
    smem = pl.BlockSpec(memory_space=pltpu.SMEM)
    S = lambda *s: jax.ShapeDtypeStruct(s, f32)
    return pl.pallas_call(
        main_kernel,
        out_shape=(S(2, 512, 512), S(2, 256, 256), S(2, 256, 256), S(2, 256, 256), S(2, 256, 512), S(2, 256, 256), S(2, 256, 256)),
        in_specs=[smem] * 3 + [any_] * 9,
        out_specs=[any_] * 7,
        scratch_shapes=[
            pltpu.VMEM((2, 768, 768), f32),
            pltpu.VMEM((2, 768, 768), f32),
            pltpu.VMEM((2, W, W), f32),
            pltpu.VMEM((2, 2, W, W), f32),
            pltpu.VMEM((2, 2, W, W), f32),
            pltpu.VMEM((8, W, W), f32),
            pltpu.VMEM((4, 768, W), bf16),
            pltpu.VMEM((4, W, 768), bf16),
            pltpu.VMEM((2, 2, W, W), f32),
            pltpu.VMEM((2, W, W), f32),
            pltpu.SemaphoreType.DMA((9,)),
        ],
        compiler_params=pltpu.CompilerParams(vmem_limit_bytes=62 * 2**20),
        name="slots",
    )(offs, live, anchor, obj, right_top, right_bot, below, corner, probe, sq, rhs, lhs)


def prep_kernel(counts, pm, pmt, out):
    i = counts[0].astype(f32).astype(bf16)
    a = jnp.dot(pm[...], i, preferred_element_type=f32).astype(bf16)
    out[0] = jnp.sqrt(jnp.dot(a, pmt[...], preferred_element_type=f32))


def prep_call(counts):
    order = np.concatenate([np.arange(0, W, 2), np.arange(1, W, 2)])
    pm = np.zeros((W, W), np.float32)
    pm[np.arange(W), order] = 1.0
    full = pl.BlockSpec((W, W), lambda s: (0, 0))
    blk = pl.BlockSpec((1, W, W), lambda s: (s, 0, 0))
    return pl.pallas_call(
        prep_kernel,
        grid=(8,),
        out_shape=jax.ShapeDtypeStruct((8, W, W), f32),
        in_specs=[blk, full, full],
        out_specs=blk,
        name="roots",
    )(counts, jnp.asarray(pm.astype(ml_dtypes.bfloat16)), jnp.asarray(pm.T.astype(ml_dtypes.bfloat16)))


def moved(value, axes, pairs):
    return lax.ppermute(value, axes, pairs)


def finish_kernel(part, above, top, bot, out):
    h = pl.program_id(1)

    @pl.when(h == 0)
    def _():
        out[0] = part[0] - 0.5 * above[0]
        out[0, :, :W] -= 0.5 * top[0]

    @pl.when(h == 1)
    def _():
        out[0, :, W:] = part[0, :, W:]
        out[0, :, :W] = part[0, :, :W] - 0.5 * bot[0]


def finish_call(part, above, top, bot):
    wide = pl.BlockSpec((1, W, 512), lambda c, h: (c, h, 0))
    return pl.pallas_call(
        finish_kernel,
        grid=(2, 2),
        out_shape=jax.ShapeDtypeStruct((2, 512, 512), f32),
        in_specs=[
            wide,
            pl.BlockSpec((1, W, 512), lambda c, h: (c, 0, 0)),
            pl.BlockSpec((1, W, W), lambda c, h: (c, 0, 0)),
            pl.BlockSpec((1, W, W), lambda c, h: (c, 0, 0)),
        ],
        out_specs=wide,
        compiler_params=pltpu.CompilerParams(vmem_limit_bytes=8 * 2**20),
        name="finish",
    )(part, above, top, bot)


def swap_cores(value):
    return lax.ppermute(value, "core", [(0, 1), (1, 0)])


def sum_along(pieces, axis):
    got = [lax.ppermute(pieces[k], axis, [(i, (i + k) % 4) for i in range(4)]) for k in (2, 1, 3)]
    return pieces[0] + got[0] + got[1] + got[2]


def spread_along(value, axis):
    return [value] + [lax.ppermute(value, axis, [(i, (i + k) % 4) for i in range(4)]) for k in (1, 2, 3)]


def sum_everywhere(value, axis):
    got = [lax.ppermute(value, axis, [(i, (i + k) % 4) for i in range(4)]) for k in (2, 1, 3)]
    return (value + got[0]) + (got[1] + got[2])


def probe_kernel(step, place, probe, x0, x1, x2, x3, rest, out):
    for kc, kx in np.ndindex(2, 4):
        row = lax.rem(place[2] + kc, 2) * 512 + lax.rem(place[3] - kx + 4, 4) * H
        at = pl.multiple_of(row, H)
        total = (x0, x1, x2, x3)[kx][...] if kc == 0 else rest[kx]
        out[pl.ds(at, H), :] = probe[pl.ds(at, H), :] - step * total


def shards(object_planes, probe_planes, offsets, photon_counts, live_counts):
    n_row = lax.axis_size("y") * lax.axis_size("core")
    n_col = lax.axis_size("x") * lax.axis_size("z")
    rows, cols = ("y", "core"), ("x", "z")
    up = [(i, i - 1) for i in range(1, n_row)]
    down = [(i - 1, i) for i in range(1, n_row)]
    to_left = [(i, i - 1) for i in range(1, n_col)]
    to_right = [(i - 1, i) for i in range(1, n_col)]

    right_top = lax.ppermute(object_planes[:, :W, :W], cols, to_left)
    below = lax.ppermute(object_planes[:, :W, :], rows, up)
    right_bot = lax.ppermute(object_planes[:, W:, :W], cols, to_left)
    corner = lax.ppermute(right_top, rows, up)
    roots = prep_call(photon_counts)
    place = jnp.stack(
        [lax.axis_index(rows) * 512, lax.axis_index(cols) * 512] + [lax.axis_index(a) for a in ("core", "x")]
    ).astype(jnp.int32)
    part, g_top, g_bot, g_corner, g_below, mine, other = main_call(
        offsets, live_counts.reshape(1), place, object_planes, right_top, right_bot, below, corner, probe_planes, roots
    )
    corner_in = lax.ppermute(g_corner, rows, down)
    bot_in = lax.ppermute(g_bot, cols, to_right)
    above_in = lax.ppermute(g_below, rows, down)
    half = (mine + swap_cores(other)).reshape(4, H, W)
    top_in = lax.ppermute(g_top + corner_in, cols, to_right)
    piece = sum_along(half, "x")
    piece = sum_everywhere(piece, "y")
    piece, bot_in, top_in = lax.optimization_barrier((piece, bot_in, top_in))
    piece = sum_everywhere(piece, "z")
    new_object = finish_call(part, above_in, top_in, bot_in)
    quarters = spread_along(piece, "x")
    rest = swap_cores(jnp.stack(quarters))
    smem, vmem = pl.BlockSpec(memory_space=pltpu.SMEM), pl.BlockSpec(memory_space=pltpu.VMEM)
    step = 1.0 / math.sqrt(offsets.shape[0] * n_row * n_col)
    new_probe = pl.pallas_call(
        functools.partial(probe_kernel, step),
        out_shape=jax.ShapeDtypeStruct((1024, W), f32),
        in_specs=[smem] + [vmem] * 6,
        out_specs=vmem,
        compiler_params=pltpu.CompilerParams(vmem_limit_bytes=8 * 2**20),
        name="probe",
    )(place, probe_planes.reshape(1024, W), *quarters, rest)
    return new_object, new_probe.reshape(probe_planes.shape)


def solution(mesh):
    split = jax.sharding.Mesh(
        mesh.devices.reshape(mesh.shape["row"] // 2, 2, mesh.shape["col"] // 4, 4), ("y", "core", "x", "z")
    )
    rows, cols = ("y", "core"), ("x", "z")
    in_specs = (
        P(None, rows, cols),
        P(),
        P(rows + cols, None),
        P(rows + cols, None, None),
        P(rows, cols),
    )
    out_specs = (P(None, rows, cols), P())
    return jax.shard_map(shards, mesh=split, in_specs=in_specs, out_specs=out_specs, check_vma=False)
```

```python
import functools
import math

import ml_dtypes
import numpy as np
import jax
import jax.numpy as jnp
from jax import lax
from jax.experimental import pallas as pl
from jax.experimental.pallas import tpu as pltpu
from jax.sharding import PartitionSpec as P

f32, bf16 = jnp.float32, jnp.bfloat16
W = 256
H = 128
HC = 128
NB = 2
LAG = 0


def make_tables():
    b = np.arange(H)[:, None]
    q = np.arange(H)[None, :]
    right = []
    for p in (0, 1):
        ang = 2.0 * np.pi * (((2 * q + p) * b) % W) / W
        c, s = np.cos(ang) / 16.0, np.sin(ang) / 16.0
        right.append(np.block([[c, -s], [s, c]]))
    out = []
    for t in (right[0], right[1], right[0].T, right[1].T):
        hi = t.astype(np.float32).astype(ml_dtypes.bfloat16)
        lo = (t - hi.astype(np.float64)).astype(np.float32).astype(ml_dtypes.bfloat16)
        out.append(np.stack([hi, lo]))
    return np.stack(out)


def split(x):
    hi = x.astype(bf16)
    lo = (x - hi.astype(f32)).astype(bf16)
    return hi, lo


def rmul2(hi, lo, t):
    return jnp.dot(jnp.concatenate([hi, lo, hi], 1), jnp.concatenate([t[0], t[0], t[1]], 0), preferred_element_type=f32)


def rmul(x, t):
    hi, lo = split(x)
    return rmul2(hi, lo, t)


def lmul2(t, hi, lo):
    return jnp.dot(jnp.concatenate([t[0], t[0], t[1]], 1), jnp.concatenate([hi, lo, hi], 0), preferred_element_type=f32)


def cat1(a, b):
    return jnp.concatenate([a, b], 1)


def cat0(a, b):
    return jnp.concatenate([a, b], 0)


def main_kernel(offs, live, anchor, obj, right_top, right_bot, below, corner, probe, sq, tables,
                o_part, o_rtop, o_rbot, o_corner, o_below, o_mine, o_other,
                cov, acc, patch, pacc, prv, sqv, tb, gs, hs, ds, term, sems, sqsems):
    ins = [
        (obj, cov.at[:, 0:512, 0:512]),
        (right_top, cov.at[:, 0:256, 512:768]),
        (right_bot, cov.at[:, 256:512, 512:768]),
        (below, cov.at[:, 512:768, 0:512]),
        (corner, cov.at[:, 512:768, 512:768]),
        (probe, prv),
        (tables, tb),
    ]
    copies = [pltpu.make_async_copy(s, d, sems.at[i]) for i, (s, d) in enumerate(ins)]
    roots = lambda s: pltpu.make_async_copy(sq.at[s], sqv.at[s], sqsems.at[s])
    for c in copies:
        c.start()
    for s in range(8):
        roots(s).start()
    acc[...] = jnp.zeros_like(acc)
    pacc[...] = jnp.zeros_like(pacc)
    for c in copies:
        c.wait()
    lane = lax.broadcasted_iota(jnp.int32, (W, H), 1)
    sub9 = lax.broadcasted_iota(jnp.int32, (33, 8, H), 1)
    sub = lax.broadcasted_iota(jnp.int32, (32, 8, H), 1)

    def place_of(s):
        top = offs[s, 0] - anchor[0]
        left = offs[s, 1] - anchor[1]
        la = pl.multiple_of(lax.div(left, 128) * 128, 128)
        ta = pl.multiple_of(lax.div(top, 8) * 8, 8)
        return ta, lax.rem(top, 8), la, lax.rem(left, 128)

    def fetch(s, b):
        ta, rs, la, ls = place_of(s)
        back = lax.rem(128 - ls, 128)
        rback = lax.rem(8 - rs, 8)
        for c in range(2):
            t = []
            for k in range(3):
                v = cov[c, pl.ds(ta, W + 8), pl.ds(la + 128 * k, H)]
                v = pltpu.roll(pltpu.roll(v, back, 1).reshape(33, 8, H), rback, 1)
                t.append(jnp.where(sub < 8 - rs, v[:32], v[1:]).reshape(W, H))
            for k in range(2):
                patch[b, c, :, 128 * k:128 * k + 128] = jnp.where(lane < 128 - ls, t[k], t[k + 1])

    def deposit(s, b):
        ta, rs, la, ls = place_of(s)
        for c in range(2):
            r = [pltpu.roll(term[b, c, :, 128 * k:128 * k + 128], ls, 1) for k in range(2)]
            z = jnp.zeros_like(r[0])
            keep = lane >= ls
            parts = [jnp.where(keep, r[0], z), jnp.where(keep, r[1], r[0]), jnp.where(keep, z, r[1])]
            for k in range(3):
                v = pltpu.roll(parts[k].reshape(32, 8, H), rs, 1)
                z8 = jnp.zeros((1, 8, H), f32)
                v = jnp.where(sub9 >= rs, jnp.concatenate([v, z8], 0), jnp.concatenate([z8, v], 0))
                acc[c, pl.ds(ta, W + 8), pl.ds(la + 128 * k, H)] += v.reshape(W + 8, H)

    def units(s, b, used):
        for m in range(2):
            for j in range(0, H, HC):
                def waves(m=m, j=j):
                    at = [slice(j, j + HC), slice(H + j, H + j + HC)]
                    get = lambda ref, *i: cat0(ref[(*i, at[0])], ref[(*i, at[1])])
                    pr, pi = get(prv, 0, m), get(prv, 1, m)
                    xr, xi = get(patch, b, 0), get(patch, b, 1)
                    wr = pr * xr - pi * xi
                    wi = pr * xi + pi * xr
                    e = cat1(wr[:, :H] + wr[:, H:], wi[:, :H] + wi[:, H:])
                    o = cat1(wr[:, :H] - wr[:, H:], wi[:, :H] - wi[:, H:])
                    return rmul(e, tb[0]), rmul(o, tb[1])

                def rows(ys, m=m, j=j):
                    for p in range(2):
                        lanes = slice(H * p, H * p + H)
                        y = ys[p]
                        for q in range(2):
                            f = y[:HC] + y[HC:] if q == 0 else y[:HC] - y[HC:]
                            hi, lo = split(f)
                            for part in range(2):
                                r = H * part + j
                                gs[b, m, q, r:r + HC, lanes] = hi[:, H * part:H * part + H]
                                gs[b, m, q, W + r:W + r + HC, lanes] = lo[:, H * part:H * part + H]

                yield waves, rows
        for q in range(2):
            for j in range(0, H, HC):
                def fars(q=q, j=j):
                    t = tb[2 + q]
                    return [lmul2(t, gs[b, m, q, :W], gs[b, m, q, W:]) for m in range(2)]

                def factors(fars, q=q, j=j):
                    mod = sum(a[:HC] * a[:HC] + a[HC:] * a[HC:] for a in fars)
                    root = sqv[s, H * q + j:H * q + j + HC, :]
                    fac = used - (used * root) * lax.rsqrt(jnp.maximum(mod, 0.1))
                    for m in range(2):
                        for part in range(2):
                            hi, lo = split(fars[m][HC * part:HC * part + HC] * fac)
                            r = H * part + j
                            hs[b, m, q, r:r + HC] = hi
                            hs[b, m, q, W + r:W + r + HC] = lo

                yield fars, factors
        for m in range(2):
            for j in range(0, H, HC):
                def backs(m=m, j=j):
                    out = []
                    for q in range(2):
                        t = tb[q]
                        out.append(lmul2(t, hs[b, m, q, :W], hs[b, m, q, W:]))
                    return out

                def columns(v, m=m, j=j):
                    for top in range(2):
                        x = v[0] + v[1] if top == 0 else v[0] - v[1]
                        for p in range(2):
                            hi, lo = split(cat1(x[:HC, H * p:H * p + H], x[HC:, H * p:H * p + H]))
                            r = H * top + j
                            ds[b, m, p, r:r + HC, :W] = hi
                            ds[b, m, p, r:r + HC, W:] = lo

                yield backs, columns
        for m in range(2):
            for j in (0, H):
                at = slice(j, j + H)

                def last(m=m, at=at):
                    return [rmul2(ds[b, m, p, at, :W], ds[b, m, p, at, W:], tb[2 + p]) for p in range(2)]

                def terms(d, m=m, at=at):
                    for h in range(2):
                        x = d[0] + d[1] if h == 0 else d[0] - d[1]
                        br, bi = x[:, :H], x[:, H:]
                        lanes = slice(H * h, H * h + H)
                        pr, pi = prv[0, m, at, lanes], prv[1, m, at, lanes]
                        xr, xi = patch[b, 0, at, lanes], patch[b, 1, at, lanes]
                        tr, ti = pr * br + pi * bi, pr * bi - pi * br
                        if m == 0:
                            term[b, 0, at, lanes], term[b, 1, at, lanes] = tr, ti
                        else:
                            term[b, 0, at, lanes] += tr
                            term[b, 1, at, lanes] += ti
                        pacc[0, m, at, lanes] += xr * br + xi * bi
                        pacc[1, m, at, lanes] += xr * bi - xi * br

                yield last, terms

    def pair(i, carry):
        slots = [i * NB + b for b in range(NB)]
        used = [jnp.where(s < live[0], 1.0, 0.0) for s in slots]
        for b in range(NB):
            roots(slots[b]).wait()
            fetch(slots[b], b)
        streams = [list(units(slots[b], b, used[b])) for b in range(NB)]
        todo = []
        for group in zip(*streams):
            for product, then in group:
                todo.append((then, product()))
                if len(todo) > LAG:
                    then, value = todo.pop(0)
                    then(value)
        for then, value in todo:
            then(value)
        for b in range(NB):
            deposit(slots[b], b)
        return carry

    pairs = lax.div(live[0] + NB - 1, NB)
    lax.fori_loop(0, pairs, pair, 0)

    def skip(s, carry):
        roots(s).wait()
        return carry

    lax.fori_loop(pairs * NB, 8, skip, 0)
    outs = [
        (acc.at[:, 512:768, 512:768], o_corner),
        (acc.at[:, 256:512, 512:768], o_rbot),
        (acc.at[:, 0:256, 512:768], o_rtop),
        (acc.at[:, 512:768, 0:512], o_below),
        (prv.at[1], o_other),
        (prv.at[0], o_mine),
        (cov.at[0, 0:512, 0:512], o_part.at[0]),
        (cov.at[1, 0:512, 0:512], o_part.at[1]),
    ]
    copies = [pltpu.make_async_copy(s, d, sems.at[i]) for i, (s, d) in enumerate(outs)]
    for c in copies[:4]:
        c.start()
    for kc, kx in np.ndindex(2, 4):
        c, x = lax.rem(anchor[2] + kc, 2), lax.rem(anchor[3] + kx, 4)
        at = pl.multiple_of(lax.rem(x, 2) * H, H)
        prv[kc, kx // 2, kx % 2 * H:kx % 2 * H + H, :] = pacc[c, lax.div(x, 2), pl.ds(at, H), :]
    for c in copies[4:6]:
        c.start()
    for c in range(2):
        cov[c, 0:512, 0:512] = cov[c, 0:512, 0:512] - 0.5 * acc[c, 0:512, 0:512]
        copies[6 + c].start()
    for c in copies:
        c.wait()


def main_call(offs, live, anchor, obj, right_top, right_bot, below, corner, probe, sq):
    any_ = pl.BlockSpec(memory_space=pl.ANY)
    smem = pl.BlockSpec(memory_space=pltpu.SMEM)
    S = lambda *s: jax.ShapeDtypeStruct(s, f32)
    return pl.pallas_call(
        main_kernel,
        out_shape=(S(2, 512, 512), S(2, 256, 256), S(2, 256, 256), S(2, 256, 256), S(2, 256, 512), S(2, 256, 256), S(2, 256, 256)),
        in_specs=[smem] * 3 + [any_] * 8,
        out_specs=[any_] * 7,
        scratch_shapes=[
            pltpu.VMEM((2, 768, 768), f32),
            pltpu.VMEM((2, 768, 768), f32),
            pltpu.VMEM((NB, 2, W, W), f32),
            pltpu.VMEM((2, 2, W, W), f32),
            pltpu.VMEM((2, 2, W, W), f32),
            pltpu.VMEM((8, W, W), f32),
            pltpu.VMEM((4, 2, W, W), bf16),
            pltpu.VMEM((NB, 2, 2, 2 * W, W), bf16),
            pltpu.VMEM((NB, 2, 2, 2 * W, W), bf16),
            pltpu.VMEM((NB, 2, 2, W, 2 * W), bf16),
            pltpu.VMEM((NB, 2, W, W), f32),
            pltpu.SemaphoreType.DMA((9,)),
            pltpu.SemaphoreType.DMA((8,)),
        ],
        compiler_params=pltpu.CompilerParams(vmem_limit_bytes=62 * 2**20),
        name="slots",
    )(offs, live, anchor, obj, right_top, right_bot, below, corner, probe, sq, jnp.asarray(make_tables()))


def prep_kernel(counts, pm, pmt, out):
    i = counts[0].astype(f32).astype(bf16)
    a = jnp.dot(pm[...], i, preferred_element_type=f32).astype(bf16)
    out[0] = jnp.sqrt(jnp.dot(a, pmt[...], preferred_element_type=f32))


def prep_call(counts):
    order = np.concatenate([np.arange(0, W, 2), np.arange(1, W, 2)])
    pm = np.zeros((W, W), np.float32)
    pm[np.arange(W), order] = 1.0
    full = pl.BlockSpec((W, W), lambda s: (0, 0))
    blk = pl.BlockSpec((1, W, W), lambda s: (s, 0, 0))
    return pl.pallas_call(
        prep_kernel,
        grid=(8,),
        out_shape=jax.ShapeDtypeStruct((8, W, W), f32),
        in_specs=[blk, full, full],
        out_specs=blk,
        name="roots",
    )(counts, jnp.asarray(pm.astype(ml_dtypes.bfloat16)), jnp.asarray(pm.T.astype(ml_dtypes.bfloat16)))


def moved(value, axes, pairs):
    return lax.ppermute(value, axes, pairs)


def finish_kernel(part, above, top, bot, out):
    h = pl.program_id(1)

    @pl.when(h == 0)
    def _():
        out[0] = part[0] - 0.5 * above[0]
        out[0, :, :W] -= 0.5 * top[0]

    @pl.when(h == 1)
    def _():
        out[0, :, W:] = part[0, :, W:]
        out[0, :, :W] = part[0, :, :W] - 0.5 * bot[0]


def finish_call(part, above, top, bot):
    wide = pl.BlockSpec((1, W, 512), lambda c, h: (c, h, 0))
    return pl.pallas_call(
        finish_kernel,
        grid=(2, 2),
        out_shape=jax.ShapeDtypeStruct((2, 512, 512), f32),
        in_specs=[
            wide,
            pl.BlockSpec((1, W, 512), lambda c, h: (c, 0, 0)),
            pl.BlockSpec((1, W, W), lambda c, h: (c, 0, 0)),
            pl.BlockSpec((1, W, W), lambda c, h: (c, 0, 0)),
        ],
        out_specs=wide,
        compiler_params=pltpu.CompilerParams(vmem_limit_bytes=8 * 2**20),
        name="finish",
    )(part, above, top, bot)


def swap_cores(value):
    return lax.ppermute(value, "core", [(0, 1), (1, 0)])


def sum_along(pieces, axis):
    got = [lax.ppermute(pieces[k], axis, [(i, (i + k) % 4) for i in range(4)]) for k in (2, 1, 3)]
    return pieces[0] + got[0] + got[1] + got[2]


def spread_along(value, axis):
    return [value] + [lax.ppermute(value, axis, [(i, (i + k) % 4) for i in range(4)]) for k in (1, 2, 3)]


def sum_everywhere(value, axis):
    got = [lax.ppermute(value, axis, [(i, (i + k) % 4) for i in range(4)]) for k in (2, 1, 3)]
    return (value + got[0]) + (got[1] + got[2])


def probe_kernel(step, place, probe, x0, x1, x2, x3, rest, out):
    for kc, kx in np.ndindex(2, 4):
        row = lax.rem(place[2] + kc, 2) * 512 + lax.rem(place[3] - kx + 4, 4) * H
        at = pl.multiple_of(row, H)
        total = (x0, x1, x2, x3)[kx][...] if kc == 0 else rest[kx]
        out[pl.ds(at, H), :] = probe[pl.ds(at, H), :] - step * total


def shards(object_planes, probe_planes, offsets, photon_counts, live_counts):
    n_row = lax.axis_size("y") * lax.axis_size("core")
    n_col = lax.axis_size("x") * lax.axis_size("z")
    rows, cols = ("y", "core"), ("x", "z")
    up = [(i, i - 1) for i in range(1, n_row)]
    down = [(i - 1, i) for i in range(1, n_row)]
    to_left = [(i, i - 1) for i in range(1, n_col)]
    to_right = [(i - 1, i) for i in range(1, n_col)]

    right_top = lax.ppermute(object_planes[:, :W, :W], cols, to_left)
    below = lax.ppermute(object_planes[:, :W, :], rows, up)
    right_bot = lax.ppermute(object_planes[:, W:, :W], cols, to_left)
    roots = prep_call(photon_counts)
    right_top, roots = lax.optimization_barrier((right_top, roots))
    corner = lax.ppermute(right_top, rows, up)
    place = jnp.stack(
        [lax.axis_index(rows) * 512, lax.axis_index(cols) * 512] + [lax.axis_index(a) for a in ("core", "x")]
    ).astype(jnp.int32)
    part, g_top, g_bot, g_corner, g_below, mine, other = main_call(
        offsets, live_counts.reshape(1), place, object_planes, right_top, right_bot, below, corner, probe_planes, roots
    )
    corner_in = lax.ppermute(g_corner, rows, down)
    bot_in = lax.ppermute(g_bot, cols, to_right)
    above_in = lax.ppermute(g_below, rows, down)
    half = (mine + swap_cores(other)).reshape(4, H, W)
    top_in = lax.ppermute(g_top + corner_in, cols, to_right)
    piece = sum_along(half, "x")
    piece, bot_in = lax.optimization_barrier((piece, bot_in))
    piece = sum_everywhere(piece, "y")
    piece, top_in = lax.optimization_barrier((piece, top_in))
    piece = sum_everywhere(piece, "z")
    new_object = finish_call(part, above_in, top_in, bot_in)
    quarters = spread_along(piece, "x")
    rest = swap_cores(jnp.stack(quarters))
    smem, vmem = pl.BlockSpec(memory_space=pltpu.SMEM), pl.BlockSpec(memory_space=pltpu.VMEM)
    step = 1.0 / math.sqrt(offsets.shape[0] * n_row * n_col)
    new_probe = pl.pallas_call(
        functools.partial(probe_kernel, step),
        out_shape=jax.ShapeDtypeStruct((1024, W), f32),
        in_specs=[smem] + [vmem] * 6,
        out_specs=vmem,
        compiler_params=pltpu.CompilerParams(vmem_limit_bytes=8 * 2**20),
        name="probe",
    )(place, probe_planes.reshape(1024, W), *quarters, rest)
    return new_object, new_probe.reshape(probe_planes.shape)


def solution(mesh):
    split = jax.sharding.Mesh(
        mesh.devices.reshape(mesh.shape["row"] // 2, 2, mesh.shape["col"] // 4, 4), ("y", "core", "x", "z")
    )
    rows, cols = ("y", "core"), ("x", "z")
    in_specs = (
        P(None, rows, cols),
        P(),
        P(rows + cols, None),
        P(rows + cols, None, None),
        P(rows, cols),
    )
    out_specs = (P(None, rows, cols), P())
    return jax.shard_map(shards, mesh=split, in_specs=in_specs, out_specs=out_specs, check_vma=False)
```

```python
import functools
import math

import ml_dtypes
import numpy as np
import jax
import jax.numpy as jnp
from jax import lax
from jax.experimental import pallas as pl
from jax.experimental.pallas import tpu as pltpu
from jax.sharding import PartitionSpec as P

f32, bf16 = jnp.float32, jnp.bfloat16
W = 256
H = 128
HC = 128
NB = 2
LAG = 0


def make_tables():
    b = np.arange(H)[:, None]
    q = np.arange(H)[None, :]
    right = []
    for p in (0, 1):
        ang = 2.0 * np.pi * (((2 * q + p) * b) % W) / W
        c, s = np.cos(ang) / 16.0, np.sin(ang) / 16.0
        right.append(np.block([[c, -s], [s, c]]))
    out = []
    for t in (right[0], right[1], right[0].T, right[1].T):
        hi = t.astype(np.float32).astype(ml_dtypes.bfloat16)
        lo = (t - hi.astype(np.float64)).astype(np.float32).astype(ml_dtypes.bfloat16)
        out.append(np.stack([hi, lo]))
    return np.stack(out)


def split(x):
    hi = x.astype(bf16)
    lo = (x - hi.astype(f32)).astype(bf16)
    return hi, lo


def rmul2(hi, lo, t):
    return jnp.dot(jnp.concatenate([hi, lo, hi], 1), jnp.concatenate([t[0], t[0], t[1]], 0), preferred_element_type=f32)


def rmul(x, t):
    hi, lo = split(x)
    return rmul2(hi, lo, t)


def lmul2(t, hi, lo):
    return jnp.dot(jnp.concatenate([t[0], t[0], t[1]], 1), jnp.concatenate([hi, lo, hi], 0), preferred_element_type=f32)


def cat1(a, b):
    return jnp.concatenate([a, b], 1)


def cat0(a, b):
    return jnp.concatenate([a, b], 0)


def main_kernel(offs, live, anchor, obj, right_top, right_bot, below, corner, probe, sq, tables,
                o_part, o_rtop, o_rbot, o_corner, o_below, o_mine, o_other,
                cov, acc, patch, pacc, prv, sqv, tb, gs, hs, ds, term, sems, sqsems):
    ins = [
        (obj, cov.at[:, 0:512, 0:512]),
        (right_top, cov.at[:, 0:256, 512:768]),
        (right_bot, cov.at[:, 256:512, 512:768]),
        (below, cov.at[:, 512:768, 0:512]),
        (corner, cov.at[:, 512:768, 512:768]),
        (probe, prv),
        (tables, tb),
    ]
    copies = [pltpu.make_async_copy(s, d, sems.at[i]) for i, (s, d) in enumerate(ins)]
    roots = lambda s: pltpu.make_async_copy(sq.at[s], sqv.at[s], sqsems.at[s])
    for c in copies:
        c.start()
    for s in range(8):
        roots(s).start()
    acc[...] = jnp.zeros_like(acc)
    pacc[...] = jnp.zeros_like(pacc)
    for c in copies:
        c.wait()
    lane = lax.broadcasted_iota(jnp.int32, (W, H), 1)
    sub9 = lax.broadcasted_iota(jnp.int32, (33, 8, H), 1)
    sub = lax.broadcasted_iota(jnp.int32, (32, 8, H), 1)

    def place_of(s):
        top = offs[s, 0] - anchor[0]
        left = offs[s, 1] - anchor[1]
        la = pl.multiple_of(lax.div(left, 128) * 128, 128)
        ta = pl.multiple_of(lax.div(top, 8) * 8, 8)
        return ta, lax.rem(top, 8), la, lax.rem(left, 128)

    def fetch(s, b):
        ta, rs, la, ls = place_of(s)
        back = lax.rem(128 - ls, 128)
        rback = lax.rem(8 - rs, 8)
        for c in range(2):
            t = []
            for k in range(3):
                v = cov[c, pl.ds(ta, W + 8), pl.ds(la + 128 * k, H)]
                v = pltpu.roll(pltpu.roll(v, back, 1).reshape(33, 8, H), rback, 1)
                t.append(jnp.where(sub < 8 - rs, v[:32], v[1:]).reshape(W, H))
            for k in range(2):
                patch[b, c, :, 128 * k:128 * k + 128] = jnp.where(lane < 128 - ls, t[k], t[k + 1])

    def deposit(s, b):
        ta, rs, la, ls = place_of(s)
        for c in range(2):
            r = [pltpu.roll(term[b, c, :, 128 * k:128 * k + 128], ls, 1) for k in range(2)]
            z = jnp.zeros_like(r[0])
            keep = lane >= ls
            parts = [jnp.where(keep, r[0], z), jnp.where(keep, r[1], r[0]), jnp.where(keep, z, r[1])]
            for k in range(3):
                v = pltpu.roll(parts[k].reshape(32, 8, H), rs, 1)
                z8 = jnp.zeros((1, 8, H), f32)
                v = jnp.where(sub9 >= rs, jnp.concatenate([v, z8], 0), jnp.concatenate([z8, v], 0))
                acc[c, pl.ds(ta, W + 8), pl.ds(la + 128 * k, H)] += v.reshape(W + 8, H)

    def units(s, b, used):
        for m in range(2):
            for j in range(0, H, HC):
                def waves(m=m, j=j):
                    at = [slice(j, j + HC), slice(H + j, H + j + HC)]
                    get = lambda ref, *i: cat0(ref[(*i, at[0])], ref[(*i, at[1])])
                    pr, pi = get(prv, 0, m), get(prv, 1, m)
                    xr, xi = get(patch, b, 0), get(patch, b, 1)
                    wr = pr * xr - pi * xi
                    wi = pr * xi + pi * xr
                    e = cat1(wr[:, :H] + wr[:, H:], wi[:, :H] + wi[:, H:])
                    o = cat1(wr[:, :H] - wr[:, H:], wi[:, :H] - wi[:, H:])
                    return rmul(e, tb[0]), rmul(o, tb[1])

                def rows(ys, m=m, j=j):
                    for p in range(2):
                        lanes = slice(H * p, H * p + H)
                        y = ys[p]
                        for q in range(2):
                            f = y[:HC] + y[HC:] if q == 0 else y[:HC] - y[HC:]
                            hi, lo = split(f)
                            for part in range(2):
                                r = H * part + j
                                gs[b, m, q, r:r + HC, lanes] = hi[:, H * part:H * part + H]
                                gs[b, m, q, W + r:W + r + HC, lanes] = lo[:, H * part:H * part + H]

                yield waves, rows
        for q in range(2):
            for j in range(0, H, HC):
                def fars(q=q, j=j):
                    t = tb[2 + q]
                    return [lmul2(t, gs[b, m, q, :W], gs[b, m, q, W:]) for m in range(2)]

                def factors(fars, q=q, j=j):
                    mod = sum(a[:HC] * a[:HC] + a[HC:] * a[HC:] for a in fars)
                    root = sqv[s, H * q + j:H * q + j + HC, :]
                    fac = used - (used * root) * lax.rsqrt(jnp.maximum(mod, 0.1))
                    for m in range(2):
                        for part in range(2):
                            hi, lo = split(fars[m][HC * part:HC * part + HC] * fac)
                            r = H * part + j
                            hs[b, m, q, r:r + HC] = hi
                            hs[b, m, q, W + r:W + r + HC] = lo

                yield fars, factors
        for m in range(2):
            for j in range(0, H, HC):
                def backs(m=m, j=j):
                    out = []
                    for q in range(2):
                        t = tb[q]
                        out.append(lmul2(t, hs[b, m, q, :W], hs[b, m, q, W:]))
                    return out

                def columns(v, m=m, j=j):
                    for top in range(2):
                        x = v[0] + v[1] if top == 0 else v[0] - v[1]
                        for p in range(2):
                            hi, lo = split(cat1(x[:HC, H * p:H * p + H], x[HC:, H * p:H * p + H]))
                            r = H * top + j
                            ds[b, m, p, r:r + HC, :W] = hi
                            ds[b, m, p, r:r + HC, W:] = lo

                yield backs, columns
        for m in range(2):
            for j in (0, H):
                at = slice(j, j + H)

                def last(m=m, at=at):
                    return [rmul2(ds[b, m, p, at, :W], ds[b, m, p, at, W:], tb[2 + p]) for p in range(2)]

                def terms(d, m=m, at=at):
                    for h in range(2):
                        x = d[0] + d[1] if h == 0 else d[0] - d[1]
                        br, bi = x[:, :H], x[:, H:]
                        lanes = slice(H * h, H * h + H)
                        pr, pi = prv[0, m, at, lanes], prv[1, m, at, lanes]
                        xr, xi = patch[b, 0, at, lanes], patch[b, 1, at, lanes]
                        tr, ti = pr * br + pi * bi, pr * bi - pi * br
                        if m == 0:
                            term[b, 0, at, lanes], term[b, 1, at, lanes] = tr, ti
                        else:
                            term[b, 0, at, lanes] += tr
                            term[b, 1, at, lanes] += ti
                        pacc[0, m, at, lanes] += xr * br + xi * bi
                        pacc[1, m, at, lanes] += xr * bi - xi * br

                yield last, terms

    def pair(i, carry):
        slots = [i * NB + b for b in range(NB)]
        used = [jnp.where(s < live[0], 1.0, 0.0) for s in slots]
        for b in range(NB):
            roots(slots[b]).wait()
            fetch(slots[b], b)
        streams = [list(units(slots[b], b, used[b])) for b in range(NB)]
        todo = []
        for group in zip(*streams):
            for product, then in group:
                todo.append((then, product()))
                if len(todo) > LAG:
                    then, value = todo.pop(0)
                    then(value)
        for then, value in todo:
            then(value)
        for b in range(NB):
            deposit(slots[b], b)
        return carry

    pairs = lax.div(live[0] + NB - 1, NB)
    lax.fori_loop(0, pairs, pair, 0)

    def skip(s, carry):
        roots(s).wait()
        return carry

    lax.fori_loop(pairs * NB, 8, skip, 0)
    outs = [
        (acc.at[:, 512:768, 512:768], o_corner),
        (acc.at[:, 256:512, 512:768], o_rbot),
        (acc.at[:, 0:256, 512:768], o_rtop),
        (acc.at[:, 512:768, 0:512], o_below),
        (prv.at[1], o_other),
        (prv.at[0], o_mine),
        (cov.at[0, 0:512, 0:512], o_part.at[0]),
        (cov.at[1, 0:512, 0:512], o_part.at[1]),
    ]
    copies = [pltpu.make_async_copy(s, d, sems.at[i]) for i, (s, d) in enumerate(outs)]
    for c in copies[:4]:
        c.start()
    for kc in range(2):
        prv[kc] = pacc[lax.rem(anchor[2] + kc, 2)]
    for c in copies[4:6]:
        c.start()
    for c in range(2):
        cov[c, 0:512, 0:512] = cov[c, 0:512, 0:512] - 0.5 * acc[c, 0:512, 0:512]
        copies[6 + c].start()
    for c in copies:
        c.wait()


def main_call(offs, live, anchor, obj, right_top, right_bot, below, corner, probe, sq):
    any_ = pl.BlockSpec(memory_space=pl.ANY)
    smem = pl.BlockSpec(memory_space=pltpu.SMEM)
    S = lambda *s: jax.ShapeDtypeStruct(s, f32)
    return pl.pallas_call(
        main_kernel,
        out_shape=(S(2, 512, 512), S(2, 256, 256), S(2, 256, 256), S(2, 256, 256), S(2, 256, 512), S(2, 256, 256), S(2, 256, 256)),
        in_specs=[smem] * 3 + [any_] * 8,
        out_specs=[any_] * 7,
        scratch_shapes=[
            pltpu.VMEM((2, 768, 768), f32),
            pltpu.VMEM((2, 768, 768), f32),
            pltpu.VMEM((NB, 2, W, W), f32),
            pltpu.VMEM((2, 2, W, W), f32),
            pltpu.VMEM((2, 2, W, W), f32),
            pltpu.VMEM((8, W, W), f32),
            pltpu.VMEM((4, 2, W, W), bf16),
            pltpu.VMEM((NB, 2, 2, 2 * W, W), bf16),
            pltpu.VMEM((NB, 2, 2, 2 * W, W), bf16),
            pltpu.VMEM((NB, 2, 2, W, 2 * W), bf16),
            pltpu.VMEM((NB, 2, W, W), f32),
            pltpu.SemaphoreType.DMA((9,)),
            pltpu.SemaphoreType.DMA((8,)),
        ],
        compiler_params=pltpu.CompilerParams(vmem_limit_bytes=62 * 2**20),
        name="slots",
    )(offs, live, anchor, obj, right_top, right_bot, below, corner, probe, sq, jnp.asarray(make_tables()))


def prep_kernel(counts, pm, pmt, out):
    i = counts[0].astype(f32).astype(bf16)
    a = jnp.dot(pm[...], i, preferred_element_type=f32).astype(bf16)
    out[0] = jnp.sqrt(jnp.dot(a, pmt[...], preferred_element_type=f32))


def prep_call(counts):
    order = np.concatenate([np.arange(0, W, 2), np.arange(1, W, 2)])
    pm = np.zeros((W, W), np.float32)
    pm[np.arange(W), order] = 1.0
    full = pl.BlockSpec((W, W), lambda s: (0, 0))
    blk = pl.BlockSpec((1, W, W), lambda s: (s, 0, 0))
    return pl.pallas_call(
        prep_kernel,
        grid=(8,),
        out_shape=jax.ShapeDtypeStruct((8, W, W), f32),
        in_specs=[blk, full, full],
        out_specs=blk,
        name="roots",
    )(counts, jnp.asarray(pm.astype(ml_dtypes.bfloat16)), jnp.asarray(pm.T.astype(ml_dtypes.bfloat16)))


def moved(value, axes, pairs):
    return lax.ppermute(value, axes, pairs)


def finish_kernel(part, above, top, bot, out):
    h = pl.program_id(1)

    @pl.when(h == 0)
    def _():
        out[0] = part[0] - 0.5 * above[0]
        out[0, :, :W] -= 0.5 * top[0]

    @pl.when(h == 1)
    def _():
        out[0, :, W:] = part[0, :, W:]
        out[0, :, :W] = part[0, :, :W] - 0.5 * bot[0]


def finish_call(part, above, top, bot):
    wide = pl.BlockSpec((1, W, 512), lambda c, h: (c, h, 0))
    return pl.pallas_call(
        finish_kernel,
        grid=(2, 2),
        out_shape=jax.ShapeDtypeStruct((2, 512, 512), f32),
        in_specs=[
            wide,
            pl.BlockSpec((1, W, 512), lambda c, h: (c, 0, 0)),
            pl.BlockSpec((1, W, W), lambda c, h: (c, 0, 0)),
            pl.BlockSpec((1, W, W), lambda c, h: (c, 0, 0)),
        ],
        out_specs=wide,
        compiler_params=pltpu.CompilerParams(vmem_limit_bytes=8 * 2**20),
        name="finish",
    )(part, above, top, bot)


def swap_cores(value):
    return lax.ppermute(value, "core", [(0, 1), (1, 0)])


def sum_everywhere(value, axis):
    got = [lax.ppermute(value, axis, [(i, (i + k) % 4) for i in range(4)]) for k in (2, 1, 3)]
    return (value + got[0]) + (got[1] + got[2])


def probe_kernel(step, place, probe, mine, rest, out):
    for kc in range(2):
        at = pl.multiple_of(lax.rem(place[2] + kc, 2) * 512, 512)
        out[pl.ds(at, 512), :] = probe[pl.ds(at, 512), :] - step * (mine, rest)[kc][...]


def shards(object_planes, probe_planes, offsets, photon_counts, live_counts):
    n_row = lax.axis_size("y") * lax.axis_size("core")
    n_col = lax.axis_size("x") * lax.axis_size("z")
    rows, cols = ("y", "core"), ("x", "z")
    up = [(i, i - 1) for i in range(1, n_row)]
    down = [(i - 1, i) for i in range(1, n_row)]
    to_left = [(i, i - 1) for i in range(1, n_col)]
    to_right = [(i - 1, i) for i in range(1, n_col)]

    right_top = lax.ppermute(object_planes[:, :W, :W], cols, to_left)
    below = lax.ppermute(object_planes[:, :W, :], rows, up)
    right_bot = lax.ppermute(object_planes[:, W:, :W], cols, to_left)
    roots = prep_call(photon_counts)
    right_top, roots = lax.optimization_barrier((right_top, roots))
    corner = lax.ppermute(right_top, rows, up)
    place = jnp.stack(
        [lax.axis_index(rows) * 512, lax.axis_index(cols) * 512] + [lax.axis_index(a) for a in ("core",)]
    ).astype(jnp.int32)
    part, g_top, g_bot, g_corner, g_below, mine, other = main_call(
        offsets, live_counts.reshape(1), place, object_planes, right_top, right_bot, below, corner, probe_planes, roots
    )
    corner_in = lax.ppermute(g_corner, rows, down)
    bot_in = lax.ppermute(g_bot, cols, to_right)
    above_in = lax.ppermute(g_below, rows, down)
    half = (mine + swap_cores(other)).reshape(16, 32, W)
    top_in = lax.ppermute(g_top + corner_in, cols, to_right)
    plane = ("y", "x")
    piece = lax.all_to_all(half, plane, 0, 0).sum(0)
    piece, bot_in = lax.optimization_barrier((piece, bot_in))
    piece = sum_everywhere(piece, "z")
    piece, top_in, above_in = lax.optimization_barrier((piece, top_in, above_in))
    new_object = finish_call(part, above_in, top_in, bot_in)
    half = lax.all_to_all(jnp.broadcast_to(piece[None], half.shape), plane, 0, 0).reshape(512, W)
    rest = swap_cores(half)
    smem, vmem = pl.BlockSpec(memory_space=pltpu.SMEM), pl.BlockSpec(memory_space=pltpu.VMEM)
    step = 1.0 / math.sqrt(offsets.shape[0] * n_row * n_col)
    new_probe = pl.pallas_call(
        functools.partial(probe_kernel, step),
        out_shape=jax.ShapeDtypeStruct((1024, W), f32),
        in_specs=[smem] + [vmem] * 3,
        out_specs=vmem,
        compiler_params=pltpu.CompilerParams(vmem_limit_bytes=8 * 2**20),
        name="probe",
    )(place, probe_planes.reshape(1024, W), half, rest)
    return new_object, new_probe.reshape(probe_planes.shape)


def solution(mesh):
    split = jax.sharding.Mesh(
        mesh.devices.reshape(mesh.shape["row"] // 2, 2, mesh.shape["col"] // 4, 4), ("y", "core", "x", "z")
    )
    rows, cols = ("y", "core"), ("x", "z")
    in_specs = (
        P(None, rows, cols),
        P(),
        P(rows + cols, None),
        P(rows + cols, None, None),
        P(rows, cols),
    )
    out_specs = (P(None, rows, cols), P())
    return jax.shard_map(shards, mesh=split, in_specs=in_specs, out_specs=out_specs, check_vma=False)
```

```python
import functools
import math

import ml_dtypes
import numpy as np
import jax
import jax.numpy as jnp
from jax import lax
from jax.experimental import pallas as pl
from jax.experimental.pallas import tpu as pltpu
from jax.sharding import PartitionSpec as P

f32, bf16 = jnp.float32, jnp.bfloat16
W = 256
H = 128
HC = 128
NB = 2
LAG = 0


def make_tables():
    b = np.arange(H)[:, None]
    q = np.arange(H)[None, :]
    right = []
    for p in (0, 1):
        ang = 2.0 * np.pi * (((2 * q + p) * b) % W) / W
        c, s = np.cos(ang) / 16.0, np.sin(ang) / 16.0
        right.append(np.block([[c, -s], [s, c]]))
    out = []
    for t in (right[0], right[1], right[0].T, right[1].T):
        hi = t.astype(np.float32).astype(ml_dtypes.bfloat16)
        lo = (t - hi.astype(np.float64)).astype(np.float32).astype(ml_dtypes.bfloat16)
        out.append(np.stack([hi, lo]))
    return np.stack(out)


def split(x):
    hi = x.astype(bf16)
    lo = (x - hi.astype(f32)).astype(bf16)
    return hi, lo


def rmul2(hi, lo, t):
    return jnp.dot(jnp.concatenate([hi, lo, hi], 1), jnp.concatenate([t[0], t[0], t[1]], 0), preferred_element_type=f32)


def rmul(x, t):
    hi, lo = split(x)
    return rmul2(hi, lo, t)


def lmul2(t, hi, lo):
    return jnp.dot(jnp.concatenate([t[0], t[0], t[1]], 1), jnp.concatenate([hi, lo, hi], 0), preferred_element_type=f32)


def cat1(a, b):
    return jnp.concatenate([a, b], 1)


def cat0(a, b):
    return jnp.concatenate([a, b], 0)


def main_kernel(offs, live, anchor, obj, right_top, right_bot, below, corner, probe, sq, tables,
                o_part, o_rtop, o_rbot, o_below, o_mine, o_other,
                cov, acc, patch, pacc, prv, sqv, tb, gs, hs, ds, term, sems, sqsems):
    ins = [
        (obj, cov.at[:, 0:512, 0:512]),
        (right_top, cov.at[:, 0:256, 512:768]),
        (right_bot, cov.at[:, 256:512, 512:768]),
        (below, cov.at[:, 512:768, 0:512]),
        (corner, cov.at[:, 512:768, 512:768]),
        (probe, prv),
        (tables, tb),
    ]
    copies = [pltpu.make_async_copy(s, d, sems.at[i]) for i, (s, d) in enumerate(ins)]
    roots = lambda s: pltpu.make_async_copy(sq.at[s], sqv.at[s], sqsems.at[s])
    for c in copies:
        c.start()
    for s in range(8):
        roots(s).start()
    acc[...] = jnp.zeros_like(acc)
    pacc[...] = jnp.zeros_like(pacc)
    for c in copies:
        c.wait()
    lane = lax.broadcasted_iota(jnp.int32, (W, H), 1)
    sub9 = lax.broadcasted_iota(jnp.int32, (33, 8, H), 1)
    sub = lax.broadcasted_iota(jnp.int32, (32, 8, H), 1)

    def place_of(s):
        top = offs[s, 0] - anchor[0]
        left = offs[s, 1] - anchor[1]
        la = pl.multiple_of(lax.div(left, 128) * 128, 128)
        ta = pl.multiple_of(lax.div(top, 8) * 8, 8)
        return ta, lax.rem(top, 8), la, lax.rem(left, 128)

    def fetch(s, b):
        ta, rs, la, ls = place_of(s)
        back = lax.rem(128 - ls, 128)
        rback = lax.rem(8 - rs, 8)
        for c in range(2):
            t = []
            for k in range(3):
                v = cov[c, pl.ds(ta, W + 8), pl.ds(la + 128 * k, H)]
                v = pltpu.roll(pltpu.roll(v, back, 1).reshape(33, 8, H), rback, 1)
                t.append(jnp.where(sub < 8 - rs, v[:32], v[1:]).reshape(W, H))
            for k in range(2):
                patch[b, c, :, 128 * k:128 * k + 128] = jnp.where(lane < 128 - ls, t[k], t[k + 1])

    def deposit(s, b):
        ta, rs, la, ls = place_of(s)
        for c in range(2):
            r = [pltpu.roll(term[b, c, :, 128 * k:128 * k + 128], ls, 1) for k in range(2)]
            z = jnp.zeros_like(r[0])
            keep = lane >= ls
            parts = [jnp.where(keep, r[0], z), jnp.where(keep, r[1], r[0]), jnp.where(keep, z, r[1])]
            for k in range(3):
                v = pltpu.roll(parts[k].reshape(32, 8, H), rs, 1)
                z8 = jnp.zeros((1, 8, H), f32)
                v = jnp.where(sub9 >= rs, jnp.concatenate([v, z8], 0), jnp.concatenate([z8, v], 0))
                acc[c, pl.ds(ta, W + 8), pl.ds(la + 128 * k, H)] += v.reshape(W + 8, H)

    def units(s, b, used):
        for m in range(2):
            for j in range(0, H, HC):
                def waves(m=m, j=j):
                    at = [slice(j, j + HC), slice(H + j, H + j + HC)]
                    get = lambda ref, *i: cat0(ref[(*i, at[0])], ref[(*i, at[1])])
                    pr, pi = get(prv, 0, m), get(prv, 1, m)
                    xr, xi = get(patch, b, 0), get(patch, b, 1)
                    wr = pr * xr - pi * xi
                    wi = pr * xi + pi * xr
                    e = cat1(wr[:, :H] + wr[:, H:], wi[:, :H] + wi[:, H:])
                    o = cat1(wr[:, :H] - wr[:, H:], wi[:, :H] - wi[:, H:])
                    return rmul(e, tb[0]), rmul(o, tb[1])

                def rows(ys, m=m, j=j):
                    for p in range(2):
                        lanes = slice(H * p, H * p + H)
                        y = ys[p]
                        for q in range(2):
                            f = y[:HC] + y[HC:] if q == 0 else y[:HC] - y[HC:]
                            hi, lo = split(f)
                            for part in range(2):
                                r = H * part + j
                                gs[b, m, q, r:r + HC, lanes] = hi[:, H * part:H * part + H]
                                gs[b, m, q, W + r:W + r + HC, lanes] = lo[:, H * part:H * part + H]

                yield waves, rows
        for q in range(2):
            for j in range(0, H, HC):
                def fars(q=q, j=j):
                    t = tb[2 + q]
                    return [lmul2(t, gs[b, m, q, :W], gs[b, m, q, W:]) for m in range(2)]

                def factors(fars, q=q, j=j):
                    mod = sum(a[:HC] * a[:HC] + a[HC:] * a[HC:] for a in fars)
                    root = sqv[s, H * q + j:H * q + j + HC, :]
                    fac = used - (used * root) * lax.rsqrt(jnp.maximum(mod, 0.1))
                    for m in range(2):
                        for part in range(2):
                            hi, lo = split(fars[m][HC * part:HC * part + HC] * fac)
                            r = H * part + j
                            hs[b, m, q, r:r + HC] = hi
                            hs[b, m, q, W + r:W + r + HC] = lo

                yield fars, factors
        for m in range(2):
            for j in range(0, H, HC):
                def backs(m=m, j=j):
                    out = []
                    for q in range(2):
                        t = tb[q]
                        out.append(lmul2(t, hs[b, m, q, :W], hs[b, m, q, W:]))
                    return out

                def columns(v, m=m, j=j):
                    for top in range(2):
                        x = v[0] + v[1] if top == 0 else v[0] - v[1]
                        for p in range(2):
                            hi, lo = split(cat1(x[:HC, H * p:H * p + H], x[HC:, H * p:H * p + H]))
                            r = H * top + j
                            ds[b, m, p, r:r + HC, :W] = hi
                            ds[b, m, p, r:r + HC, W:] = lo

                yield backs, columns
        for m in range(2):
            for j in (0, H):
                at = slice(j, j + H)

                def last(m=m, at=at):
                    return [rmul2(ds[b, m, p, at, :W], ds[b, m, p, at, W:], tb[2 + p]) for p in range(2)]

                def terms(d, m=m, at=at):
                    for h in range(2):
                        x = d[0] + d[1] if h == 0 else d[0] - d[1]
                        br, bi = x[:, :H], x[:, H:]
                        lanes = slice(H * h, H * h + H)
                        pr, pi = prv[0, m, at, lanes], prv[1, m, at, lanes]
                        xr, xi = patch[b, 0, at, lanes], patch[b, 1, at, lanes]
                        tr, ti = pr * br + pi * bi, pr * bi - pi * br
                        if m == 0:
                            term[b, 0, at, lanes], term[b, 1, at, lanes] = tr, ti
                        else:
                            term[b, 0, at, lanes] += tr
                            term[b, 1, at, lanes] += ti
                        pacc[0, m, at, lanes] += xr * br + xi * bi
                        pacc[1, m, at, lanes] += xr * bi - xi * br

                yield last, terms

    def pair(i, carry):
        slots = [i * NB + b for b in range(NB)]
        used = [jnp.where(s < live[0], 1.0, 0.0) for s in slots]
        for b in range(NB):
            roots(slots[b]).wait()
            fetch(slots[b], b)
        streams = [list(units(slots[b], b, used[b])) for b in range(NB)]
        todo = []
        for group in zip(*streams):
            for product, then in group:
                todo.append((then, product()))
                if len(todo) > LAG:
                    then, value = todo.pop(0)
                    then(value)
        for then, value in todo:
            then(value)
        for b in range(NB):
            deposit(slots[b], b)
        return carry

    pairs = lax.div(live[0] + NB - 1, NB)
    lax.fori_loop(0, pairs, pair, 0)

    def skip(s, carry):
        roots(s).wait()
        return carry

    lax.fori_loop(pairs * NB, 8, skip, 0)
    outs = [
        (acc.at[:, 256:512, 512:768], o_rbot),
        (acc.at[:, 0:256, 512:768], o_rtop),
        (acc.at[:, 512:768, :], o_below),
        (prv.at[1], o_other),
        (prv.at[0], o_mine),
        (cov.at[0, 0:512, 0:512], o_part.at[0]),
        (cov.at[1, 0:512, 0:512], o_part.at[1]),
    ]
    copies = [pltpu.make_async_copy(s, d, sems.at[i]) for i, (s, d) in enumerate(outs)]
    for c in copies[:3]:
        c.start()
    for kc in range(2):
        prv[kc] = pacc[lax.rem(anchor[2] + kc, 2)]
    for c in copies[3:5]:
        c.start()
    for c in range(2):
        cov[c, 0:512, 0:512] = cov[c, 0:512, 0:512] - 0.5 * acc[c, 0:512, 0:512]
        copies[5 + c].start()
    for c in copies:
        c.wait()


def main_call(offs, live, anchor, obj, right_top, right_bot, below, corner, probe, sq):
    any_ = pl.BlockSpec(memory_space=pl.ANY)
    smem = pl.BlockSpec(memory_space=pltpu.SMEM)
    S = lambda *s: jax.ShapeDtypeStruct(s, f32)
    return pl.pallas_call(
        main_kernel,
        out_shape=(S(2, 512, 512), S(2, 256, 256), S(2, 256, 256), S(2, 256, 768), S(2, 256, 256), S(2, 256, 256)),
        in_specs=[smem] * 3 + [any_] * 8,
        out_specs=[any_] * 6,
        scratch_shapes=[
            pltpu.VMEM((2, 768, 768), f32),
            pltpu.VMEM((2, 768, 768), f32),
            pltpu.VMEM((NB, 2, W, W), f32),
            pltpu.VMEM((2, 2, W, W), f32),
            pltpu.VMEM((2, 2, W, W), f32),
            pltpu.VMEM((8, W, W), f32),
            pltpu.VMEM((4, 2, W, W), bf16),
            pltpu.VMEM((NB, 2, 2, 2 * W, W), bf16),
            pltpu.VMEM((NB, 2, 2, 2 * W, W), bf16),
            pltpu.VMEM((NB, 2, 2, W, 2 * W), bf16),
            pltpu.VMEM((NB, 2, W, W), f32),
            pltpu.SemaphoreType.DMA((9,)),
            pltpu.SemaphoreType.DMA((8,)),
        ],
        compiler_params=pltpu.CompilerParams(vmem_limit_bytes=62 * 2**20),
        name="slots",
    )(offs, live, anchor, obj, right_top, right_bot, below, corner, probe, sq, jnp.asarray(make_tables()))


def prep_kernel(counts, pm, pmt, out):
    i = counts[0].astype(f32).astype(bf16)
    a = jnp.dot(pm[...], i, preferred_element_type=f32).astype(bf16)
    out[0] = jnp.sqrt(jnp.dot(a, pmt[...], preferred_element_type=f32))


def prep_call(counts):
    order = np.concatenate([np.arange(0, W, 2), np.arange(1, W, 2)])
    pm = np.zeros((W, W), np.float32)
    pm[np.arange(W), order] = 1.0
    full = pl.BlockSpec((W, W), lambda s: (0, 0))
    blk = pl.BlockSpec((1, W, W), lambda s: (s, 0, 0))
    return pl.pallas_call(
        prep_kernel,
        grid=(8,),
        out_shape=jax.ShapeDtypeStruct((8, W, W), f32),
        in_specs=[blk, full, full],
        out_specs=blk,
        name="roots",
    )(counts, jnp.asarray(pm.astype(ml_dtypes.bfloat16)), jnp.asarray(pm.T.astype(ml_dtypes.bfloat16)))


def moved(value, axes, pairs):
    return lax.ppermute(value, axes, pairs)


def finish_kernel(part, above, top, bot, out):
    h = pl.program_id(1)

    @pl.when(h == 0)
    def _():
        out[0] = part[0] - 0.5 * above[0]
        out[0, :, :W] -= 0.5 * top[0]

    @pl.when(h == 1)
    def _():
        out[0, :, W:] = part[0, :, W:]
        out[0, :, :W] = part[0, :, :W] - 0.5 * bot[0]


def finish_call(part, above, top, bot):
    wide = pl.BlockSpec((1, W, 512), lambda c, h: (c, h, 0))
    return pl.pallas_call(
        finish_kernel,
        grid=(2, 2),
        out_shape=jax.ShapeDtypeStruct((2, 512, 512), f32),
        in_specs=[
            wide,
            pl.BlockSpec((1, W, 512), lambda c, h: (c, 0, 0)),
            pl.BlockSpec((1, W, W), lambda c, h: (c, 0, 0)),
            pl.BlockSpec((1, W, W), lambda c, h: (c, 0, 0)),
        ],
        out_specs=wide,
        compiler_params=pltpu.CompilerParams(vmem_limit_bytes=8 * 2**20),
        name="finish",
    )(part, above, top, bot)


def swap_cores(value):
    return lax.ppermute(value, "core", [(0, 1), (1, 0)])


def sum_everywhere(value, axis):
    got = [lax.ppermute(value, axis, [(i, (i + k) % 4) for i in range(4)]) for k in (2, 1, 3)]
    return (value + got[0]) + (got[1] + got[2])


def probe_kernel(step, place, probe, mine, rest, out):
    for kc in range(2):
        at = pl.multiple_of(lax.rem(place[2] + kc, 2) * 512, 512)
        out[pl.ds(at, 512), :] = probe[pl.ds(at, 512), :] - step * (mine, rest)[kc][...]


def shards(object_planes, probe_planes, offsets, photon_counts, live_counts):
    n_row = lax.axis_size("y") * lax.axis_size("core")
    n_col = lax.axis_size("x") * lax.axis_size("z")
    rows, cols = ("y", "core"), ("x", "z")
    up = [(i, i - 1) for i in range(1, n_row)]
    down = [(i - 1, i) for i in range(1, n_row)]
    to_left = [(i, i - 1) for i in range(1, n_col)]
    to_right = [(i - 1, i) for i in range(1, n_col)]

    edge = object_planes[:, :W, :W]
    edge, whole = lax.optimization_barrier((edge, object_planes))
    right_top = lax.ppermute(edge, cols, to_left)
    below = lax.ppermute(whole[:, :W, :], rows, up)
    right_bot = lax.ppermute(whole[:, W:, :W], cols, to_left)
    roots = prep_call(photon_counts)
    right_top, roots = lax.optimization_barrier((right_top, roots))
    corner = lax.ppermute(right_top, rows, up)
    place = jnp.stack(
        [lax.axis_index(rows) * 512, lax.axis_index(cols) * 512] + [lax.axis_index(a) for a in ("core",)]
    ).astype(jnp.int32)
    part, g_top, g_bot, g_below, mine, other = main_call(
        offsets, live_counts.reshape(1), place, object_planes, right_top, right_bot, below, corner, probe_planes, roots
    )
    bot_in = lax.ppermute(g_bot, cols, to_right)
    above_in = lax.ppermute(g_below, rows, down)
    half = (mine + swap_cores(other)).reshape(16, 32, W)
    top_in = lax.ppermute(g_top + above_in[:, :, 512:], cols, to_right)
    plane = ("y", "x")
    piece = lax.all_to_all(half, plane, 0, 0).sum(0)
    piece, bot_in = lax.optimization_barrier((piece, bot_in))
    piece = sum_everywhere(piece, "z")
    piece, top_in, above_in = lax.optimization_barrier((piece, top_in, above_in))
    new_object = finish_call(part, above_in, top_in, bot_in)
    half = lax.all_to_all(jnp.broadcast_to(piece[None], half.shape), plane, 0, 0).reshape(512, W)
    half, new_object = lax.optimization_barrier((half, new_object))
    rest = swap_cores(half)
    smem, vmem = pl.BlockSpec(memory_space=pltpu.SMEM), pl.BlockSpec(memory_space=pltpu.VMEM)
    step = 1.0 / math.sqrt(offsets.shape[0] * n_row * n_col)
    new_probe = pl.pallas_call(
        functools.partial(probe_kernel, step),
        out_shape=jax.ShapeDtypeStruct((1024, W), f32),
        in_specs=[smem] + [vmem] * 3,
        out_specs=vmem,
        compiler_params=pltpu.CompilerParams(vmem_limit_bytes=8 * 2**20),
        name="probe",
    )(place, probe_planes.reshape(1024, W), half, rest)
    return new_object, new_probe.reshape(probe_planes.shape)


def solution(mesh):
    split = jax.sharding.Mesh(
        mesh.devices.reshape(mesh.shape["row"] // 2, 2, mesh.shape["col"] // 4, 4), ("y", "core", "x", "z")
    )
    rows, cols = ("y", "core"), ("x", "z")
    in_specs = (
        P(None, rows, cols),
        P(),
        P(rows + cols, None),
        P(rows + cols, None, None),
        P(rows, cols),
    )
    out_specs = (P(None, rows, cols), P())
    return jax.shard_map(shards, mesh=split, in_specs=in_specs, out_specs=out_specs, check_vma=False)
```

```python
import functools
import math

import ml_dtypes
import numpy as np
import jax
import jax.numpy as jnp
from jax import lax
from jax.experimental import pallas as pl
from jax.experimental.pallas import tpu as pltpu
from jax.sharding import PartitionSpec as P

f32, bf16 = jnp.float32, jnp.bfloat16
W = 256
H = 128
HC = 128
NB = 2
LAG = 0


def make_tables():
    b = np.arange(H)[:, None]
    q = np.arange(H)[None, :]
    right = []
    for p in (0, 1):
        ang = 2.0 * np.pi * (((2 * q + p) * b) % W) / W
        c, s = np.cos(ang) / 16.0, np.sin(ang) / 16.0
        right.append(np.block([[c, -s], [s, c]]))
    out = []
    for t in (right[0], right[1], right[0].T, right[1].T):
        hi = t.astype(np.float32).astype(ml_dtypes.bfloat16)
        lo = (t - hi.astype(np.float64)).astype(np.float32).astype(ml_dtypes.bfloat16)
        out.append(np.stack([hi, lo]))
    return np.stack(out)


def split(x):
    hi = x.astype(bf16)
    lo = (x - hi.astype(f32)).astype(bf16)
    return hi, lo


def rmul2(hi, lo, t):
    return jnp.dot(jnp.concatenate([hi, lo, hi], 1), jnp.concatenate([t[0], t[0], t[1]], 0), preferred_element_type=f32)


def rmul(x, t):
    hi, lo = split(x)
    return rmul2(hi, lo, t)


def lmul2(t, hi, lo):
    return jnp.dot(jnp.concatenate([t[0], t[0], t[1]], 1), jnp.concatenate([hi, lo, hi], 0), preferred_element_type=f32)


def cat1(a, b):
    return jnp.concatenate([a, b], 1)


def cat0(a, b):
    return jnp.concatenate([a, b], 0)


def main_kernel(offs, live, anchor, obj, right_top, right_bot, below, corner, probe, sq, tables,
                o_part, o_rtop, o_rbot, o_corner, o_below, o_mine, o_other,
                cov, acc, patch, pacc, prv, sqv, tb, gs, hs, ds, term, sems, sqsems):
    ins = [
        (obj, cov.at[:, 0:512, 0:512]),
        (right_top, cov.at[:, 0:256, 512:768]),
        (right_bot, cov.at[:, 256:512, 512:768]),
        (below, cov.at[:, 512:768, 0:512]),
        (corner, cov.at[:, 512:768, 512:768]),
        (probe, prv),
        (tables, tb),
    ]
    copies = [pltpu.make_async_copy(s, d, sems.at[i]) for i, (s, d) in enumerate(ins)]
    roots = lambda s: pltpu.make_async_copy(sq.at[s], sqv.at[s], sqsems.at[s])
    for c in copies:
        c.start()
    for s in range(8):
        roots(s).start()
    acc[...] = jnp.zeros_like(acc)
    pacc[...] = jnp.zeros_like(pacc)
    for c in copies:
        c.wait()
    lane = lax.broadcasted_iota(jnp.int32, (W, H), 1)
    sub9 = lax.broadcasted_iota(jnp.int32, (33, 8, H), 1)
    sub = lax.broadcasted_iota(jnp.int32, (32, 8, H), 1)

    def place_of(s):
        top = offs[s, 0] - anchor[0]
        left = offs[s, 1] - anchor[1]
        la = pl.multiple_of(lax.div(left, 128) * 128, 128)
        ta = pl.multiple_of(lax.div(top, 8) * 8, 8)
        return ta, lax.rem(top, 8), la, lax.rem(left, 128)

    def fetch(s, b):
        ta, rs, la, ls = place_of(s)
        back = lax.rem(128 - ls, 128)
        rback = lax.rem(8 - rs, 8)
        for c in range(2):
            t = []
            for k in range(3):
                v = cov[c, pl.ds(ta, W + 8), pl.ds(la + 128 * k, H)]
                v = pltpu.roll(pltpu.roll(v, back, 1).reshape(33, 8, H), rback, 1)
                t.append(jnp.where(sub < 8 - rs, v[:32], v[1:]).reshape(W, H))
            for k in range(2):
                patch[b, c, :, 128 * k:128 * k + 128] = jnp.where(lane < 128 - ls, t[k], t[k + 1])

    def deposit(s, b):
        ta, rs, la, ls = place_of(s)
        for c in range(2):
            r = [pltpu.roll(term[b, c, :, 128 * k:128 * k + 128], ls, 1) for k in range(2)]
            z = jnp.zeros_like(r[0])
            keep = lane >= ls
            parts = [jnp.where(keep, r[0], z), jnp.where(keep, r[1], r[0]), jnp.where(keep, z, r[1])]
            for k in range(3):
                v = pltpu.roll(parts[k].reshape(32, 8, H), rs, 1)
                z8 = jnp.zeros((1, 8, H), f32)
                v = jnp.where(sub9 >= rs, jnp.concatenate([v, z8], 0), jnp.concatenate([z8, v], 0))
                acc[c, pl.ds(ta, W + 8), pl.ds(la + 128 * k, H)] += v.reshape(W + 8, H)

    def units(s, b, used):
        for m in range(2):
            for j in range(0, H, HC):
                def waves(m=m, j=j):
                    at = [slice(j, j + HC), slice(H + j, H + j + HC)]
                    get = lambda ref, *i: cat0(ref[(*i, at[0])], ref[(*i, at[1])])
                    pr, pi = get(prv, 0, m), get(prv, 1, m)
                    xr, xi = get(patch, b, 0), get(patch, b, 1)
                    wr = pr * xr - pi * xi
                    wi = pr * xi + pi * xr
                    e = cat1(wr[:, :H] + wr[:, H:], wi[:, :H] + wi[:, H:])
                    o = cat1(wr[:, :H] - wr[:, H:], wi[:, :H] - wi[:, H:])
                    return rmul(e, tb[0]), rmul(o, tb[1])

                def rows(ys, m=m, j=j):
                    for p in range(2):
                        lanes = slice(H * p, H * p + H)
                        y = ys[p]
                        for q in range(2):
                            f = y[:HC] + y[HC:] if q == 0 else y[:HC] - y[HC:]
                            hi, lo = split(f)
                            for part in range(2):
                                r = H * part + j
                                gs[b, m, q, r:r + HC, lanes] = hi[:, H * part:H * part + H]
                                gs[b, m, q, W + r:W + r + HC, lanes] = lo[:, H * part:H * part + H]

                yield waves, rows
        for q in range(2):
            for j in range(0, H, HC):
                def fars(q=q, j=j):
                    t = tb[2 + q]
                    return [lmul2(t, gs[b, m, q, :W], gs[b, m, q, W:]) for m in range(2)]

                def factors(fars, q=q, j=j):
                    mod = sum(a[:HC] * a[:HC] + a[HC:] * a[HC:] for a in fars)
                    root = sqv[s, H * q + j:H * q + j + HC, :]
                    fac = used - (used * root) * lax.rsqrt(jnp.maximum(mod, 0.1))
                    for m in range(2):
                        for part in range(2):
                            hi, lo = split(fars[m][HC * part:HC * part + HC] * fac)
                            r = H * part + j
                            hs[b, m, q, r:r + HC] = hi
                            hs[b, m, q, W + r:W + r + HC] = lo

                yield fars, factors
        for m in range(2):
            for j in range(0, H, HC):
                def backs(m=m, j=j):
                    out = []
                    for q in range(2):
                        t = tb[q]
                        out.append(lmul2(t, hs[b, m, q, :W], hs[b, m, q, W:]))
                    return out

                def columns(v, m=m, j=j):
                    for top in range(2):
                        x = v[0] + v[1] if top == 0 else v[0] - v[1]
                        for p in range(2):
                            hi, lo = split(cat1(x[:HC, H * p:H * p + H], x[HC:, H * p:H * p + H]))
                            r = H * top + j
                            ds[b, m, p, r:r + HC, :W] = hi
                            ds[b, m, p, r:r + HC, W:] = lo

                yield backs, columns
        for m in range(2):
            for j in (0, H):
                at = slice(j, j + H)

                def last(m=m, at=at):
                    return [rmul2(ds[b, m, p, at, :W], ds[b, m, p, at, W:], tb[2 + p]) for p in range(2)]

                def terms(d, m=m, at=at):
                    for h in range(2):
                        x = d[0] + d[1] if h == 0 else d[0] - d[1]
                        br, bi = x[:, :H], x[:, H:]
                        lanes = slice(H * h, H * h + H)
                        pr, pi = prv[0, m, at, lanes], prv[1, m, at, lanes]
                        xr, xi = patch[b, 0, at, lanes], patch[b, 1, at, lanes]
                        tr, ti = pr * br + pi * bi, pr * bi - pi * br
                        if m == 0:
                            term[b, 0, at, lanes], term[b, 1, at, lanes] = tr, ti
                        else:
                            term[b, 0, at, lanes] += tr
                            term[b, 1, at, lanes] += ti
                        pacc[0, m, at, lanes] += xr * br + xi * bi
                        pacc[1, m, at, lanes] += xr * bi - xi * br

                yield last, terms

    def pair(i, carry):
        slots = [i * NB + b for b in range(NB)]
        used = [jnp.where(s < live[0], 1.0, 0.0) for s in slots]
        for b in range(NB):
            roots(slots[b]).wait()
            fetch(slots[b], b)
        streams = [list(units(slots[b], b, used[b])) for b in range(NB)]
        todo = []
        for group in zip(*streams):
            for product, then in group:
                todo.append((then, product()))
                if len(todo) > LAG:
                    then, value = todo.pop(0)
                    then(value)
        for then, value in todo:
            then(value)
        for b in range(NB):
            deposit(slots[b], b)
        return carry

    pairs = lax.div(live[0] + NB - 1, NB)
    lax.fori_loop(0, pairs, pair, 0)

    def skip(s, carry):
        roots(s).wait()
        return carry

    lax.fori_loop(pairs * NB, 8, skip, 0)
    outs = [
        (acc.at[:, 512:768, 512:768], o_corner),
        (acc.at[:, 256:512, 512:768], o_rbot),
        (acc.at[:, 0:256, 512:768], o_rtop),
        (acc.at[:, 512:768, 0:512], o_below),
        (prv.at[1], o_other),
        (prv.at[0], o_mine),
        (cov.at[0, 0:512, 0:512], o_part.at[0]),
        (cov.at[1, 0:512, 0:512], o_part.at[1]),
    ]
    copies = [pltpu.make_async_copy(s, d, sems.at[i]) for i, (s, d) in enumerate(outs)]
    for c in copies[:4]:
        c.start()
    for kc in range(2):
        prv[kc] = pacc[lax.rem(anchor[2] + kc, 2)]
    for c in copies[4:6]:
        c.start()
    for c in range(2):
        cov[c, 0:512, 0:512] = cov[c, 0:512, 0:512] - 0.5 * acc[c, 0:512, 0:512]
        copies[6 + c].start()
    for c in copies:
        c.wait()


def main_call(offs, live, anchor, obj, right_top, right_bot, below, corner, probe, sq):
    any_ = pl.BlockSpec(memory_space=pl.ANY)
    smem = pl.BlockSpec(memory_space=pltpu.SMEM)
    S = lambda *s: jax.ShapeDtypeStruct(s, f32)
    return pl.pallas_call(
        main_kernel,
        out_shape=(S(2, 512, 512), S(2, 256, 256), S(2, 256, 256), S(2, 256, 256), S(2, 256, 512), S(2, 256, 256), S(2, 256, 256)),
        in_specs=[smem] * 3 + [any_] * 8,
        out_specs=[any_] * 7,
        scratch_shapes=[
            pltpu.VMEM((2, 768, 768), f32),
            pltpu.VMEM((2, 768, 768), f32),
            pltpu.VMEM((NB, 2, W, W), f32),
            pltpu.VMEM((2, 2, W, W), f32),
            pltpu.VMEM((2, 2, W, W), f32),
            pltpu.VMEM((8, W, W), f32),
            pltpu.VMEM((4, 2, W, W), bf16),
            pltpu.VMEM((NB, 2, 2, 2 * W, W), bf16),
            pltpu.VMEM((NB, 2, 2, 2 * W, W), bf16),
            pltpu.VMEM((NB, 2, 2, W, 2 * W), bf16),
            pltpu.VMEM((NB, 2, W, W), f32),
            pltpu.SemaphoreType.DMA((9,)),
            pltpu.SemaphoreType.DMA((8,)),
        ],
        compiler_params=pltpu.CompilerParams(vmem_limit_bytes=62 * 2**20),
        name="slots",
    )(offs, live, anchor, obj, right_top, right_bot, below, corner, probe, sq, jnp.asarray(make_tables()))


def prep_kernel(counts, pm, pmt, out):
    i = counts[0].astype(f32).astype(bf16)
    a = jnp.dot(pm[...], i, preferred_element_type=f32).astype(bf16)
    out[0] = jnp.sqrt(jnp.dot(a, pmt[...], preferred_element_type=f32))


def prep_call(counts):
    order = np.concatenate([np.arange(0, W, 2), np.arange(1, W, 2)])
    pm = np.zeros((W, W), np.float32)
    pm[np.arange(W), order] = 1.0
    full = pl.BlockSpec((W, W), lambda s: (0, 0))
    blk = pl.BlockSpec((1, W, W), lambda s: (s, 0, 0))
    return pl.pallas_call(
        prep_kernel,
        grid=(8,),
        out_shape=jax.ShapeDtypeStruct((8, W, W), f32),
        in_specs=[blk, full, full],
        out_specs=blk,
        name="roots",
    )(counts, jnp.asarray(pm.astype(ml_dtypes.bfloat16)), jnp.asarray(pm.T.astype(ml_dtypes.bfloat16)))


def moved(value, axes, pairs):
    return lax.ppermute(value, axes, pairs)


def finish_kernel(part, above, top, bot, out):
    q = pl.program_id(1)

    @pl.when(q == 0)
    def _():
        out[...] = part[...] - 0.5 * (above[...] + top[...])

    @pl.when(q == 1)
    def _():
        out[...] = part[...] - 0.5 * above[...]

    @pl.when(q == 2)
    def _():
        out[...] = part[...] - 0.5 * bot[...]


def finish_call(part, above, top, bot):
    quarter = pl.BlockSpec((1, W, W), lambda c, q: (c, q // 2, q % 2))
    plane = pl.BlockSpec((1, W, W), lambda c, q: (c, 0, 0))
    return pl.pallas_call(
        finish_kernel,
        grid=(2, 3),
        out_shape=jax.ShapeDtypeStruct((2, 512, 512), f32),
        in_specs=[quarter, pl.BlockSpec((1, W, W), lambda c, q: (c, 0, q % 2)), plane, plane],
        out_specs=quarter,
        input_output_aliases={0: 0},
        compiler_params=pltpu.CompilerParams(vmem_limit_bytes=8 * 2**20),
        name="finish",
    )(part, above, top, bot)


def swap_cores(value):
    return lax.ppermute(value, "core", [(0, 1), (1, 0)])


def sum_everywhere(value, axis):
    got = [lax.ppermute(value, axis, [(i, (i + k) % 4) for i in range(4)]) for k in (2, 1, 3)]
    return (value + got[0]) + (got[1] + got[2])


def probe_kernel(step, place, probe, mine, rest, out):
    for kc in range(2):
        at = pl.multiple_of(lax.rem(place[2] + kc, 2) * 512, 512)
        out[pl.ds(at, 512), :] = probe[pl.ds(at, 512), :] - step * (mine, rest)[kc][...]


def shards(object_planes, probe_planes, offsets, photon_counts, live_counts):
    n_row = lax.axis_size("y") * lax.axis_size("core")
    n_col = lax.axis_size("x") * lax.axis_size("z")
    rows, cols = ("y", "core"), ("x", "z")
    up = [(i, i - 1) for i in range(1, n_row)]
    down = [(i - 1, i) for i in range(1, n_row)]
    to_left = [(i, i - 1) for i in range(1, n_col)]
    to_right = [(i - 1, i) for i in range(1, n_col)]

    right_top = lax.ppermute(object_planes[:, :W, :W], cols, to_left)
    below = lax.ppermute(object_planes[:, :W, :], rows, up)
    right_bot = lax.ppermute(object_planes[:, W:, :W], cols, to_left)
    roots = prep_call(photon_counts)
    right_top, roots = lax.optimization_barrier((right_top, roots))
    corner = lax.ppermute(right_top, rows, up)
    place = jnp.stack(
        [lax.axis_index(rows) * 512, lax.axis_index(cols) * 512] + [lax.axis_index(a) for a in ("core",)]
    ).astype(jnp.int32)
    part, g_top, g_bot, g_corner, g_below, mine, other = main_call(
        offsets, live_counts.reshape(1), place, object_planes, right_top, right_bot, below, corner, probe_planes, roots
    )
    corner_in = lax.ppermute(g_corner, rows, down)
    bot_in = lax.ppermute(g_bot, cols, to_right)
    above_in = lax.ppermute(g_below, rows, down)
    half = (mine + swap_cores(other)).reshape(16, 32, W)
    top_in = lax.ppermute(g_top + corner_in, cols, to_right)
    plane = ("y", "x")
    piece = lax.all_to_all(half, plane, 0, 0).sum(0)
    piece, bot_in = lax.optimization_barrier((piece, bot_in))
    piece = sum_everywhere(piece, "z")
    piece, top_in = lax.optimization_barrier((piece, top_in))
    new_object = finish_call(part, above_in, top_in, bot_in)
    half = lax.all_to_all(jnp.broadcast_to(piece[None], half.shape), plane, 0, 0).reshape(512, W)
    rest = swap_cores(half)
    smem, vmem = pl.BlockSpec(memory_space=pltpu.SMEM), pl.BlockSpec(memory_space=pltpu.VMEM)
    step = 1.0 / math.sqrt(offsets.shape[0] * n_row * n_col)
    new_probe = pl.pallas_call(
        functools.partial(probe_kernel, step),
        out_shape=jax.ShapeDtypeStruct((1024, W), f32),
        in_specs=[smem] + [vmem] * 3,
        out_specs=vmem,
        compiler_params=pltpu.CompilerParams(vmem_limit_bytes=8 * 2**20),
        name="probe",
    )(place, probe_planes.reshape(1024, W), half, rest)
    return new_object, new_probe.reshape(probe_planes.shape)


def solution(mesh):
    split = jax.sharding.Mesh(
        mesh.devices.reshape(mesh.shape["row"] // 2, 2, mesh.shape["col"] // 4, 4), ("y", "core", "x", "z")
    )
    rows, cols = ("y", "core"), ("x", "z")
    in_specs = (
        P(None, rows, cols),
        P(),
        P(rows + cols, None),
        P(rows + cols, None, None),
        P(rows, cols),
    )
    out_specs = (P(None, rows, cols), P())
    return jax.shard_map(shards, mesh=split, in_specs=in_specs, out_specs=out_specs, check_vma=False)
```

```python
import functools
import math

import ml_dtypes
import numpy as np
import jax
import jax.numpy as jnp
from jax import lax
from jax.experimental import pallas as pl
from jax.experimental.pallas import tpu as pltpu
from jax.sharding import PartitionSpec as P

f32, bf16 = jnp.float32, jnp.bfloat16
W = 256
H = 128
HC = 128
NB = 2
LAG = 0


def make_tables():
    b = np.arange(H)[:, None]
    q = np.arange(H)[None, :]
    right = []
    for p in (0, 1):
        ang = 2.0 * np.pi * (((2 * q + p) * b) % W) / W
        c, s = np.cos(ang) / 16.0, np.sin(ang) / 16.0
        right.append(np.block([[c, -s], [s, c]]))
    out = []
    for t in (right[0], right[1], right[0].T, right[1].T):
        hi = t.astype(np.float32).astype(ml_dtypes.bfloat16)
        lo = (t - hi.astype(np.float64)).astype(np.float32).astype(ml_dtypes.bfloat16)
        out.append(np.stack([hi, lo]))
    return np.stack(out)


def split(x):
    hi = x.astype(bf16)
    lo = (x - hi.astype(f32)).astype(bf16)
    return hi, lo


def rmul2(hi, lo, t):
    return jnp.dot(jnp.concatenate([hi, lo, hi], 1), jnp.concatenate([t[0], t[0], t[1]], 0), preferred_element_type=f32)


def rmul(x, t):
    hi, lo = split(x)
    return rmul2(hi, lo, t)


def lmul2(t, hi, lo):
    return jnp.dot(jnp.concatenate([t[0], t[0], t[1]], 1), jnp.concatenate([hi, lo, hi], 0), preferred_element_type=f32)


def cat1(a, b):
    return jnp.concatenate([a, b], 1)


def cat0(a, b):
    return jnp.concatenate([a, b], 0)


def main_kernel(offs, live, anchor, obj, right_top, right_bot, below, corner, probe, sq, tables,
                o_part, o_rtop, o_rbot, o_corner, o_below, o_mine, o_other,
                cov, acc, patch, pacc, prv, sqv, tb, gs, hs, ds, term, sems, sqsems):
    ins = [
        (obj, cov.at[:, 0:512, 0:512]),
        (right_top, cov.at[:, 0:256, 512:768]),
        (right_bot, cov.at[:, 256:512, 512:768]),
        (below, cov.at[:, 512:768, 0:512]),
        (corner, cov.at[:, 512:768, 512:768]),
        (probe, prv),
        (tables, tb),
    ]
    copies = [pltpu.make_async_copy(s, d, sems.at[i]) for i, (s, d) in enumerate(ins)]
    roots = lambda s: pltpu.make_async_copy(sq.at[s], sqv.at[s], sqsems.at[s])
    for c in copies:
        c.start()
    for s in range(8):
        roots(s).start()
    acc[...] = jnp.zeros_like(acc)
    pacc[...] = jnp.zeros_like(pacc)
    for c in copies:
        c.wait()
    lane = lax.broadcasted_iota(jnp.int32, (W, H), 1)
    sub9 = lax.broadcasted_iota(jnp.int32, (33, 8, H), 1)
    sub = lax.broadcasted_iota(jnp.int32, (32, 8, H), 1)

    def place_of(s):
        top = offs[s, 0] - anchor[0]
        left = offs[s, 1] - anchor[1]
        la = pl.multiple_of(lax.div(left, 128) * 128, 128)
        ta = pl.multiple_of(lax.div(top, 8) * 8, 8)
        return ta, lax.rem(top, 8), la, lax.rem(left, 128)

    def fetch(s, b):
        ta, rs, la, ls = place_of(s)
        back = lax.rem(128 - ls, 128)
        rback = lax.rem(8 - rs, 8)
        for c in range(2):
            t = []
            for k in range(3):
                v = cov[c, pl.ds(ta, W + 8), pl.ds(la + 128 * k, H)]
                v = pltpu.roll(pltpu.roll(v, back, 1).reshape(33, 8, H), rback, 1)
                t.append(jnp.where(sub < 8 - rs, v[:32], v[1:]).reshape(W, H))
            for k in range(2):
                patch[b, c, :, 128 * k:128 * k + 128] = jnp.where(lane < 128 - ls, t[k], t[k + 1])

    def deposit(s, b):
        ta, rs, la, ls = place_of(s)
        for c in range(2):
            r = [pltpu.roll(term[b, c, :, 128 * k:128 * k + 128], ls, 1) for k in range(2)]
            z = jnp.zeros_like(r[0])
            keep = lane >= ls
            parts = [jnp.where(keep, r[0], z), jnp.where(keep, r[1], r[0]), jnp.where(keep, z, r[1])]
            for k in range(3):
                v = pltpu.roll(parts[k].reshape(32, 8, H), rs, 1)
                z8 = jnp.zeros((1, 8, H), f32)
                v = jnp.where(sub9 >= rs, jnp.concatenate([v, z8], 0), jnp.concatenate([z8, v], 0))
                acc[c, pl.ds(ta, W + 8), pl.ds(la + 128 * k, H)] += v.reshape(W + 8, H)

    def units(s, b, used):
        for m in range(2):
            for j in range(0, H, HC):
                def waves(m=m, j=j):
                    at = [slice(j, j + HC), slice(H + j, H + j + HC)]
                    get = lambda ref, *i: cat0(ref[(*i, at[0])], ref[(*i, at[1])])
                    pr, pi = get(prv, 0, m), get(prv, 1, m)
                    xr, xi = get(patch, b, 0), get(patch, b, 1)
                    wr = pr * xr - pi * xi
                    wi = pr * xi + pi * xr
                    e = cat1(wr[:, :H] + wr[:, H:], wi[:, :H] + wi[:, H:])
                    o = cat1(wr[:, :H] - wr[:, H:], wi[:, :H] - wi[:, H:])
                    return rmul(e, tb[0]), rmul(o, tb[1])

                def rows(ys, m=m, j=j):
                    for p in range(2):
                        lanes = slice(H * p, H * p + H)
                        y = ys[p]
                        for q in range(2):
                            f = y[:HC] + y[HC:] if q == 0 else y[:HC] - y[HC:]
                            hi, lo = split(f)
                            for part in range(2):
                                r = H * part + j
                                gs[b, m, q, r:r + HC, lanes] = hi[:, H * part:H * part + H]
                                gs[b, m, q, W + r:W + r + HC, lanes] = lo[:, H * part:H * part + H]

                yield waves, rows
        for q in range(2):
            for j in range(0, H, HC):
                def fars(q=q, j=j):
                    t = tb[2 + q]
                    return [lmul2(t, gs[b, m, q, :W], gs[b, m, q, W:]) for m in range(2)]

                def factors(fars, q=q, j=j):
                    mod = sum(a[:HC] * a[:HC] + a[HC:] * a[HC:] for a in fars)
                    root = sqv[s, H * q + j:H * q + j + HC, :]
                    fac = used - (used * root) * lax.rsqrt(jnp.maximum(mod, 0.1))
                    for m in range(2):
                        for part in range(2):
                            hi, lo = split(fars[m][HC * part:HC * part + HC] * fac)
                            r = H * part + j
                            hs[b, m, q, r:r + HC] = hi
                            hs[b, m, q, W + r:W + r + HC] = lo

                yield fars, factors
        for m in range(2):
            for j in range(0, H, HC):
                def backs(m=m, j=j):
                    out = []
                    for q in range(2):
                        t = tb[q]
                        out.append(lmul2(t, hs[b, m, q, :W], hs[b, m, q, W:]))
                    return out

                def columns(v, m=m, j=j):
                    for top in range(2):
                        x = v[0] + v[1] if top == 0 else v[0] - v[1]
                        for p in range(2):
                            hi, lo = split(cat1(x[:HC, H * p:H * p + H], x[HC:, H * p:H * p + H]))
                            r = H * top + j
                            ds[b, m, p, r:r + HC, :W] = hi
                            ds[b, m, p, r:r + HC, W:] = lo

                yield backs, columns
        for m in range(2):
            for j in (0, H):
                at = slice(j, j + H)

                def last(m=m, at=at):
                    return [rmul2(ds[b, m, p, at, :W], ds[b, m, p, at, W:], tb[2 + p]) for p in range(2)]

                def terms(d, m=m, at=at):
                    for h in range(2):
                        x = d[0] + d[1] if h == 0 else d[0] - d[1]
                        br, bi = x[:, :H], x[:, H:]
                        lanes = slice(H * h, H * h + H)
                        pr, pi = prv[0, m, at, lanes], prv[1, m, at, lanes]
                        xr, xi = patch[b, 0, at, lanes], patch[b, 1, at, lanes]
                        tr, ti = pr * br + pi * bi, pr * bi - pi * br
                        if m == 0:
                            term[b, 0, at, lanes], term[b, 1, at, lanes] = tr, ti
                        else:
                            term[b, 0, at, lanes] += tr
                            term[b, 1, at, lanes] += ti
                        pacc[0, m, at, lanes] += xr * br + xi * bi
                        pacc[1, m, at, lanes] += xr * bi - xi * br

                yield last, terms

    def pair(i, carry):
        slots = [i * NB + b for b in range(NB)]
        used = [jnp.where(s < live[0], 1.0, 0.0) for s in slots]
        for b in range(NB):
            roots(slots[b]).wait()
            fetch(slots[b], b)
        streams = [list(units(slots[b], b, used[b])) for b in range(NB)]
        todo = []
        for group in zip(*streams):
            for product, then in group:
                todo.append((then, product()))
                if len(todo) > LAG:
                    then, value = todo.pop(0)
                    then(value)
        for then, value in todo:
            then(value)
        for b in range(NB):
            deposit(slots[b], b)
        return carry

    pairs = lax.div(live[0] + NB - 1, NB)
    lax.fori_loop(0, pairs, pair, 0)

    def skip(s, carry):
        roots(s).wait()
        return carry

    lax.fori_loop(pairs * NB, 8, skip, 0)
    outs = [
        (acc.at[:, 512:768, 512:768], o_corner),
        (acc.at[:, 256:512, 512:768], o_rbot),
        (acc.at[:, 0:256, 512:768], o_rtop),
        (acc.at[:, 512:768, 0:512], o_below),
        (prv.at[1], o_other),
        (prv.at[0], o_mine),
        (cov.at[0, 0:512, 0:512], o_part.at[0]),
        (cov.at[1, 0:512, 0:512], o_part.at[1]),
    ]
    copies = [pltpu.make_async_copy(s, d, sems.at[i]) for i, (s, d) in enumerate(outs)]
    for c in copies[:4]:
        c.start()
    for kc in range(2):
        prv[kc] = pacc[lax.rem(anchor[2] + kc, 2)]
    for c in copies[4:6]:
        c.start()
    for c in range(2):
        cov[c, 0:512, 0:512] = cov[c, 0:512, 0:512] - 0.5 * acc[c, 0:512, 0:512]
        copies[6 + c].start()
    for c in copies:
        c.wait()


def main_call(offs, live, anchor, obj, right_top, right_bot, below, corner, probe, sq):
    any_ = pl.BlockSpec(memory_space=pl.ANY)
    smem = pl.BlockSpec(memory_space=pltpu.SMEM)
    S = lambda *s: jax.ShapeDtypeStruct(s, f32)
    return pl.pallas_call(
        main_kernel,
        out_shape=(S(2, 512, 512), S(2, 256, 256), S(2, 256, 256), S(2, 256, 256), S(2, 256, 512), S(2, 256, 256), S(2, 256, 256)),
        in_specs=[smem] * 3 + [any_] * 8,
        out_specs=[any_] * 7,
        scratch_shapes=[
            pltpu.VMEM((2, 768, 768), f32),
            pltpu.VMEM((2, 768, 768), f32),
            pltpu.VMEM((NB, 2, W, W), f32),
            pltpu.VMEM((2, 2, W, W), f32),
            pltpu.VMEM((2, 2, W, W), f32),
            pltpu.VMEM((8, W, W), f32),
            pltpu.VMEM((4, 2, W, W), bf16),
            pltpu.VMEM((NB, 2, 2, 2 * W, W), bf16),
            pltpu.VMEM((NB, 2, 2, 2 * W, W), bf16),
            pltpu.VMEM((NB, 2, 2, W, 2 * W), bf16),
            pltpu.VMEM((NB, 2, W, W), f32),
            pltpu.SemaphoreType.DMA((9,)),
            pltpu.SemaphoreType.DMA((8,)),
        ],
        compiler_params=pltpu.CompilerParams(vmem_limit_bytes=62 * 2**20),
        name="slots",
    )(offs, live, anchor, obj, right_top, right_bot, below, corner, probe, sq, jnp.asarray(make_tables()))


def prep_kernel(counts, pm, pmt, out):
    i = counts[0].astype(f32).astype(bf16)
    a = jnp.dot(pm[...], i, preferred_element_type=f32).astype(bf16)
    out[0] = jnp.sqrt(jnp.dot(a, pmt[...], preferred_element_type=f32))


def prep_call(counts):
    order = np.concatenate([np.arange(0, W, 2), np.arange(1, W, 2)])
    pm = np.zeros((W, W), np.float32)
    pm[np.arange(W), order] = 1.0
    full = pl.BlockSpec((W, W), lambda s: (0, 0))
    blk = pl.BlockSpec((1, W, W), lambda s: (s, 0, 0))
    return pl.pallas_call(
        prep_kernel,
        grid=(8,),
        out_shape=jax.ShapeDtypeStruct((8, W, W), f32),
        in_specs=[blk, full, full],
        out_specs=blk,
        name="roots",
    )(counts, jnp.asarray(pm.astype(ml_dtypes.bfloat16)), jnp.asarray(pm.T.astype(ml_dtypes.bfloat16)))


def moved(value, axes, pairs):
    return lax.ppermute(value, axes, pairs)


def finish_kernel(part, above, top, bot, out, upper, lower, ab, tp, bt, sems):
    ins, outs = [], []
    for c in range(2):
        moves = [
            (part.at[c, 0:W], upper.at[c]),
            (above.at[c], ab.at[c]),
            (top.at[c], tp.at[c]),
            (part.at[c, W:, 0:W], lower.at[c]),
            (bot.at[c], bt.at[c]),
        ]
        ins.append([pltpu.make_async_copy(s, d, sems.at[c, i]) for i, (s, d) in enumerate(moves)])
        moves = [(upper.at[c], out.at[c, 0:W]), (lower.at[c], out.at[c, W:, 0:W])]
        outs.append([pltpu.make_async_copy(s, d, sems.at[c, 5 + i]) for i, (s, d) in enumerate(moves)])
    for copy in ins[0] + ins[1]:
        copy.start()
    for c in range(2):
        for copy in ins[c]:
            copy.wait()
        upper[c, :, :W] = upper[c, :, :W] - 0.5 * (ab[c, :, :W] + tp[c])
        upper[c, :, W:] = upper[c, :, W:] - 0.5 * ab[c, :, W:]
        lower[c] = lower[c] - 0.5 * bt[c]
        for copy in outs[c]:
            copy.start()
    for copy in outs[0] + outs[1]:
        copy.wait()


def finish_call(part, above, top, bot):
    any_ = pl.BlockSpec(memory_space=pl.ANY)
    return pl.pallas_call(
        finish_kernel,
        out_shape=jax.ShapeDtypeStruct((2, 512, 512), f32),
        in_specs=[any_] * 4,
        out_specs=any_,
        scratch_shapes=[
            pltpu.VMEM((2, W, 512), f32),
            pltpu.VMEM((2, W, W), f32),
            pltpu.VMEM((2, W, 512), f32),
            pltpu.VMEM((2, W, W), f32),
            pltpu.VMEM((2, W, W), f32),
            pltpu.SemaphoreType.DMA((2, 7)),
        ],
        input_output_aliases={0: 0},
        compiler_params=pltpu.CompilerParams(vmem_limit_bytes=8 * 2**20),
        name="finish",
    )(part, above, top, bot)


def swap_cores(value):
    return lax.ppermute(value, "core", [(0, 1), (1, 0)])


def sum_everywhere(value, axis):
    got = [lax.ppermute(value, axis, [(i, (i + k) % 4) for i in range(4)]) for k in (2, 1, 3)]
    return (value + got[0]) + (got[1] + got[2])


def probe_kernel(step, place, probe, mine, rest, out):
    for kc in range(2):
        at = pl.multiple_of(lax.rem(place[2] + kc, 2) * 512, 512)
        out[pl.ds(at, 512), :] = probe[pl.ds(at, 512), :] - step * (mine, rest)[kc][...]


def shards(object_planes, probe_planes, offsets, photon_counts, live_counts):
    n_row = lax.axis_size("y") * lax.axis_size("core")
    n_col = lax.axis_size("x") * lax.axis_size("z")
    rows, cols = ("y", "core"), ("x", "z")
    up = [(i, i - 1) for i in range(1, n_row)]
    down = [(i - 1, i) for i in range(1, n_row)]
    to_left = [(i, i - 1) for i in range(1, n_col)]
    to_right = [(i - 1, i) for i in range(1, n_col)]

    right_top = lax.ppermute(object_planes[:, :W, :W], cols, to_left)
    below = lax.ppermute(object_planes[:, :W, :], rows, up)
    right_bot = lax.ppermute(object_planes[:, W:, :W], cols, to_left)
    roots = prep_call(photon_counts)
    right_top, roots = lax.optimization_barrier((right_top, roots))
    corner = lax.ppermute(right_top, rows, up)
    place = jnp.stack(
        [lax.axis_index(rows) * 512, lax.axis_index(cols) * 512] + [lax.axis_index(a) for a in ("core",)]
    ).astype(jnp.int32)
    part, g_top, g_bot, g_corner, g_below, mine, other = main_call(
        offsets, live_counts.reshape(1), place, object_planes, right_top, right_bot, below, corner, probe_planes, roots
    )
    corner_in = lax.ppermute(g_corner, rows, down)
    bot_in = lax.ppermute(g_bot, cols, to_right)
    above_in = lax.ppermute(g_below, rows, down)
    half = (mine + swap_cores(other)).reshape(16, 32, W)
    top_in = lax.ppermute(g_top + corner_in, cols, to_right)
    plane = ("y", "x")
    piece = lax.all_to_all(half, plane, 0, 0).sum(0)
    piece, bot_in = lax.optimization_barrier((piece, bot_in))
    piece = sum_everywhere(piece, "z")
    piece, top_in = lax.optimization_barrier((piece, top_in))
    new_object = finish_call(part, above_in, top_in, bot_in)
    half = lax.all_to_all(jnp.broadcast_to(piece[None], half.shape), plane, 0, 0).reshape(512, W)
    rest = swap_cores(half)
    smem, vmem = pl.BlockSpec(memory_space=pltpu.SMEM), pl.BlockSpec(memory_space=pltpu.VMEM)
    step = 1.0 / math.sqrt(offsets.shape[0] * n_row * n_col)
    new_probe = pl.pallas_call(
        functools.partial(probe_kernel, step),
        out_shape=jax.ShapeDtypeStruct((1024, W), f32),
        in_specs=[smem] + [vmem] * 3,
        out_specs=vmem,
        compiler_params=pltpu.CompilerParams(vmem_limit_bytes=8 * 2**20),
        name="probe",
    )(place, probe_planes.reshape(1024, W), half, rest)
    return new_object, new_probe.reshape(probe_planes.shape)


def solution(mesh):
    split = jax.sharding.Mesh(
        mesh.devices.reshape(mesh.shape["row"] // 2, 2, mesh.shape["col"] // 4, 4), ("y", "core", "x", "z")
    )
    rows, cols = ("y", "core"), ("x", "z")
    in_specs = (
        P(None, rows, cols),
        P(),
        P(rows + cols, None),
        P(rows + cols, None, None),
        P(rows, cols),
    )
    out_specs = (P(None, rows, cols), P())
    return jax.shard_map(shards, mesh=split, in_specs=in_specs, out_specs=out_specs, check_vma=False)
```

```python
import functools
import math

import ml_dtypes
import numpy as np
import jax
import jax.numpy as jnp
from jax import lax
from jax.experimental import pallas as pl
from jax.experimental.pallas import tpu as pltpu
from jax.sharding import PartitionSpec as P

f32, bf16 = jnp.float32, jnp.bfloat16
W = 256
H = 128
HC = 128
NB = 2
LAG = 0


def make_tables():
    b = np.arange(H)[:, None]
    q = np.arange(H)[None, :]
    right = []
    for p in (0, 1):
        ang = 2.0 * np.pi * (((2 * q + p) * b) % W) / W
        c, s = np.cos(ang) / 16.0, np.sin(ang) / 16.0
        right.append(np.block([[c, -s], [s, c]]))
    out = []
    for t in (right[0], right[1], right[0].T, right[1].T):
        hi = t.astype(np.float32).astype(ml_dtypes.bfloat16)
        lo = (t - hi.astype(np.float64)).astype(np.float32).astype(ml_dtypes.bfloat16)
        out.append(np.stack([hi, lo]))
    return np.stack(out)


def split(x):
    hi = x.astype(bf16)
    lo = (x - hi.astype(f32)).astype(bf16)
    return hi, lo


def rmul2(hi, lo, t):
    return jnp.dot(jnp.concatenate([hi, lo, hi], 1), jnp.concatenate([t[0], t[0], t[1]], 0), preferred_element_type=f32)


def rmul(x, t):
    hi, lo = split(x)
    return rmul2(hi, lo, t)


def lmul2(t, hi, lo):
    return jnp.dot(jnp.concatenate([t[0], t[0], t[1]], 1), jnp.concatenate([hi, lo, hi], 0), preferred_element_type=f32)


def cat1(a, b):
    return jnp.concatenate([a, b], 1)


def cat0(a, b):
    return jnp.concatenate([a, b], 0)


def main_kernel(offs, live, anchor, obj, right_top, right_bot, below, corner, probe, sq, tables,
                o_part, o_rtop, o_rbot, o_corner, o_below, o_mine, o_other,
                cov, acc, patch, pacc, prv, sqv, tb, gs, hs, ds, term, sems, sqsems):
    ins = [
        (obj, cov.at[:, 0:512, 0:512]),
        (right_top, cov.at[:, 0:256, 512:768]),
        (right_bot, cov.at[:, 256:512, 512:768]),
        (below, cov.at[:, 512:768, 0:512]),
        (corner, cov.at[:, 512:768, 512:768]),
        (probe, prv),
        (tables, tb),
    ]
    copies = [pltpu.make_async_copy(s, d, sems.at[i]) for i, (s, d) in enumerate(ins)]
    roots = lambda s: pltpu.make_async_copy(sq.at[s], sqv.at[s], sqsems.at[s])
    for c in copies:
        c.start()
    for s in range(8):
        roots(s).start()
    acc[...] = jnp.zeros_like(acc)
    pacc[...] = jnp.zeros_like(pacc)
    for c in copies:
        c.wait()
    lane = lax.broadcasted_iota(jnp.int32, (W, H), 1)
    sub9 = lax.broadcasted_iota(jnp.int32, (33, 8, H), 1)
    sub = lax.broadcasted_iota(jnp.int32, (32, 8, H), 1)

    def place_of(s):
        top = offs[s, 0] - anchor[0]
        left = offs[s, 1] - anchor[1]
        la = pl.multiple_of(lax.div(left, 128) * 128, 128)
        ta = pl.multiple_of(lax.div(top, 8) * 8, 8)
        return ta, lax.rem(top, 8), la, lax.rem(left, 128)

    def fetch(s, b):
        ta, rs, la, ls = place_of(s)
        back = lax.rem(128 - ls, 128)
        rback = lax.rem(8 - rs, 8)
        for c in range(2):
            t = []
            for k in range(3):
                v = cov[c, pl.ds(ta, W + 8), pl.ds(la + 128 * k, H)]
                v = pltpu.roll(pltpu.roll(v, back, 1).reshape(33, 8, H), rback, 1)
                t.append(jnp.where(sub < 8 - rs, v[:32], v[1:]).reshape(W, H))
            for k in range(2):
                patch[b, c, :, 128 * k:128 * k + 128] = jnp.where(lane < 128 - ls, t[k], t[k + 1])

    def deposit(s, b):
        ta, rs, la, ls = place_of(s)
        for c in range(2):
            r = [pltpu.roll(term[b, c, :, 128 * k:128 * k + 128], ls, 1) for k in range(2)]
            z = jnp.zeros_like(r[0])
            keep = lane >= ls
            parts = [jnp.where(keep, r[0], z), jnp.where(keep, r[1], r[0]), jnp.where(keep, z, r[1])]
            for k in range(3):
                v = pltpu.roll(parts[k].reshape(32, 8, H), rs, 1)
                z8 = jnp.zeros((1, 8, H), f32)
                v = jnp.where(sub9 >= rs, jnp.concatenate([v, z8], 0), jnp.concatenate([z8, v], 0))
                acc[c, pl.ds(ta, W + 8), pl.ds(la + 128 * k, H)] += v.reshape(W + 8, H)

    def units(s, b, used):
        for m in range(2):
            for j in range(0, H, HC):
                def waves(m=m, j=j):
                    at = [slice(j, j + HC), slice(H + j, H + j + HC)]
                    get = lambda ref, *i: cat0(ref[(*i, at[0])], ref[(*i, at[1])])
                    pr, pi = get(prv, 0, m), get(prv, 1, m)
                    xr, xi = get(patch, b, 0), get(patch, b, 1)
                    wr = pr * xr - pi * xi
                    wi = pr * xi + pi * xr
                    e = cat1(wr[:, :H] + wr[:, H:], wi[:, :H] + wi[:, H:])
                    o = cat1(wr[:, :H] - wr[:, H:], wi[:, :H] - wi[:, H:])
                    return rmul(e, tb[0]), rmul(o, tb[1])

                def rows(ys, m=m, j=j):
                    for p in range(2):
                        lanes = slice(H * p, H * p + H)
                        y = ys[p]
                        for q in range(2):
                            f = y[:HC] + y[HC:] if q == 0 else y[:HC] - y[HC:]
                            hi, lo = split(f)
                            for part in range(2):
                                r = H * part + j
                                gs[b, m, q, r:r + HC, lanes] = hi[:, H * part:H * part + H]
                                gs[b, m, q, W + r:W + r + HC, lanes] = lo[:, H * part:H * part + H]

                yield waves, rows
        for q in range(2):
            for j in range(0, H, HC):
                def fars(q=q, j=j):
                    t = tb[2 + q]
                    return [lmul2(t, gs[b, m, q, :W], gs[b, m, q, W:]) for m in range(2)]

                def factors(fars, q=q, j=j):
                    mod = sum(a[:HC] * a[:HC] + a[HC:] * a[HC:] for a in fars)
                    root = sqv[s, H * q + j:H * q + j + HC, :]
                    fac = used - (used * root) * lax.rsqrt(jnp.maximum(mod, 0.1))
                    for m in range(2):
                        for part in range(2):
                            hi, lo = split(fars[m][HC * part:HC * part + HC] * fac)
                            r = H * part + j
                            hs[b, m, q, r:r + HC] = hi
                            hs[b, m, q, W + r:W + r + HC] = lo

                yield fars, factors
        for m in range(2):
            for j in range(0, H, HC):
                def backs(m=m, j=j):
                    out = []
                    for q in range(2):
                        t = tb[q]
                        out.append(lmul2(t, hs[b, m, q, :W], hs[b, m, q, W:]))
                    return out

                def columns(v, m=m, j=j):
                    for top in range(2):
                        x = v[0] + v[1] if top == 0 else v[0] - v[1]
                        for p in range(2):
                            hi, lo = split(cat1(x[:HC, H * p:H * p + H], x[HC:, H * p:H * p + H]))
                            r = H * top + j
                            ds[b, m, p, r:r + HC, :W] = hi
                            ds[b, m, p, r:r + HC, W:] = lo

                yield backs, columns
        for m in range(2):
            for j in (0, H):
                at = slice(j, j + H)

                def last(m=m, at=at):
                    return [rmul2(ds[b, m, p, at, :W], ds[b, m, p, at, W:], tb[2 + p]) for p in range(2)]

                def terms(d, m=m, at=at):
                    for h in range(2):
                        x = d[0] + d[1] if h == 0 else d[0] - d[1]
                        br, bi = x[:, :H], x[:, H:]
                        lanes = slice(H * h, H * h + H)
                        pr, pi = prv[0, m, at, lanes], prv[1, m, at, lanes]
                        xr, xi = patch[b, 0, at, lanes], patch[b, 1, at, lanes]
                        tr, ti = pr * br + pi * bi, pr * bi - pi * br
                        if m == 0:
                            term[b, 0, at, lanes], term[b, 1, at, lanes] = tr, ti
                        else:
                            term[b, 0, at, lanes] += tr
                            term[b, 1, at, lanes] += ti
                        pacc[0, m, at, lanes] += xr * br + xi * bi
                        pacc[1, m, at, lanes] += xr * bi - xi * br

                yield last, terms

    def pair(i, carry):
        slots = [i * NB + b for b in range(NB)]
        used = [jnp.where(s < live[0], 1.0, 0.0) for s in slots]
        for b in range(NB):
            roots(slots[b]).wait()
            fetch(slots[b], b)
        streams = [list(units(slots[b], b, used[b])) for b in range(NB)]
        todo = []
        for group in zip(*streams):
            for product, then in group:
                todo.append((then, product()))
                if len(todo) > LAG:
                    then, value = todo.pop(0)
                    then(value)
        for then, value in todo:
            then(value)
        for b in range(NB):
            deposit(slots[b], b)
        return carry

    pairs = lax.div(live[0] + NB - 1, NB)
    lax.fori_loop(0, pairs, pair, 0)

    def skip(s, carry):
        roots(s).wait()
        return carry

    lax.fori_loop(pairs * NB, 8, skip, 0)
    outs = [
        (acc.at[:, 512:768, 512:768], o_corner),
        (acc.at[:, 256:512, 512:768], o_rbot),
        (acc.at[:, 0:256, 512:768], o_rtop),
        (acc.at[:, 512:768, 0:512], o_below),
        (prv.at[1], o_other),
        (prv.at[0], o_mine),
        (cov.at[0, 0:512, 0:512], o_part.at[0]),
        (cov.at[1, 0:512, 0:512], o_part.at[1]),
    ]
    copies = [pltpu.make_async_copy(s, d, sems.at[i]) for i, (s, d) in enumerate(outs)]
    for c in copies[:4]:
        c.start()
    for kc in range(2):
        prv[kc] = pacc[lax.rem(anchor[2] + kc, 2)]
    for c in copies[4:6]:
        c.start()
    for c in range(2):
        cov[c, 0:512, 0:512] = cov[c, 0:512, 0:512] - 0.5 * acc[c, 0:512, 0:512]
        copies[6 + c].start()
    for c in copies:
        c.wait()


def main_call(offs, live, anchor, obj, right_top, right_bot, below, corner, probe, sq):
    any_ = pl.BlockSpec(memory_space=pl.ANY)
    smem = pl.BlockSpec(memory_space=pltpu.SMEM)
    S = lambda *s: jax.ShapeDtypeStruct(s, f32)
    return pl.pallas_call(
        main_kernel,
        out_shape=(S(2, 512, 512), S(2, 256, 256), S(2, 256, 256), S(2, 256, 256), S(2, 256, 512), S(2, 256, 256), S(2, 256, 256)),
        in_specs=[smem] * 3 + [any_] * 8,
        out_specs=[any_] * 7,
        scratch_shapes=[
            pltpu.VMEM((2, 768, 768), f32),
            pltpu.VMEM((2, 768, 768), f32),
            pltpu.VMEM((NB, 2, W, W), f32),
            pltpu.VMEM((2, 2, W, W), f32),
            pltpu.VMEM((2, 2, W, W), f32),
            pltpu.VMEM((8, W, W), f32),
            pltpu.VMEM((4, 2, W, W), bf16),
            pltpu.VMEM((NB, 2, 2, 2 * W, W), bf16),
            pltpu.VMEM((NB, 2, 2, 2 * W, W), bf16),
            pltpu.VMEM((NB, 2, 2, W, 2 * W), bf16),
            pltpu.VMEM((NB, 2, W, W), f32),
            pltpu.SemaphoreType.DMA((9,)),
            pltpu.SemaphoreType.DMA((8,)),
        ],
        compiler_params=pltpu.CompilerParams(vmem_limit_bytes=62 * 2**20),
        name="slots",
    )(offs, live, anchor, obj, right_top, right_bot, below, corner, probe, sq, jnp.asarray(make_tables()))


def prep_kernel(counts, pm, pmt, out):
    i = counts[0].astype(f32).astype(bf16)
    a = jnp.dot(pm[...], i, preferred_element_type=f32).astype(bf16)
    out[0] = jnp.sqrt(jnp.dot(a, pmt[...], preferred_element_type=f32))


def prep_call(counts):
    order = np.concatenate([np.arange(0, W, 2), np.arange(1, W, 2)])
    pm = np.zeros((W, W), np.float32)
    pm[np.arange(W), order] = 1.0
    full = pl.BlockSpec((W, W), lambda s: (0, 0))
    blk = pl.BlockSpec((1, W, W), lambda s: (s, 0, 0))
    return pl.pallas_call(
        prep_kernel,
        grid=(8,),
        out_shape=jax.ShapeDtypeStruct((8, W, W), f32),
        in_specs=[blk, full, full],
        out_specs=blk,
        name="roots",
    )(counts, jnp.asarray(pm.astype(ml_dtypes.bfloat16)), jnp.asarray(pm.T.astype(ml_dtypes.bfloat16)))


def moved(value, axes, pairs):
    return lax.ppermute(value, axes, pairs)


def finish_kernel(part, above, top, bot, out, upper, lower, ab, tp, bt, sems):
    ins, outs = [], []
    for c in range(2):
        moves = [
            (part.at[c, 0:W], upper.at[c]),
            (above.at[c], ab.at[c]),
            (top.at[c], tp.at[c]),
            (part.at[c, W:, 0:W], lower.at[c]),
            (bot.at[c], bt.at[c]),
        ]
        ins.append([pltpu.make_async_copy(s, d, sems.at[c, i]) for i, (s, d) in enumerate(moves)])
        moves = [(upper.at[c], out.at[c, 0:W]), (lower.at[c], out.at[c, W:, 0:W])]
        outs.append([pltpu.make_async_copy(s, d, sems.at[c, 5 + i]) for i, (s, d) in enumerate(moves)])
    for copy in ins[0] + ins[1]:
        copy.start()
    for c in range(2):
        for copy in ins[c]:
            copy.wait()
        upper[c, :, :W] = upper[c, :, :W] - 0.5 * (ab[c, :, :W] + tp[c])
        upper[c, :, W:] = upper[c, :, W:] - 0.5 * ab[c, :, W:]
        lower[c] = lower[c] - 0.5 * bt[c]
        for copy in outs[c]:
            copy.start()
    for copy in outs[0] + outs[1]:
        copy.wait()


def finish_call(part, above, top, bot):
    any_ = pl.BlockSpec(memory_space=pl.ANY)
    return pl.pallas_call(
        finish_kernel,
        out_shape=jax.ShapeDtypeStruct((2, 512, 512), f32),
        in_specs=[any_] * 4,
        out_specs=any_,
        scratch_shapes=[
            pltpu.VMEM((2, W, 512), f32),
            pltpu.VMEM((2, W, W), f32),
            pltpu.VMEM((2, W, 512), f32),
            pltpu.VMEM((2, W, W), f32),
            pltpu.VMEM((2, W, W), f32),
            pltpu.SemaphoreType.DMA((2, 7)),
        ],
        input_output_aliases={0: 0},
        compiler_params=pltpu.CompilerParams(vmem_limit_bytes=8 * 2**20),
        name="finish",
    )(part, above, top, bot)


def edges_kernel(obj, o_top, o_bot, o_below, sems):
    moves = [(obj.at[:, 0:W, 0:W], o_top), (obj.at[:, W:, 0:W], o_bot), (obj.at[:, 0:W], o_below)]
    copies = [pltpu.make_async_copy(s, d, sems.at[i]) for i, (s, d) in enumerate(moves)]
    for copy in copies:
        copy.start()
    for copy in copies:
        copy.wait()


def edges_call(obj):
    any_ = pl.BlockSpec(memory_space=pl.ANY)
    S = lambda *s: jax.ShapeDtypeStruct(s, f32)
    return pl.pallas_call(
        edges_kernel,
        out_shape=(S(2, W, W), S(2, W, W), S(2, W, 512)),
        in_specs=[any_],
        out_specs=[any_] * 3,
        scratch_shapes=[pltpu.SemaphoreType.DMA((3,))],
        compiler_params=pltpu.CompilerParams(vmem_limit_bytes=62 * 2**20),
        name="edges",
    )(obj)


def swap_cores(value):
    return lax.ppermute(value, "core", [(0, 1), (1, 0)])


def sum_everywhere(value, axis):
    got = [lax.ppermute(value, axis, [(i, (i + k) % 4) for i in range(4)]) for k in (2, 1, 3)]
    return (value + got[0]) + (got[1] + got[2])


def probe_kernel(step, place, probe, mine, rest, out):
    for kc in range(2):
        at = pl.multiple_of(lax.rem(place[2] + kc, 2) * 512, 512)
        out[pl.ds(at, 512), :] = probe[pl.ds(at, 512), :] - step * (mine, rest)[kc][...]


def shards(object_planes, probe_planes, offsets, photon_counts, live_counts):
    n_row = lax.axis_size("y") * lax.axis_size("core")
    n_col = lax.axis_size("x") * lax.axis_size("z")
    rows, cols = ("y", "core"), ("x", "z")
    up = [(i, i - 1) for i in range(1, n_row)]
    down = [(i - 1, i) for i in range(1, n_row)]
    to_left = [(i, i - 1) for i in range(1, n_col)]
    to_right = [(i - 1, i) for i in range(1, n_col)]

    edge_top, edge_bot, edge_below = edges_call(object_planes)
    right_top = lax.ppermute(edge_top, cols, to_left)
    below = lax.ppermute(edge_below, rows, up)
    right_bot = lax.ppermute(edge_bot, cols, to_left)
    roots = prep_call(photon_counts)
    right_top, roots = lax.optimization_barrier((right_top, roots))
    corner = lax.ppermute(right_top, rows, up)
    place = jnp.stack(
        [lax.axis_index(rows) * 512, lax.axis_index(cols) * 512] + [lax.axis_index(a) for a in ("core",)]
    ).astype(jnp.int32)
    part, g_top, g_bot, g_corner, g_below, mine, other = main_call(
        offsets, live_counts.reshape(1), place, object_planes, right_top, right_bot, below, corner, probe_planes, roots
    )
    corner_in = lax.ppermute(g_corner, rows, down)
    bot_in = lax.ppermute(g_bot, cols, to_right)
    above_in = lax.ppermute(g_below, rows, down)
    half = (mine + swap_cores(other)).reshape(16, 32, W)
    top_in = lax.ppermute(g_top + corner_in, cols, to_right)
    plane = ("y", "x")
    piece = lax.all_to_all(half, plane, 0, 0).sum(0)
    piece, bot_in = lax.optimization_barrier((piece, bot_in))
    piece = sum_everywhere(piece, "z")
    half = lax.all_to_all(jnp.broadcast_to(piece[None], half.shape), plane, 0, 0).reshape(512, W)
    half, top_in = lax.optimization_barrier((half, top_in))
    rest = swap_cores(half)
    new_object = finish_call(part, above_in, top_in, bot_in)
    smem, vmem = pl.BlockSpec(memory_space=pltpu.SMEM), pl.BlockSpec(memory_space=pltpu.VMEM)
    step = 1.0 / math.sqrt(offsets.shape[0] * n_row * n_col)
    new_probe = pl.pallas_call(
        functools.partial(probe_kernel, step),
        out_shape=jax.ShapeDtypeStruct((1024, W), f32),
        in_specs=[smem] + [vmem] * 3,
        out_specs=vmem,
        compiler_params=pltpu.CompilerParams(vmem_limit_bytes=8 * 2**20),
        name="probe",
    )(place, probe_planes.reshape(1024, W), half, rest)
    return new_object, new_probe.reshape(probe_planes.shape)


def solution(mesh):
    split = jax.sharding.Mesh(
        mesh.devices.reshape(mesh.shape["row"] // 2, 2, mesh.shape["col"] // 4, 4), ("y", "core", "x", "z")
    )
    rows, cols = ("y", "core"), ("x", "z")
    in_specs = (
        P(None, rows, cols),
        P(),
        P(rows + cols, None),
        P(rows + cols, None, None),
        P(rows, cols),
    )
    out_specs = (P(None, rows, cols), P())
    return jax.shard_map(shards, mesh=split, in_specs=in_specs, out_specs=out_specs, check_vma=False)
```

```python
import functools
import math

import ml_dtypes
import numpy as np
import jax
import jax.numpy as jnp
from jax import lax
from jax.experimental import pallas as pl
from jax.experimental.pallas import tpu as pltpu
from jax.sharding import PartitionSpec as P

f32, bf16 = jnp.float32, jnp.bfloat16
W = 256
H = 128
HC = 128
NB = 2
LAG = 0


def make_tables():
    b = np.arange(H)[:, None]
    q = np.arange(H)[None, :]
    right = []
    for p in (0, 1):
        ang = 2.0 * np.pi * (((2 * q + p) * b) % W) / W
        c, s = np.cos(ang) / 16.0, np.sin(ang) / 16.0
        right.append(np.block([[c, -s], [s, c]]))
    out = []
    for t in (right[0], right[1], right[0].T, right[1].T):
        hi = t.astype(np.float32).astype(ml_dtypes.bfloat16)
        lo = (t - hi.astype(np.float64)).astype(np.float32).astype(ml_dtypes.bfloat16)
        out.append(np.stack([hi, lo]))
    return np.stack(out)


def split(x):
    hi = x.astype(bf16)
    lo = (x - hi.astype(f32)).astype(bf16)
    return hi, lo


def rmul2(hi, lo, t):
    return jnp.dot(jnp.concatenate([hi, lo, hi], 1), jnp.concatenate([t[0], t[0], t[1]], 0), preferred_element_type=f32)


def rmul(x, t):
    hi, lo = split(x)
    return rmul2(hi, lo, t)


def lmul2(t, hi, lo):
    return jnp.dot(jnp.concatenate([t[0], t[0], t[1]], 1), jnp.concatenate([hi, lo, hi], 0), preferred_element_type=f32)


def cat1(a, b):
    return jnp.concatenate([a, b], 1)


def cat0(a, b):
    return jnp.concatenate([a, b], 0)


def main_kernel(offs, live, anchor, obj, right_top, right_bot, below, corner, probe, sq, tables,
                o_part, o_rtop, o_rbot, o_corner, o_below, o_mine, o_other,
                cov, acc, patch, pacc, prv, sqv, tb, gs, hs, ds, term, sems, sqsems):
    ins = [
        (obj, cov.at[:, 0:512, 0:512]),
        (right_top, cov.at[:, 0:256, 512:768]),
        (right_bot, cov.at[:, 256:512, 512:768]),
        (below, cov.at[:, 512:768, 0:512]),
        (corner, cov.at[:, 512:768, 512:768]),
        (probe, prv),
        (tables, tb),
    ]
    copies = [pltpu.make_async_copy(s, d, sems.at[i]) for i, (s, d) in enumerate(ins)]
    roots = lambda s: pltpu.make_async_copy(sq.at[s], sqv.at[s], sqsems.at[s])
    for c in copies:
        c.start()
    for s in range(8):
        roots(s).start()
    acc[...] = jnp.zeros_like(acc)
    pacc[...] = jnp.zeros_like(pacc)
    for c in copies:
        c.wait()
    lane = lax.broadcasted_iota(jnp.int32, (W, H), 1)
    sub9 = lax.broadcasted_iota(jnp.int32, (33, 8, H), 1)
    sub = lax.broadcasted_iota(jnp.int32, (32, 8, H), 1)

    def place_of(s):
        top = offs[s, 0] - anchor[0]
        left = offs[s, 1] - anchor[1]
        la = pl.multiple_of(lax.div(left, 128) * 128, 128)
        ta = pl.multiple_of(lax.div(top, 8) * 8, 8)
        return ta, lax.rem(top, 8), la, lax.rem(left, 128)

    def fetch(s, b):
        ta, rs, la, ls = place_of(s)
        back = lax.rem(128 - ls, 128)
        rback = lax.rem(8 - rs, 8)
        for c in range(2):
            t = []
            for k in range(3):
                v = cov[c, pl.ds(ta, W + 8), pl.ds(la + 128 * k, H)]
                v = pltpu.roll(pltpu.roll(v, back, 1).reshape(33, 8, H), rback, 1)
                t.append(jnp.where(sub < 8 - rs, v[:32], v[1:]).reshape(W, H))
            for k in range(2):
                patch[b, c, :, 128 * k:128 * k + 128] = jnp.where(lane < 128 - ls, t[k], t[k + 1])

    def deposit(s, b):
        ta, rs, la, ls = place_of(s)
        for c in range(2):
            r = [pltpu.roll(term[b, c, :, 128 * k:128 * k + 128], ls, 1) for k in range(2)]
            z = jnp.zeros_like(r[0])
            keep = lane >= ls
            parts = [jnp.where(keep, r[0], z), jnp.where(keep, r[1], r[0]), jnp.where(keep, z, r[1])]
            for k in range(3):
                v = pltpu.roll(parts[k].reshape(32, 8, H), rs, 1)
                z8 = jnp.zeros((1, 8, H), f32)
                v = jnp.where(sub9 >= rs, jnp.concatenate([v, z8], 0), jnp.concatenate([z8, v], 0))
                acc[c, pl.ds(ta, W + 8), pl.ds(la + 128 * k, H)] += v.reshape(W + 8, H)

    def units(s, b, used):
        for m in range(2):
            for j in range(0, H, HC):
                def waves(m=m, j=j):
                    at = [slice(j, j + HC), slice(H + j, H + j + HC)]
                    get = lambda ref, *i: cat0(ref[(*i, at[0])], ref[(*i, at[1])])
                    pr, pi = get(prv, 0, m), get(prv, 1, m)
                    xr, xi = get(patch, b, 0), get(patch, b, 1)
                    wr = pr * xr - pi * xi
                    wi = pr * xi + pi * xr
                    e = cat1(wr[:, :H] + wr[:, H:], wi[:, :H] + wi[:, H:])
                    o = cat1(wr[:, :H] - wr[:, H:], wi[:, :H] - wi[:, H:])
                    return rmul(e, tb[0]), rmul(o, tb[1])

                def rows(ys, m=m, j=j):
                    for p in range(2):
                        lanes = slice(H * p, H * p + H)
                        y = ys[p]
                        for q in range(2):
                            f = y[:HC] + y[HC:] if q == 0 else y[:HC] - y[HC:]
                            hi, lo = split(f)
                            for part in range(2):
                                r = H * part + j
                                gs[b, m, q, r:r + HC, lanes] = hi[:, H * part:H * part + H]
                                gs[b, m, q, W + r:W + r + HC, lanes] = lo[:, H * part:H * part + H]

                yield waves, rows
        for q in range(2):
            for j in range(0, H, HC):
                def fars(q=q, j=j):
                    t = tb[2 + q]
                    return [lmul2(t, gs[b, m, q, :W], gs[b, m, q, W:]) for m in range(2)]

                def factors(fars, q=q, j=j):
                    mod = sum(a[:HC] * a[:HC] + a[HC:] * a[HC:] for a in fars)
                    root = sqv[s, H * q + j:H * q + j + HC, :]
                    fac = used - (used * root) * lax.rsqrt(jnp.maximum(mod, 0.1))
                    for m in range(2):
                        for part in range(2):
                            hi, lo = split(fars[m][HC * part:HC * part + HC] * fac)
                            r = H * part + j
                            hs[b, m, q, r:r + HC] = hi
                            hs[b, m, q, W + r:W + r + HC] = lo

                yield fars, factors
        for m in range(2):
            for j in range(0, H, HC):
                def backs(m=m, j=j):
                    out = []
                    for q in range(2):
                        t = tb[q]
                        out.append(lmul2(t, hs[b, m, q, :W], hs[b, m, q, W:]))
                    return out

                def columns(v, m=m, j=j):
                    for top in range(2):
                        x = v[0] + v[1] if top == 0 else v[0] - v[1]
                        for p in range(2):
                            hi, lo = split(cat1(x[:HC, H * p:H * p + H], x[HC:, H * p:H * p + H]))
                            r = H * top + j
                            ds[b, m, p, r:r + HC, :W] = hi
                            ds[b, m, p, r:r + HC, W:] = lo

                yield backs, columns
        for m in range(2):
            for j in (0, H):
                at = slice(j, j + H)

                def last(m=m, at=at):
                    return [rmul2(ds[b, m, p, at, :W], ds[b, m, p, at, W:], tb[2 + p]) for p in range(2)]

                def terms(d, m=m, at=at):
                    for h in range(2):
                        x = d[0] + d[1] if h == 0 else d[0] - d[1]
                        br, bi = x[:, :H], x[:, H:]
                        lanes = slice(H * h, H * h + H)
                        pr, pi = prv[0, m, at, lanes], prv[1, m, at, lanes]
                        xr, xi = patch[b, 0, at, lanes], patch[b, 1, at, lanes]
                        tr, ti = pr * br + pi * bi, pr * bi - pi * br
                        if m == 0:
                            term[b, 0, at, lanes], term[b, 1, at, lanes] = tr, ti
                        else:
                            term[b, 0, at, lanes] += tr
                            term[b, 1, at, lanes] += ti
                        pacc[0, m, at, lanes] += xr * br + xi * bi
                        pacc[1, m, at, lanes] += xr * bi - xi * br

                yield last, terms

    def pair(i, carry):
        slots = [i * NB + b for b in range(NB)]
        used = [jnp.where(s < live[0], 1.0, 0.0) for s in slots]
        for b in range(NB):
            roots(slots[b]).wait()
            fetch(slots[b], b)
        streams = [list(units(slots[b], b, used[b])) for b in range(NB)]
        todo = []
        for group in zip(*streams):
            for product, then in group:
                todo.append((then, product()))
                if len(todo) > LAG:
                    then, value = todo.pop(0)
                    then(value)
        for then, value in todo:
            then(value)
        for b in range(NB):
            deposit(slots[b], b)
        return carry

    pairs = lax.div(live[0] + NB - 1, NB)
    lax.fori_loop(0, pairs, pair, 0)

    def skip(s, carry):
        roots(s).wait()
        return carry

    lax.fori_loop(pairs * NB, 8, skip, 0)
    outs = [
        (acc.at[:, 512:768, 512:768], o_corner),
        (acc.at[:, 256:512, 512:768], o_rbot),
        (acc.at[:, 0:256, 512:768], o_rtop),
        (acc.at[:, 512:768, 0:512], o_below),
        (prv.at[1], o_other),
        (prv.at[0], o_mine),
        (cov.at[0, 0:512, 0:512], o_part.at[0]),
        (cov.at[1, 0:512, 0:512], o_part.at[1]),
    ]
    copies = [pltpu.make_async_copy(s, d, sems.at[i]) for i, (s, d) in enumerate(outs)]
    for c in copies[:4]:
        c.start()
    for kc in range(2):
        prv[kc] = pacc[lax.rem(anchor[2] + kc, 2)]
    for c in copies[4:6]:
        c.start()
    for c in range(2):
        cov[c, 0:512, 0:512] = cov[c, 0:512, 0:512] - 0.5 * acc[c, 0:512, 0:512]
        copies[6 + c].start()
    for c in copies:
        c.wait()


def main_call(offs, live, anchor, obj, right_top, right_bot, below, corner, probe, sq):
    any_ = pl.BlockSpec(memory_space=pl.ANY)
    smem = pl.BlockSpec(memory_space=pltpu.SMEM)
    S = lambda *s: jax.ShapeDtypeStruct(s, f32)
    return pl.pallas_call(
        main_kernel,
        out_shape=(S(2, 512, 512), S(2, 256, 256), S(2, 256, 256), S(2, 256, 256), S(2, 256, 512), S(2, 256, 256), S(2, 256, 256)),
        in_specs=[smem] * 3 + [any_] * 8,
        out_specs=[any_] * 7,
        scratch_shapes=[
            pltpu.VMEM((2, 768, 768), f32),
            pltpu.VMEM((2, 768, 768), f32),
            pltpu.VMEM((NB, 2, W, W), f32),
            pltpu.VMEM((2, 2, W, W), f32),
            pltpu.VMEM((2, 2, W, W), f32),
            pltpu.VMEM((8, W, W), f32),
            pltpu.VMEM((4, 2, W, W), bf16),
            pltpu.VMEM((NB, 2, 2, 2 * W, W), bf16),
            pltpu.VMEM((NB, 2, 2, 2 * W, W), bf16),
            pltpu.VMEM((NB, 2, 2, W, 2 * W), bf16),
            pltpu.VMEM((NB, 2, W, W), f32),
            pltpu.SemaphoreType.DMA((9,)),
            pltpu.SemaphoreType.DMA((8,)),
        ],
        compiler_params=pltpu.CompilerParams(vmem_limit_bytes=62 * 2**20),
        name="slots",
    )(offs, live, anchor, obj, right_top, right_bot, below, corner, probe, sq, jnp.asarray(make_tables()))


def prep_kernel(counts, pm, pmt, out):
    i = counts[0].astype(f32).astype(bf16)
    a = jnp.dot(pm[...], i, preferred_element_type=f32).astype(bf16)
    out[0] = jnp.sqrt(jnp.dot(a, pmt[...], preferred_element_type=f32))


def prep_call(counts):
    order = np.concatenate([np.arange(0, W, 2), np.arange(1, W, 2)])
    pm = np.zeros((W, W), np.float32)
    pm[np.arange(W), order] = 1.0
    full = pl.BlockSpec((W, W), lambda s: (0, 0))
    blk = pl.BlockSpec((1, W, W), lambda s: (s, 0, 0))
    return pl.pallas_call(
        prep_kernel,
        grid=(8,),
        out_shape=jax.ShapeDtypeStruct((8, W, W), f32),
        in_specs=[blk, full, full],
        out_specs=blk,
        compiler_params=pltpu.CompilerParams(vmem_limit_bytes=4 * 2**20),
        name="roots",
    )(counts, jnp.asarray(pm.astype(ml_dtypes.bfloat16)), jnp.asarray(pm.T.astype(ml_dtypes.bfloat16)))


def moved(value, axes, pairs):
    return lax.ppermute(value, axes, pairs)


def finish_kernel(part, above, top, bot, out, upper, lower, ab, tp, bt, sems):
    ins, outs = [], []
    for c in range(2):
        moves = [
            (part.at[c, 0:W], upper.at[c]),
            (above.at[c], ab.at[c]),
            (top.at[c], tp.at[c]),
            (part.at[c, W:, 0:W], lower.at[c]),
            (bot.at[c], bt.at[c]),
        ]
        ins.append([pltpu.make_async_copy(s, d, sems.at[c, i]) for i, (s, d) in enumerate(moves)])
        moves = [(upper.at[c], out.at[c, 0:W]), (lower.at[c], out.at[c, W:, 0:W])]
        outs.append([pltpu.make_async_copy(s, d, sems.at[c, 5 + i]) for i, (s, d) in enumerate(moves)])
    for copy in ins[0] + ins[1]:
        copy.start()
    for c in range(2):
        for copy in ins[c]:
            copy.wait()
        upper[c, :, :W] = upper[c, :, :W] - 0.5 * (ab[c, :, :W] + tp[c])
        upper[c, :, W:] = upper[c, :, W:] - 0.5 * ab[c, :, W:]
        lower[c] = lower[c] - 0.5 * bt[c]
        for copy in outs[c]:
            copy.start()
    for copy in outs[0] + outs[1]:
        copy.wait()


def finish_call(part, above, top, bot):
    any_ = pl.BlockSpec(memory_space=pl.ANY)
    return pl.pallas_call(
        finish_kernel,
        out_shape=jax.ShapeDtypeStruct((2, 512, 512), f32),
        in_specs=[any_] * 4,
        out_specs=any_,
        scratch_shapes=[
            pltpu.VMEM((2, W, 512), f32),
            pltpu.VMEM((2, W, W), f32),
            pltpu.VMEM((2, W, 512), f32),
            pltpu.VMEM((2, W, W), f32),
            pltpu.VMEM((2, W, W), f32),
            pltpu.SemaphoreType.DMA((2, 7)),
        ],
        input_output_aliases={0: 0},
        compiler_params=pltpu.CompilerParams(vmem_limit_bytes=8 * 2**20),
        name="finish",
    )(part, above, top, bot)


def swap_cores(value):
    return lax.ppermute(value, "core", [(0, 1), (1, 0)])


def sum_everywhere(value, axis):
    got = [lax.ppermute(value, axis, [(i, (i + k) % 4) for i in range(4)]) for k in (2, 1, 3)]
    return (value + got[0]) + (got[1] + got[2])


def probe_kernel(step, place, probe, mine, rest, out):
    for kc in range(2):
        at = pl.multiple_of(lax.rem(place[2] + kc, 2) * 512, 512)
        out[pl.ds(at, 512), :] = probe[pl.ds(at, 512), :] - step * (mine, rest)[kc][...]


def shards(object_planes, probe_planes, offsets, photon_counts, live_counts):
    n_row = lax.axis_size("y") * lax.axis_size("core")
    n_col = lax.axis_size("x") * lax.axis_size("z")
    rows, cols = ("y", "core"), ("x", "z")
    up = [(i, i - 1) for i in range(1, n_row)]
    down = [(i - 1, i) for i in range(1, n_row)]
    to_left = [(i, i - 1) for i in range(1, n_col)]
    to_right = [(i - 1, i) for i in range(1, n_col)]

    right_top = lax.ppermute(object_planes[:, :W, :W], cols, to_left)
    below = lax.ppermute(object_planes[:, :W, :], rows, up)
    right_bot = lax.ppermute(object_planes[:, W:, :W], cols, to_left)
    roots = prep_call(photon_counts)
    right_top, roots = lax.optimization_barrier((right_top, roots))
    corner = lax.ppermute(right_top, rows, up)
    place = jnp.stack(
        [lax.axis_index(rows) * 512, lax.axis_index(cols) * 512] + [lax.axis_index(a) for a in ("core",)]
    ).astype(jnp.int32)
    part, g_top, g_bot, g_corner, g_below, mine, other = main_call(
        offsets, live_counts.reshape(1), place, object_planes, right_top, right_bot, below, corner, probe_planes, roots
    )
    corner_in = lax.ppermute(g_corner, rows, down)
    bot_in = lax.ppermute(g_bot, cols, to_right)
    above_in = lax.ppermute(g_below, rows, down)
    half = (mine + swap_cores(other)).reshape(16, 32, W)
    top_in = lax.ppermute(g_top + corner_in, cols, to_right)
    plane = ("y", "x")
    piece = lax.all_to_all(half, plane, 0, 0).sum(0)
    piece, bot_in = lax.optimization_barrier((piece, bot_in))
    piece = sum_everywhere(piece, "z")
    piece, top_in = lax.optimization_barrier((piece, top_in))
    new_object = finish_call(part, above_in, top_in, bot_in)
    half = lax.all_to_all(jnp.broadcast_to(piece[None], half.shape), plane, 0, 0).reshape(512, W)
    rest = swap_cores(half)
    smem, vmem = pl.BlockSpec(memory_space=pltpu.SMEM), pl.BlockSpec(memory_space=pltpu.VMEM)
    step = 1.0 / math.sqrt(offsets.shape[0] * n_row * n_col)
    new_probe = pl.pallas_call(
        functools.partial(probe_kernel, step),
        out_shape=jax.ShapeDtypeStruct((1024, W), f32),
        in_specs=[smem] + [vmem] * 3,
        out_specs=vmem,
        compiler_params=pltpu.CompilerParams(vmem_limit_bytes=8 * 2**20),
        name="probe",
    )(place, probe_planes.reshape(1024, W), half, rest)
    return new_object, new_probe.reshape(probe_planes.shape)


def solution(mesh):
    split = jax.sharding.Mesh(
        mesh.devices.reshape(mesh.shape["row"] // 2, 2, mesh.shape["col"] // 4, 4), ("y", "core", "x", "z")
    )
    rows, cols = ("y", "core"), ("x", "z")
    in_specs = (
        P(None, rows, cols),
        P(),
        P(rows + cols, None),
        P(rows + cols, None, None),
        P(rows, cols),
    )
    out_specs = (P(None, rows, cols), P())
    return jax.shard_map(shards, mesh=split, in_specs=in_specs, out_specs=out_specs, check_vma=False)
```

```python
import functools
import math

import ml_dtypes
import numpy as np
import jax
import jax.numpy as jnp
from jax import lax
from jax.experimental import pallas as pl
from jax.experimental.pallas import tpu as pltpu
from jax.sharding import PartitionSpec as P

f32, bf16 = jnp.float32, jnp.bfloat16
W = 256
H = 128
HC = 128
NB = 2
LAG = 0


def make_tables():
    b = np.arange(H)[:, None]
    q = np.arange(H)[None, :]
    right = []
    for p in (0, 1):
        ang = 2.0 * np.pi * (((2 * q + p) * b) % W) / W
        c, s = np.cos(ang) / 16.0, np.sin(ang) / 16.0
        right.append(np.block([[c, -s], [s, c]]))
    out = []
    for t in (right[0], right[1], right[0].T, right[1].T):
        hi = t.astype(np.float32).astype(ml_dtypes.bfloat16)
        lo = (t - hi.astype(np.float64)).astype(np.float32).astype(ml_dtypes.bfloat16)
        out.append(np.stack([hi, lo]))
    return np.stack(out)


def split(x):
    hi = x.astype(bf16)
    lo = (x - hi.astype(f32)).astype(bf16)
    return hi, lo


def rmul2(hi, lo, t):
    return jnp.dot(jnp.concatenate([hi, lo, hi], 1), jnp.concatenate([t[0], t[0], t[1]], 0), preferred_element_type=f32)


def rmul(x, t):
    hi, lo = split(x)
    return rmul2(hi, lo, t)


def lmul2(t, hi, lo):
    return jnp.dot(jnp.concatenate([t[0], t[0], t[1]], 1), jnp.concatenate([hi, lo, hi], 0), preferred_element_type=f32)


def cat1(a, b):
    return jnp.concatenate([a, b], 1)


def cat0(a, b):
    return jnp.concatenate([a, b], 0)


def main_kernel(offs, live, anchor, obj, right_top, right_bot, below, corner, probe, sq, tables,
                o_part, o_rtop, o_rbot, o_corner, o_below, o_mine, o_other,
                cov, acc, patch, pacc, prv, sqv, tb, gs, hs, ds, term, sems, sqsems):
    ins = [
        (obj, cov.at[:, 0:512, 0:512]),
        (right_top, cov.at[:, 0:256, 512:768]),
        (right_bot, cov.at[:, 256:512, 512:768]),
        (below, cov.at[:, 512:768, 0:512]),
        (corner, cov.at[:, 512:768, 512:768]),
        (probe, prv),
        (tables, tb),
    ]
    copies = [pltpu.make_async_copy(s, d, sems.at[i]) for i, (s, d) in enumerate(ins)]
    roots = lambda s: pltpu.make_async_copy(sq.at[s], sqv.at[s], sqsems.at[s])
    for c in copies:
        c.start()
    for s in range(8):
        roots(s).start()
    acc[...] = jnp.zeros_like(acc)
    pacc[...] = jnp.zeros_like(pacc)
    for c in copies:
        c.wait()
    lane = lax.broadcasted_iota(jnp.int32, (W, H), 1)
    sub9 = lax.broadcasted_iota(jnp.int32, (33, 8, H), 1)
    sub = lax.broadcasted_iota(jnp.int32, (32, 8, H), 1)

    def place_of(s):
        top = offs[s, 0] - anchor[0]
        left = offs[s, 1] - anchor[1]
        la = pl.multiple_of(lax.div(left, 128) * 128, 128)
        ta = pl.multiple_of(lax.div(top, 8) * 8, 8)
        return ta, lax.rem(top, 8), la, lax.rem(left, 128)

    def fetch(s, b):
        ta, rs, la, ls = place_of(s)
        back = lax.rem(128 - ls, 128)
        rback = lax.rem(8 - rs, 8)
        for c in range(2):
            t = []
            for k in range(3):
                v = cov[c, pl.ds(ta, W + 8), pl.ds(la + 128 * k, H)]
                v = pltpu.roll(pltpu.roll(v, back, 1).reshape(33, 8, H), rback, 1)
                t.append(jnp.where(sub < 8 - rs, v[:32], v[1:]).reshape(W, H))
            for k in range(2):
                patch[b, c, :, 128 * k:128 * k + 128] = jnp.where(lane < 128 - ls, t[k], t[k + 1])

    def deposit(s, b):
        ta, rs, la, ls = place_of(s)
        for c in range(2):
            r = [pltpu.roll(term[b, c, :, 128 * k:128 * k + 128], ls, 1) for k in range(2)]
            z = jnp.zeros_like(r[0])
            keep = lane >= ls
            parts = [jnp.where(keep, r[0], z), jnp.where(keep, r[1], r[0]), jnp.where(keep, z, r[1])]
            for k in range(3):
                v = pltpu.roll(parts[k].reshape(32, 8, H), rs, 1)
                z8 = jnp.zeros((1, 8, H), f32)
                v = jnp.where(sub9 >= rs, jnp.concatenate([v, z8], 0), jnp.concatenate([z8, v], 0))
                acc[c, pl.ds(ta, W + 8), pl.ds(la + 128 * k, H)] += v.reshape(W + 8, H)

    def units(s, b, used):
        for m in range(2):
            for j in range(0, H, HC):
                def waves(m=m, j=j):
                    at = [slice(j, j + HC), slice(H + j, H + j + HC)]
                    get = lambda ref, *i: cat0(ref[(*i, at[0])], ref[(*i, at[1])])
                    pr, pi = get(prv, 0, m), get(prv, 1, m)
                    xr, xi = get(patch, b, 0), get(patch, b, 1)
                    wr = pr * xr - pi * xi
                    wi = pr * xi + pi * xr
                    e = cat1(wr[:, :H] + wr[:, H:], wi[:, :H] + wi[:, H:])
                    o = cat1(wr[:, :H] - wr[:, H:], wi[:, :H] - wi[:, H:])
                    return rmul(e, tb[0]), rmul(o, tb[1])

                def rows(ys, m=m, j=j):
                    for p in range(2):
                        lanes = slice(H * p, H * p + H)
                        y = ys[p]
                        for q in range(2):
                            f = y[:HC] + y[HC:] if q == 0 else y[:HC] - y[HC:]
                            hi, lo = split(f)
                            for part in range(2):
                                r = H * part + j
                                gs[b, m, q, r:r + HC, lanes] = hi[:, H * part:H * part + H]
                                gs[b, m, q, W + r:W + r + HC, lanes] = lo[:, H * part:H * part + H]

                yield waves, rows
        for q in range(2):
            for j in range(0, H, HC):
                def fars(q=q, j=j):
                    t = tb[2 + q]
                    return [lmul2(t, gs[b, m, q, :W], gs[b, m, q, W:]) for m in range(2)]

                def factors(fars, q=q, j=j):
                    mod = sum(a[:HC] * a[:HC] + a[HC:] * a[HC:] for a in fars)
                    root = sqv[s, H * q + j:H * q + j + HC, :]
                    fac = used - (used * root) * lax.rsqrt(jnp.maximum(mod, 0.1))
                    for m in range(2):
                        for part in range(2):
                            hi, lo = split(fars[m][HC * part:HC * part + HC] * fac)
                            r = H * part + j
                            hs[b, m, q, r:r + HC] = hi
                            hs[b, m, q, W + r:W + r + HC] = lo

                yield fars, factors
        for m in range(2):
            for j in range(0, H, HC):
                def backs(m=m, j=j):
                    out = []
                    for q in range(2):
                        t = tb[q]
                        out.append(lmul2(t, hs[b, m, q, :W], hs[b, m, q, W:]))
                    return out

                def columns(v, m=m, j=j):
                    for top in range(2):
                        x = v[0] + v[1] if top == 0 else v[0] - v[1]
                        for p in range(2):
                            hi, lo = split(cat1(x[:HC, H * p:H * p + H], x[HC:, H * p:H * p + H]))
                            r = H * top + j
                            ds[b, m, p, r:r + HC, :W] = hi
                            ds[b, m, p, r:r + HC, W:] = lo

                yield backs, columns
        for m in range(2):
            for j in (0, H):
                at = slice(j, j + H)

                def last(m=m, at=at):
                    return [rmul2(ds[b, m, p, at, :W], ds[b, m, p, at, W:], tb[2 + p]) for p in range(2)]

                def terms(d, m=m, at=at):
                    for h in range(2):
                        x = d[0] + d[1] if h == 0 else d[0] - d[1]
                        br, bi = x[:, :H], x[:, H:]
                        lanes = slice(H * h, H * h + H)
                        pr, pi = prv[0, m, at, lanes], prv[1, m, at, lanes]
                        xr, xi = patch[b, 0, at, lanes], patch[b, 1, at, lanes]
                        tr, ti = pr * br + pi * bi, pr * bi - pi * br
                        if m == 0:
                            term[b, 0, at, lanes], term[b, 1, at, lanes] = tr, ti
                        else:
                            term[b, 0, at, lanes] += tr
                            term[b, 1, at, lanes] += ti
                        pacc[0, m, at, lanes] += xr * br + xi * bi
                        pacc[1, m, at, lanes] += xr * bi - xi * br

                yield last, terms

    def pair(i, carry):
        slots = [i * NB + b for b in range(NB)]
        used = [jnp.where(s < live[0], 1.0, 0.0) for s in slots]
        for b in range(NB):
            roots(slots[b]).wait()
            fetch(slots[b], b)
        streams = [list(units(slots[b], b, used[b])) for b in range(NB)]
        todo = []
        for group in zip(*streams):
            for product, then in group:
                todo.append((then, product()))
                if len(todo) > LAG:
                    then, value = todo.pop(0)
                    then(value)
        for then, value in todo:
            then(value)
        for b in range(NB):
            deposit(slots[b], b)
        return carry

    pairs = lax.div(live[0] + NB - 1, NB)
    lax.fori_loop(0, pairs, pair, 0)

    def skip(s, carry):
        roots(s).wait()
        return carry

    lax.fori_loop(pairs * NB, 8, skip, 0)
    outs = [
        (acc.at[:, 512:768, 512:768], o_corner),
        (acc.at[:, 256:512, 512:768], o_rbot),
        (acc.at[:, 0:256, 512:768], o_rtop),
        (acc.at[:, 512:768, 0:512], o_below),
        (prv.at[1], o_other),
        (prv.at[0], o_mine),
        (cov.at[0, 0:512, 0:512], o_part.at[0]),
        (cov.at[1, 0:512, 0:512], o_part.at[1]),
    ]
    copies = [pltpu.make_async_copy(s, d, sems.at[i]) for i, (s, d) in enumerate(outs)]
    for c in copies[:4]:
        c.start()
    for kc in range(2):
        prv[kc] = pacc[lax.rem(anchor[2] + kc, 2)]
    for c in copies[4:6]:
        c.start()
    for c in range(2):
        cov[c, 0:512, 0:512] = cov[c, 0:512, 0:512] - 0.5 * acc[c, 0:512, 0:512]
        copies[6 + c].start()
    for c in copies:
        c.wait()


def main_call(offs, live, anchor, obj, right_top, right_bot, below, corner, probe, sq):
    any_ = pl.BlockSpec(memory_space=pl.ANY)
    smem = pl.BlockSpec(memory_space=pltpu.SMEM)
    S = lambda *s: jax.ShapeDtypeStruct(s, f32)
    return pl.pallas_call(
        main_kernel,
        out_shape=(S(2, 512, 512), S(2, 256, 256), S(2, 256, 256), S(2, 256, 256), S(2, 256, 512), S(2, 256, 256), S(2, 256, 256)),
        in_specs=[smem] * 3 + [any_] * 8,
        out_specs=[any_] * 7,
        scratch_shapes=[
            pltpu.VMEM((2, 768, 768), f32),
            pltpu.VMEM((2, 768, 768), f32),
            pltpu.VMEM((NB, 2, W, W), f32),
            pltpu.VMEM((2, 2, W, W), f32),
            pltpu.VMEM((2, 2, W, W), f32),
            pltpu.VMEM((8, W, W), f32),
            pltpu.VMEM((4, 2, W, W), bf16),
            pltpu.VMEM((NB, 2, 2, 2 * W, W), bf16),
            pltpu.VMEM((NB, 2, 2, 2 * W, W), bf16),
            pltpu.VMEM((NB, 2, 2, W, 2 * W), bf16),
            pltpu.VMEM((NB, 2, W, W), f32),
            pltpu.SemaphoreType.DMA((9,)),
            pltpu.SemaphoreType.DMA((8,)),
        ],
        compiler_params=pltpu.CompilerParams(vmem_limit_bytes=62 * 2**20),
        name="slots",
    )(offs, live, anchor, obj, right_top, right_bot, below, corner, probe, sq, jnp.asarray(make_tables()))


def prep_kernel(counts, pm, pmt, out):
    i = counts[0].astype(f32).astype(bf16)
    a = jnp.dot(pm[...], i, preferred_element_type=f32).astype(bf16)
    out[0] = jnp.sqrt(jnp.dot(a, pmt[...], preferred_element_type=f32))


def prep_call(counts):
    order = np.concatenate([np.arange(0, W, 2), np.arange(1, W, 2)])
    pm = np.zeros((W, W), np.float32)
    pm[np.arange(W), order] = 1.0
    full = pl.BlockSpec((W, W), lambda s: (0, 0))
    blk = pl.BlockSpec((1, W, W), lambda s: (s, 0, 0))
    return pl.pallas_call(
        prep_kernel,
        grid=(8,),
        out_shape=jax.ShapeDtypeStruct((8, W, W), f32),
        in_specs=[blk, full, full],
        out_specs=blk,
        compiler_params=pltpu.CompilerParams(vmem_limit_bytes=4 * 2**20),
        name="roots",
    )(counts, jnp.asarray(pm.astype(ml_dtypes.bfloat16)), jnp.asarray(pm.T.astype(ml_dtypes.bfloat16)))


def moved(value, axes, pairs):
    return lax.ppermute(value, axes, pairs)


def finish_kernel(part, above, top, bot, out, upper, lower, ab, tp, bt, sems):
    ins, outs = [], []
    for c in range(2):
        moves = [
            (part.at[c, 0:W], upper.at[c]),
            (above.at[c], ab.at[c]),
            (top.at[c], tp.at[c]),
            (part.at[c, W:, 0:W], lower.at[c]),
            (bot.at[c], bt.at[c]),
        ]
        ins.append([pltpu.make_async_copy(s, d, sems.at[c, i]) for i, (s, d) in enumerate(moves)])
        moves = [(upper.at[c], out.at[c, 0:W]), (lower.at[c], out.at[c, W:, 0:W])]
        outs.append([pltpu.make_async_copy(s, d, sems.at[c, 5 + i]) for i, (s, d) in enumerate(moves)])
    for copy in ins[0] + ins[1]:
        copy.start()
    for c in range(2):
        for copy in ins[c]:
            copy.wait()
        upper[c, :, :W] = upper[c, :, :W] - 0.5 * (ab[c, :, :W] + tp[c])
        upper[c, :, W:] = upper[c, :, W:] - 0.5 * ab[c, :, W:]
        lower[c] = lower[c] - 0.5 * bt[c]
        for copy in outs[c]:
            copy.start()
    for copy in outs[0] + outs[1]:
        copy.wait()


def finish_call(part, above, top, bot):
    any_ = pl.BlockSpec(memory_space=pl.ANY)
    return pl.pallas_call(
        finish_kernel,
        out_shape=jax.ShapeDtypeStruct((2, 512, 512), f32),
        in_specs=[any_] * 4,
        out_specs=any_,
        scratch_shapes=[
            pltpu.VMEM((2, W, 512), f32),
            pltpu.VMEM((2, W, W), f32),
            pltpu.VMEM((2, W, 512), f32),
            pltpu.VMEM((2, W, W), f32),
            pltpu.VMEM((2, W, W), f32),
            pltpu.SemaphoreType.DMA((2, 7)),
        ],
        input_output_aliases={0: 0},
        compiler_params=pltpu.CompilerParams(vmem_limit_bytes=8 * 2**20),
        name="finish",
    )(part, above, top, bot)


def swap_cores(value):
    return lax.ppermute(value, "core", [(0, 1), (1, 0)])


def sum_everywhere(value, axis):
    got = [lax.ppermute(value, axis, [(i, (i + k) % 4) for i in range(4)]) for k in (2, 1, 3)]
    return (value + got[0]) + (got[1] + got[2])


def probe_kernel(step, place, probe, mine, rest, out):
    for kc in range(2):
        at = pl.multiple_of(lax.rem(place[2] + kc, 2) * 512, 512)
        out[pl.ds(at, 512), :] = probe[pl.ds(at, 512), :] - step * (mine, rest)[kc][...]


def shards(object_planes, probe_planes, offsets, photon_counts, live_counts):
    n_row = lax.axis_size("y") * lax.axis_size("core")
    n_col = lax.axis_size("x") * lax.axis_size("z")
    rows, cols = ("y", "core"), ("x", "z")
    up = [(i, i - 1) for i in range(1, n_row)]
    down = [(i - 1, i) for i in range(1, n_row)]
    to_left = [(i, i - 1) for i in range(1, n_col)]
    to_right = [(i - 1, i) for i in range(1, n_col)]

    right_top = lax.ppermute(object_planes[:, :W, :W], cols, to_left)
    below = lax.ppermute(object_planes[:, :W, :], rows, up)
    right_bot = lax.ppermute(object_planes[:, W:, :W], cols, to_left)
    roots = prep_call(photon_counts)
    right_top, roots = lax.optimization_barrier((right_top, roots))
    corner = lax.ppermute(right_top, rows, up)
    place = jnp.stack(
        [lax.axis_index(rows) * 512, lax.axis_index(cols) * 512] + [lax.axis_index(a) for a in ("core",)]
    ).astype(jnp.int32)
    part, g_top, g_bot, g_corner, g_below, mine, other = main_call(
        offsets, live_counts.reshape(1), place, object_planes, right_top, right_bot, below, corner, probe_planes, roots
    )
    bot_in = lax.ppermute(g_bot, cols, to_right)
    above_in = lax.ppermute(g_below, rows, down)
    half = (mine + swap_cores(other)).reshape(16, 32, W)
    half, g_corner = lax.optimization_barrier((half, g_corner))
    corner_in = lax.ppermute(g_corner, rows, down)
    top_in = lax.ppermute(g_top + corner_in, cols, to_right)
    plane = ("y", "x")
    piece = lax.all_to_all(half, plane, 0, 0).sum(0)
    piece, bot_in = lax.optimization_barrier((piece, bot_in))
    piece = sum_everywhere(piece, "z")
    piece, top_in = lax.optimization_barrier((piece, top_in))
    new_object = finish_call(part, above_in, top_in, bot_in)
    half = lax.all_to_all(jnp.broadcast_to(piece[None], half.shape), plane, 0, 0).reshape(512, W)
    rest = swap_cores(half)
    smem, vmem = pl.BlockSpec(memory_space=pltpu.SMEM), pl.BlockSpec(memory_space=pltpu.VMEM)
    step = 1.0 / math.sqrt(offsets.shape[0] * n_row * n_col)
    new_probe = pl.pallas_call(
        functools.partial(probe_kernel, step),
        out_shape=jax.ShapeDtypeStruct((1024, W), f32),
        in_specs=[smem] + [vmem] * 3,
        out_specs=vmem,
        compiler_params=pltpu.CompilerParams(vmem_limit_bytes=8 * 2**20),
        name="probe",
    )(place, probe_planes.reshape(1024, W), half, rest)
    return new_object, new_probe.reshape(probe_planes.shape)


def solution(mesh):
    split = jax.sharding.Mesh(
        mesh.devices.reshape(mesh.shape["row"] // 2, 2, mesh.shape["col"] // 4, 4), ("y", "core", "x", "z")
    )
    rows, cols = ("y", "core"), ("x", "z")
    in_specs = (
        P(None, rows, cols),
        P(),
        P(rows + cols, None),
        P(rows + cols, None, None),
        P(rows, cols),
    )
    out_specs = (P(None, rows, cols), P())
    return jax.shard_map(shards, mesh=split, in_specs=in_specs, out_specs=out_specs, check_vma=False)
```
